128 devices in a mesh: fsdp: 32 (over x, y, core), grp: 4 (over z).
Axes of the slice: x: 4, y: 4, z: 4, core: 2. Of those that a mesh axis runs over, the one named last changes fastest.
Arguments:
- q_values: bfloat16 [2048, 65536], P('fsdp', 'grp'), may hold values from -6 to 6
- scales: bfloat16 [2048, 512], P('fsdp', 'grp'), may hold values from 0.5 to 18
- block_slots: int32 [4, 32], P('grp'), may hold values from 0 to 31, each once within a row
- left_root: float32 [4, 32, 1024, 1024], P('grp', 'fsdp'), may hold values from -1 to 3
- right_root: float32 [4, 32, 1024, 1024], P('grp', 'fsdp'), may hold values from -1 to 3
- second_moment: float32 [4, 32, 1024, 1024], P('grp', 'fsdp'), may hold values from 0.02 to 0.5
Outputs:
- update: bfloat16 [2048, 65536], P('fsdp', 'grp')
- new_moment: float32 [4, 32, 1024, 1024], P('grp', 'fsdp')
The draws below stay inside these ranges and needn't reach their ends.
All inputs are finite; a program needn't handle non-finite values.
Results may differ from the reference program's by a relative error of at most 0.0004.
Values may be sent and summed in bfloat16 or wider, within the bound.
No kernel may reach another device: no remote copies, remote signals or barrier semaphores. Data moves between devices by JAX's collectives and lax.ppermute only.
A program may use at most 128 MiB of HBM per device.

```python
import math
import jax
import jax.numpy as jnp
from jax import lax

BS = 1024
GROUP = 128
CBG = 16
RB = 2
ROWS = 2048
COLS = 65536
SLOTS_G = 32
N_GRP = 4


def make_root(key):
    diag_key, off_key = jax.random.split(key)
    shape = (N_GRP, SLOTS_G, BS, BS)
    diagonal = jnp.exp(jax.random.uniform(diag_key, (N_GRP, SLOTS_G, BS, 1), jnp.float32, 0.0, 0.6931))
    off = jnp.clip(jax.random.normal(off_key, shape, jnp.float32) * 0.35, -1.4, 1.4)
    eye = (lax_iota_rows() == lax_iota_cols()).astype(jnp.float32)
    return off / jnp.sqrt(jnp.float32(BS)) + diagonal * eye


def lax_iota_rows():
    return jnp.arange(BS, dtype=jnp.int32)[:, None]


def lax_iota_cols():
    return jnp.arange(BS, dtype=jnp.int32)[None, :]


def draw_scales(key, part):
    key = jax.random.fold_in(key, 11)
    rand_key = jax.random.fold_in(key, 1)
    height = jnp.arange(ROWS, dtype=jnp.float32) / jnp.float32(ROWS)
    base = jnp.exp(height * 1.0986)
    factor = jnp.exp(jax.random.uniform(rand_key, (ROWS, COLS // GROUP), jnp.float32, -0.6931, 0.6931))
    return (base[:, None] * factor).astype(jnp.bfloat16)


def draw_left_root(key, part):
    key = jax.random.fold_in(key, 21)
    return make_root(key)


def draw_right_root(key, part):
    key = jax.random.fold_in(key, 22)
    return make_root(key)


def block_scale(rng, shape, cuts, least, largest):
    def one(dim, blocks):
        heights = jax.random.uniform(jax.random.fold_in(jax.random.fold_in(rng, 6), dim), (blocks,), jnp.float32, least / len(cuts), largest / len(cuts))
        return jnp.repeat(jnp.exp(heights), shape[dim] // blocks).reshape((-1,) + (1,) * (len(shape) - dim - 1))

    factor_of = one(*cuts[0])
    for cut in cuts[1:]:
        factor_of = factor_of * one(*cut)
    return factor_of


def centred(key, dims, scale, bound, cuts=(), kind=jnp.bfloat16):
    values = scale * jax.random.normal(key, dims, jnp.float32)
    if cuts:
        values = values * block_scale(key, dims, cuts, -0.22, 0.18)
    return jnp.clip(values, -bound, bound).astype(kind)


def setup_inputs(seed: int = 0) -> dict:
    key_list = jax.random.split(jax.random.key(seed), 7)
    q_values = centred(key_list[0], (ROWS, COLS), 1.0, 6.0, ((0, 32), (1, 4)))
    scales = draw_scales(jax.random.fold_in(key_list[6], 71), 0)
    block_slots = jax.vmap(lambda own: jax.random.permutation(own, SLOTS_G))(jax.random.split(key_list[2], N_GRP)).reshape((N_GRP, SLOTS_G)).astype(jnp.int32)
    left_root = draw_left_root(jax.random.fold_in(key_list[6], 71), 0)
    right_root = draw_right_root(jax.random.fold_in(key_list[6], 71), 0)
    second_moment = jnp.clip(jnp.exp(math.log(0.5) - 3.218876 * jax.random.uniform(key_list[5], (N_GRP, SLOTS_G, BS, BS), jnp.float32) ** block_scale(key_list[5], (N_GRP, SLOTS_G, BS, BS), ((0, 4), (1, 32)), -0.2, 0.2)), 0.02, 0.5)
    return {"q_values": q_values, "scales": scales, "block_slots": block_slots, "left_root": left_root, "right_root": right_root, "second_moment": second_moment}


def precondition(held, left, right, moment):
    precond = jnp.matmul(jnp.matmul(left, held, precision=lax.Precision.HIGHEST), right, precision=lax.Precision.HIGHEST)
    fresh = 0.9 * moment + 0.1 * held * held
    adam = held / (jnp.sqrt(fresh) + 1e-08)
    ratio = jnp.sqrt(jnp.sum(adam * adam)) / jnp.sqrt(jnp.sum(precond * precond) + 1e-12)
    return ((precond * ratio).astype(jnp.bfloat16), fresh)

def reference(q_values, scales, block_slots, left_root, right_root, second_moment):
    grad = q_values.astype(jnp.float32) * jnp.repeat(scales.astype(jnp.float32), GROUP, axis=1)
    total = jnp.sum(grad * grad)
    clip = jnp.minimum(1.0, 0.5 * jnp.sqrt(jnp.float32(ROWS * COLS)) / jnp.sqrt(total))
    clipped = grad * clip
    tiles = clipped.reshape(RB, BS, N_GRP, CBG, BS).transpose(2, 0, 3, 1, 4).reshape(N_GRP, RB * CBG, BS, BS)
    held = jax.vmap(lambda part, order: jnp.take(part, order, axis=0))(tiles, block_slots)

    def one_slot(items):
        return precondition(items[0], items[1], items[2], items[3])
    flat = (held.reshape(N_GRP * SLOTS_G, BS, BS), left_root.reshape(N_GRP * SLOTS_G, BS, BS), right_root.reshape(N_GRP * SLOTS_G, BS, BS), second_moment.reshape(N_GRP * SLOTS_G, BS, BS))
    grafted, fresh = lax.map(one_slot, flat)
    grafted = grafted.reshape(N_GRP, SLOTS_G, BS, BS)
    inverse = jnp.argsort(block_slots, axis=1).astype(jnp.int32)
    placed = jax.vmap(lambda part, order: jnp.take(part, order, axis=0))(grafted, inverse)
    update = placed.reshape(N_GRP, RB, CBG, BS, BS).transpose(1, 3, 0, 2, 4).reshape(ROWS, COLS)
    return (update, fresh.reshape(N_GRP, SLOTS_G, BS, BS))
```

```python
import jax
import jax.numpy as jnp
from jax import lax
from jax.experimental import pallas as pl
from jax.experimental.pallas import tpu as pltpu
from jax.sharding import PartitionSpec as P

LANES = 128
EXTRA = 16
STEPS = 4
PARTS = 8
F32 = jnp.float32
BF16 = jnp.bfloat16
HBM = pl.BlockSpec(memory_space=pltpu.HBM)
SMEM = pl.BlockSpec(memory_space=pltpu.SMEM)
PARAMS = pltpu.CompilerParams(vmem_limit_bytes=60 * 1024 * 1024)


def cost(flops, nbytes):
    return pl.CostEstimate(flops=flops, bytes_accessed=nbytes, transcendentals=0)


def pack(slots, q_values, scales, width, start, part, with_scales):
    owners = slots.shape[1]
    rows, cols = q_values.shape
    columns = cols // width
    groups = width // LANES
    here = part // LANES
    tall = here * rows + (EXTRA if with_scales else 0)
    per = owners // PARTS
    piece = cols // PARTS

    def body(slots_hbm, q_hbm, s_hbm, out_hbm, slots_ref, q_ref, s_ref, turned, out_ref, ins, outs):
        reads = [
            pltpu.make_async_copy(slots_hbm, slots_ref, ins.at[PARTS]),
            pltpu.make_async_copy(s_hbm, s_ref, ins.at[PARTS + 1]),
        ]
        for k in range(PARTS):
            at = slice(k * piece, (k + 1) * piece)
            reads.append(pltpu.make_async_copy(q_hbm.at[:, at], q_ref.at[:, at], ins.at[k]))
        for read in reads:
            read.start()
        for read in reads[:2]:
            read.wait()
        if with_scales:
            padded = jnp.concatenate([s_ref[...].astype(F32), jnp.zeros((LANES - rows, LANES), F32)], axis=0)
            turned[...] = padded.T
            pad = jnp.zeros((EXTRA - groups, LANES), F32)
            for o in range(owners):
                column = lax.rem(slots_ref[0, o], columns)
                scale = turned[pl.ds(pl.multiple_of(column * groups, groups), groups), :]
                out_ref[o, here * rows :, :] = jnp.concatenate([scale, pad], axis=0).astype(BF16)
        for read in reads[2:]:
            read.wait()
        writes = []
        for k in range(PARTS):
            for o in range(k * per, (k + 1) * per):
                column = lax.rem(slots_ref[0, o], columns)
                for j in range(here):
                    at = pl.multiple_of(column * width + start + j * LANES, LANES)
                    out_ref[o, j * rows : (j + 1) * rows, :] = q_ref[:, pl.ds(at, LANES)]
            at = slice(k * per, (k + 1) * per)
            write = pltpu.make_async_copy(out_ref.at[at], out_hbm.at[at], outs.at[k])
            write.start()
            writes.append(write)
        for write in writes:
            write.wait()

    return pl.pallas_call(
        body,
        out_shape=jax.ShapeDtypeStruct((owners, tall, LANES), BF16),
        in_specs=[HBM] * 3,
        out_specs=HBM,
        scratch_shapes=[
            pltpu.SMEM(slots.shape, jnp.int32),
            pltpu.VMEM((rows, cols), BF16),
            pltpu.VMEM(scales.shape, BF16),
            pltpu.VMEM((scales.shape[1], LANES), F32),
            pltpu.VMEM((owners, tall, LANES), BF16),
            pltpu.SemaphoreType.DMA((PARTS + 2,)),
            pltpu.SemaphoreType.DMA((PARTS,)),
        ],
        compiler_params=PARAMS,
        cost_estimate=cost(0, 2 * rows * cols + 2 * owners * tall * LANES),
        name=f"pack_{start}",
    )(slots, q_values, scales)


def square_sum(q_values, scales):
    rows, cols = q_values.shape
    groups = scales.shape[1]
    group = cols // groups

    def body(q_hbm, s_hbm, out_ref, q_ref, s_ref, sems):
        reads = [pltpu.make_async_copy(q_hbm, q_ref, sems.at[0]), pltpu.make_async_copy(s_hbm, s_ref, sems.at[1])]
        for read in reads:
            read.start()
        for read in reads:
            read.wait()
        total = jnp.zeros((rows, group), F32)
        for j in range(groups):
            grad = q_ref[:, j * group : (j + 1) * group].astype(F32) * s_ref[:, j : j + 1].astype(F32)
            total = total + grad * grad
        out_ref[...] = jnp.full((8, LANES), jnp.sum(total))

    return pl.pallas_call(
        body,
        out_shape=jax.ShapeDtypeStruct((8, LANES), F32),
        in_specs=[HBM] * 2,
        scratch_shapes=[
            pltpu.VMEM((rows, cols), BF16),
            pltpu.VMEM(scales.shape, BF16),
            pltpu.SemaphoreType.DMA((2,)),
        ],
        compiler_params=PARAMS,
        cost_estimate=cost(3 * rows * cols, 2 * rows * cols),
        name="square_sum",
    )(q_values, scales)


def split_roots(left, right):
    size = left.shape[0]
    rows = size // STEPS

    def body(l_hbm, r_hbm, l1_hbm, l2_hbm, r1_hbm, r2_hbm, full, top, low, ins, outs):
        jobs = []
        for src, high_hbm, low_hbm in ((l_hbm, l1_hbm, l2_hbm), (r_hbm, r1_hbm, r2_hbm)):
            for n in range(STEPS):
                at = pl.ds(n * rows, rows)
                jobs.append((src.at[at], high_hbm.at[at], low_hbm.at[at]))
        reads = [pltpu.make_async_copy(job[0], full.at[k], ins.at[k]) for k, job in enumerate(jobs)]
        for read in reads:
            read.start()
        writes = []
        for k, (_, high_to, low_to) in enumerate(jobs):
            reads[k].wait()
            top[k], low[k] = two(full[k])
            for h, (src, to) in enumerate(((top.at[k], high_to), (low.at[k], low_to))):
                write = pltpu.make_async_copy(src, to, outs.at[2 * k + h])
                write.start()
                writes.append(write)
        for write in writes:
            write.wait()

    jobs = 2 * STEPS
    return pl.pallas_call(
        body,
        out_shape=[jax.ShapeDtypeStruct((size, size), BF16)] * 4,
        in_specs=[HBM] * 2,
        out_specs=[HBM] * 4,
        scratch_shapes=[
            pltpu.VMEM((jobs, rows, size), F32),
            pltpu.VMEM((jobs, rows, size), BF16),
            pltpu.VMEM((jobs, rows, size), BF16),
            pltpu.SemaphoreType.DMA((jobs,)),
            pltpu.SemaphoreType.DMA((2 * jobs,)),
        ],
        compiler_params=PARAMS,
        cost_estimate=cost(4 * size * size, 16 * size * size),
        name="split_roots",
    )(left, right)


def dot(a, b):
    return jnp.dot(a, b, preferred_element_type=F32)


def two(value):
    top = value.astype(BF16)
    return top, (value - top.astype(F32)).astype(BF16)


def fold(value):
    rows, cols = value.shape
    total = value[:, :LANES]
    for j in range(1, cols // LANES):
        total = total + value[:, j * LANES : (j + 1) * LANES]
    return total.reshape(rows // 8, 8, LANES).sum(axis=0)


def everywhere(value):
    return jnp.sum(value, axis=(0, 1), keepdims=True)


def dequant(a_ref, turned, first, rows, h1, h2, at_lane):
    pieces, tall, _ = a_ref.shape
    for piece in range(pieces):
        at = slice(piece * rows, (piece + 1) * rows)
        for j in range(tall // rows):
            group = piece * EXTRA + first + j
            grad = a_ref[piece, j * rows : (j + 1) * rows, :].astype(F32) * turned[:rows, group : group + 1]
            lanes = slice(at_lane + j * LANES, at_lane + (j + 1) * LANES)
            h1[at, lanes], h2[at, lanes] = two(grad)


def products(band, arrived, l1, l2, r1, r2, rows):
    size = l1.shape[0]
    _, tall, _ = arrived.shape
    pieces = size // rows
    part = tall // rows * LANES
    block = size // STEPS

    def body(
        band_ref, a_hbm, l1_hbm, l2_hbm, r1_hbm, r2_hbm, p_hbm, h1_hbm, h2_hbm, turned,
        a_ref, l1_ref, l2_ref, r1_ref, r2_ref, h1, h2, t1, t2, p_ref, ins, outs,
    ):
        deep = pl.ds(0, part)
        sources = [a_hbm.at[pl.ds(band_ref[0] * pieces, pieces)], l1_hbm, l2_hbm, r1_hbm.at[deep], r2_hbm.at[deep]]
        targets = [a_ref, l1_ref, l2_ref, r1_ref, r2_ref]
        reads = [pltpu.make_async_copy(s, t, ins.at[k]) for k, (s, t) in enumerate(zip(sources, targets))]
        for read in reads:
            read.start()
        reads[0].wait()
        scale = a_ref[:, part // LANES * rows :, :].astype(F32).reshape(pieces * EXTRA, LANES)
        turned[...] = scale.T
        dequant(a_ref, turned, 0, rows, h1, h2, 0)
        keeps = [pltpu.make_async_copy(h1, h1_hbm, outs.at[STEPS]), pltpu.make_async_copy(h2, h2_hbm, outs.at[STEPS + 1])]
        for keep in keeps:
            keep.start()
        for read in reads[1:3]:
            read.wait()

        @pl.loop(0, part // block)
        def _(n):
            at = pl.ds(pl.multiple_of(n * block, block), block)
            half = dot(l1_ref[...], h1[:, at]) + (dot(l1_ref[...], h2[:, at]) + dot(l2_ref[...], h1[:, at]))
            t1[:, at], t2[:, at] = two(half)

        for read in reads[3:]:
            read.wait()

        def p_copy(n):
            at = pl.ds(pl.multiple_of(n * block, block), block)
            return pltpu.make_async_copy(p_ref.at[:, at], p_hbm.at[:, at], outs.at[n])

        @pl.loop(0, STEPS)
        def _(n):
            at = pl.ds(pl.multiple_of(n * block, block), block)
            p_ref[:, at] = dot(t1[...], r1_ref[:, at]) + (dot(t1[...], r2_ref[:, at]) + dot(t2[...], r1_ref[:, at]))
            p_copy(n).start()

        for n in range(STEPS):
            p_copy(n).wait()
        for keep in keeps:
            keep.wait()

    square = (size, size)
    narrow = (size, part)
    return pl.pallas_call(
        body,
        out_shape=[
            jax.ShapeDtypeStruct(square, F32),
            jax.ShapeDtypeStruct(narrow, BF16),
            jax.ShapeDtypeStruct(narrow, BF16),
            jax.ShapeDtypeStruct((LANES, pieces * EXTRA), F32),
        ],
        in_specs=[SMEM] + [HBM] * 5,
        out_specs=[HBM] * 3 + [pl.BlockSpec(memory_space=pltpu.VMEM)],
        scratch_shapes=[
            pltpu.VMEM((pieces, tall, LANES), BF16),
            pltpu.VMEM(square, BF16),
            pltpu.VMEM(square, BF16),
            pltpu.VMEM((part, size), BF16),
            pltpu.VMEM((part, size), BF16),
            pltpu.VMEM(narrow, BF16),
            pltpu.VMEM(narrow, BF16),
            pltpu.VMEM(narrow, BF16),
            pltpu.VMEM(narrow, BF16),
            pltpu.VMEM(square, F32),
            pltpu.SemaphoreType.DMA((5,)),
            pltpu.SemaphoreType.DMA((STEPS + 2,)),
        ],
        compiler_params=PARAMS,
        cost_estimate=cost(12 * size * size * part, 20 * size * size),
        name="products",
    )(band, arrived, l1, l2, r1, r2)


def graft(band, clip, arrived, turned, l1, l2, r1, r2, earlier, k1, k2, moment, owners, rows):
    size = moment.shape[0]
    pieces = size // rows
    block = size // STEPS
    done = k1.shape[1]
    part = size - done
    _, tall, _ = arrived.shape

    def body(
        band_ref, clip_ref, a_hbm, turned_ref, l1_hbm, l2_hbm, r1_hbm, r2_hbm, p_hbm, h1_hbm, h2_hbm, m_hbm,
        out_hbm, fresh_hbm,
        a_ref, l1_ref, l2_ref, r1_ref, r2_ref, p_ref, h1, h2, m_ref, out_ref, asum, psum, ins, outs,
    ):
        def cut(n):
            return pl.ds(pl.multiple_of(n * block, block), block)

        deep = pl.ds(done, part)
        old = pl.ds(0, done)
        whole = [
            (a_hbm.at[pl.ds(band_ref[0] * pieces, pieces)], a_ref),
            (r1_hbm.at[deep], r1_ref),
            (r2_hbm.at[deep], r2_ref),
        ]
        whole = [pltpu.make_async_copy(s, t, ins.at[6, k]) for k, (s, t) in enumerate(whole)]

        def reads(n):
            at = cut(n)
            pairs = (
                (l1_hbm.at[at], l1_ref.at[at]),
                (l2_hbm.at[at], l2_ref.at[at]),
                (h1_hbm.at[at], h1.at[at, old]),
                (h2_hbm.at[at], h2.at[at, old]),
                (m_hbm.at[at], m_ref.at[at]),
                (p_hbm.at[at], p_ref.at[at]),
            )
            return [pltpu.make_async_copy(s, t, ins.at[k, n]) for k, (s, t) in enumerate(pairs)]

        for read in whole:
            read.start()
        for n in range(STEPS):
            for read in reads(n):
                read.start()
        clip_now = clip_ref[0, 0]
        asum[...] = jnp.zeros_like(asum)
        psum[...] = jnp.zeros_like(psum)
        whole[0].wait()
        dequant(a_ref, turned_ref, done // LANES, rows, h1, h2, done)
        for read in whole[1:]:
            read.wait()

        def fresh_copy(n):
            return pltpu.make_async_copy(m_ref.at[cut(n)], fresh_hbm.at[cut(n)], outs.at[0, n])

        def out_copy(n):
            to = pl.ds(pl.multiple_of(band_ref[0] * size + n * block, block), block)
            return pltpu.make_async_copy(out_ref.at[cut(n)], out_hbm.at[to], outs.at[1, n])

        @pl.loop(0, STEPS)
        def _(n):
            for read in reads(n):
                read.wait()
            at = cut(n)
            new = slice(done, size)
            half = dot(l1_ref[at, :], h1[:, new]) + (dot(l1_ref[at, :], h2[:, new]) + dot(l2_ref[at, :], h1[:, new]))
            high, low = two(half)
            product = dot(high, r1_ref[...]) + (dot(high, r2_ref[...]) + dot(low, r1_ref[...]))
            product = p_ref[at, :] + product
            p_ref[at, :] = product
            psum[...] += fold(product * product)
            held = (h1[at, :].astype(F32) + h2[at, :].astype(F32)) * clip_now
            fresh = 0.9 * m_ref[at, :] + 0.1 * held * held
            m_ref[at, :] = fresh
            adam = held / (jnp.sqrt(fresh) + 1e-08)
            asum[...] += fold(adam * adam)
            fresh_copy(n).start()

        clips = jnp.full((1, 1), clip_now)
        norm = jnp.sqrt(everywhere(psum[...]) * (clips * clips) + 1e-12)
        ratio = clips * (jnp.sqrt(everywhere(asum[...])) / norm)

        @pl.loop(0, STEPS)
        def _(n):
            at = cut(n)
            out_ref[at, :] = (p_ref[at, :] * ratio).astype(BF16)
            out_copy(n).start()

        for n in range(STEPS):
            fresh_copy(n).wait()
            out_copy(n).wait()

    square = (size, size)
    return pl.pallas_call(
        body,
        out_shape=[
            jax.ShapeDtypeStruct((owners * rows, size), BF16),
            jax.ShapeDtypeStruct(square, F32),
        ],
        in_specs=[SMEM, SMEM, HBM, pl.BlockSpec(memory_space=pltpu.VMEM)] + [HBM] * 8,
        out_specs=[HBM, HBM],
        scratch_shapes=[
            pltpu.VMEM((pieces, tall, LANES), BF16),
            pltpu.VMEM(square, BF16),
            pltpu.VMEM(square, BF16),
            pltpu.VMEM((part, size), BF16),
            pltpu.VMEM((part, size), BF16),
            pltpu.VMEM(square, F32),
            pltpu.VMEM(square, BF16),
            pltpu.VMEM(square, BF16),
            pltpu.VMEM(square, F32),
            pltpu.VMEM(square, BF16),
            pltpu.VMEM((8, LANES), F32),
            pltpu.VMEM((8, LANES), F32),
            pltpu.SemaphoreType.DMA((7, STEPS)),
            pltpu.SemaphoreType.DMA((2, STEPS)),
        ],
        compiler_params=PARAMS,
        cost_estimate=cost(12 * size * size * part, 24 * size * size),
        name="graft",
    )(band, clip, arrived, turned, l1, l2, r1, r2, earlier, k1, k2, moment)


def place(slots, band, returned, cols):
    owners, rows, width = returned.shape
    columns = cols // width

    def body(slots_ref, band_ref, r_hbm, out_hbm, out_ref, ins, outs):
        def each(act):
            for owner in range(owners):
                here = slots_ref[0, owner]

                @pl.when(lax.div(here, columns) == band_ref[0])
                def _():
                    act(owner, pl.ds(pl.multiple_of(lax.rem(here, columns) * width, width), width))

        def read(owner, at):
            return pltpu.make_async_copy(r_hbm.at[owner], out_ref.at[:, at], ins.at[owner])

        def write(owner, at):
            return pltpu.make_async_copy(out_ref.at[:, at], out_hbm.at[:, at], outs.at[owner])

        def pass_on(owner, at):
            read(owner, at).wait()
            write(owner, at).start()

        each(lambda owner, at: read(owner, at).start())
        each(pass_on)
        each(lambda owner, at: write(owner, at).wait())

    return pl.pallas_call(
        body,
        out_shape=jax.ShapeDtypeStruct((rows, cols), BF16),
        in_specs=[SMEM, SMEM, HBM],
        out_specs=HBM,
        scratch_shapes=[
            pltpu.VMEM((rows, cols), BF16),
            pltpu.SemaphoreType.DMA((owners,)),
            pltpu.SemaphoreType.DMA((owners,)),
        ],
        compiler_params=PARAMS,
        cost_estimate=cost(0, 4 * rows * cols),
        name="place",
    )(slots, band, returned)


def add_over(value, axis, stride, size):
    whole = lax.axis_size(axis)

    def turn(i, k):
        digit = i // stride % size
        return i + ((digit + k) % size - digit) * stride

    sent = [lax.ppermute(value, axis, [(i, turn(i, k)) for i in range(whole)]) for k in range(1, size)]
    return sum(sent, value)


def on_device(q_values, scales, block_slots, left_root, right_root, second_moment):
    count = lax.axis_size("fsdp")
    index = lax.axis_index("fsdp")
    rows, cols = q_values.shape
    width = left_root.shape[-1]
    columns = cols // width
    band_devs = width // rows
    my_band = (index // band_devs).astype(jnp.int32).reshape(1)
    slots = block_slots[0]
    mine = lax.dynamic_index_in_dim(slots, index, 0, keepdims=False)
    mine_band = (mine // columns).reshape(1)

    first = width * 3 // 4

    def exchange(value):
        return lax.all_to_all(value, "fsdp", split_axis=0, concat_axis=0, tiled=True)

    arrived = exchange(pack(block_slots, q_values, scales, width, 0, first, True))
    later = exchange(pack(block_slots, q_values, scales, width, first, width - first, False))

    total = square_sum(q_values, scales)
    for axis, stride, size in (("grp", 1, 2), ("grp", 2, 2), ("fsdp", 1, 2)):
        total = add_over(total, axis, stride, size)
    roots = split_roots(left_root[0, 0], right_root[0, 0])
    total, *roots = lax.optimization_barrier((total, *roots))
    total = add_over(total, "fsdp", 2, 4)
    product, h1, h2, turned = products(mine_band, arrived, *roots, rows)
    total, product = lax.optimization_barrier((total, product))
    total = add_over(total, "fsdp", 8, 4)[:1, :1]
    count_all = rows * count * cols * lax.axis_size("grp")
    clip = jnp.minimum(1.0, 0.5 * jnp.sqrt(F32(count_all)) / jnp.sqrt(total))

    outgoing, fresh = graft(
        mine_band, clip, later, turned, *roots, product, h1, h2, second_moment[0, 0], count, rows
    )
    outgoing = outgoing.reshape(count, rows, width)
    update = place(block_slots, my_band, exchange(outgoing), cols)
    return (update, fresh[None, None])


def solution(mesh):
    in_specs = (
        P("fsdp", "grp"),
        P("fsdp", "grp"),
        P("grp", None),
        P("grp", "fsdp", None, None),
        P("grp", "fsdp", None, None),
        P("grp", "fsdp", None, None),
    )
    out_specs = (P("fsdp", "grp"), P("grp", "fsdp", None, None))
    return jax.shard_map(
        on_device, mesh=mesh, in_specs=in_specs, out_specs=out_specs, check_vma=False
    )
```

```python
import jax
import jax.numpy as jnp
from jax import lax
from jax.experimental import pallas as pl
from jax.experimental.pallas import tpu as pltpu
from jax.sharding import PartitionSpec as P

LANES = 128
EXTRA = 16
STEPS = 4
FINE = 32
F32 = jnp.float32
BF16 = jnp.bfloat16
HBM = pl.BlockSpec(memory_space=pltpu.HBM)
SMEM = pl.BlockSpec(memory_space=pltpu.SMEM)
VMEM = pl.BlockSpec(memory_space=pltpu.VMEM)
DMA = pltpu.SemaphoreType.DMA


def grant(mib):
    return pltpu.CompilerParams(vmem_limit_bytes=mib * 1024 * 1024)


def cost(flops, nbytes):
    return pl.CostEstimate(flops=flops, bytes_accessed=nbytes, transcendentals=0)


def dot(a, b):
    return jnp.dot(a, b, preferred_element_type=F32)


def two(value):
    top = value.astype(BF16)
    return top, (value - top.astype(F32)).astype(BF16)


def fold(value):
    rows, cols = value.shape
    total = value[:, :LANES]
    for j in range(1, cols // LANES):
        total = total + value[:, j * LANES : (j + 1) * LANES]
    return total.reshape(rows // 8, 8, LANES).sum(axis=0)


def everywhere(value):
    return jnp.sum(value, axis=(0, 1), keepdims=True)


def invert(slots_ref, inverse_ref):
    for owner in range(slots_ref.shape[1]):
        inverse_ref[slots_ref[0, owner]] = owner


def own_band(slots_ref, columns):
    return lax.div(slots_ref[0, lax.axis_index("fsdp")], columns)


def pack(slots, q_values, scales, sums_of, width, start, part):
    owners = slots.shape[1]
    rows, cols = q_values.shape
    columns = cols // width
    groups = width // LANES
    here = part // LANES
    tall = here * rows + EXTRA
    sums = EXTRA - groups

    def body(slots_hbm, q_hbm, s_hbm, *rest):
        e_hbm = rest[: len(sums_of)]
        out_hbm, slots_ref, inverse, q_ref, s_ref, e_ref, turned, out_ref, ins, outs = rest[-10:]

        def q_read(k):
            at = pl.ds(pl.multiple_of(k * width + start, LANES), part)
            return pltpu.make_async_copy(q_hbm.at[:, at], q_ref.at[k], ins.at[k])

        def write(k, band):
            at = band * columns + k
            return pltpu.make_async_copy(out_ref.at[k], out_hbm.at[inverse[at]], outs.at[at])

        reads = [
            pltpu.make_async_copy(slots_hbm, slots_ref, ins.at[columns]),
            pltpu.make_async_copy(s_hbm, s_ref, ins.at[columns + 1]),
        ]
        for k, src in enumerate(e_hbm):
            reads.append(pltpu.make_async_copy(src, e_ref.at[k], ins.at[columns + 2 + k]))
        for read in reads:
            read.start()

        @pl.loop(0, columns)
        def _(k):
            q_read(k).start()

        for read in reads:
            read.wait()
        invert(slots_ref, inverse)
        padded = jnp.concatenate([s_ref[...].astype(F32), jnp.zeros((LANES - rows, LANES), F32)], axis=0)
        turned[...] = padded.T
        head = jnp.zeros((sums, LANES), F32)
        if e_hbm:
            value = e_ref[0]
            for k in range(1, len(e_hbm)):
                value = value + e_ref[k]
            high = value.astype(BF16)
            mid, low = two(value - high.astype(F32))
            row = lax.broadcasted_iota(jnp.int32, head.shape, 0)
            for k, term in enumerate((high, mid, low)):
                head = jnp.where(row == k, jnp.broadcast_to(term[:1].astype(F32), head.shape), head)

        @pl.loop(0, columns)
        def _(k):
            scale = turned[pl.ds(pl.multiple_of(k * groups, groups), groups), :]
            out_ref[k, here * rows :, :] = jnp.concatenate([head, scale], axis=0).astype(BF16)
            q_read(k).wait()
            for j in range(here):
                out_ref[k, j * rows : (j + 1) * rows, :] = q_ref[k, :, j * LANES : (j + 1) * LANES]
            for band in range(owners // columns):
                write(k, band).start()

        @pl.loop(0, columns)
        def _(k):
            for band in range(owners // columns):
                write(k, band).wait()

    operands = [slots, q_values, scales, *sums_of]
    return pl.pallas_call(
        body,
        out_shape=jax.ShapeDtypeStruct((owners, tall, LANES), BF16),
        in_specs=[HBM] * len(operands),
        out_specs=HBM,
        scratch_shapes=[
            pltpu.SMEM(slots.shape, jnp.int32),
            pltpu.SMEM((owners,), jnp.int32),
            pltpu.VMEM((columns, rows, part), BF16),
            pltpu.VMEM(scales.shape, BF16),
            pltpu.VMEM((max(len(sums_of), 1), 8, LANES), F32),
            pltpu.VMEM((LANES, LANES), F32),
            pltpu.VMEM((columns, tall, LANES), BF16),
            DMA((columns + 2 + len(sums_of),)),
            DMA((owners,)),
        ],
        compiler_params=grant(16 if sums_of else 60),
        cost_estimate=cost(0, 2 * rows * cols + 2 * owners * tall * LANES),
        name=f"pack_{start}",
    )(*operands)


def square_sum(q_values, scales):
    rows, cols = q_values.shape
    groups = scales.shape[1]
    group = cols // groups

    def body(q_hbm, s_hbm, out_ref, q_ref, s_ref, sems):
        reads = [pltpu.make_async_copy(q_hbm, q_ref, sems.at[0]), pltpu.make_async_copy(s_hbm, s_ref, sems.at[1])]
        for read in reads:
            read.start()
        for read in reads:
            read.wait()
        total = jnp.zeros((rows, group), F32)
        for j in range(groups):
            grad = q_ref[:, j * group : (j + 1) * group].astype(F32) * s_ref[:, j : j + 1].astype(F32)
            total = total + grad * grad
        out_ref[...] = jnp.full((8, LANES), jnp.sum(total))

    return pl.pallas_call(
        body,
        out_shape=jax.ShapeDtypeStruct((8, LANES), F32),
        in_specs=[HBM] * 2,
        scratch_shapes=[pltpu.VMEM((rows, cols), BF16), pltpu.VMEM(scales.shape, BF16), DMA((2,))],
        compiler_params=grant(60),
        cost_estimate=cost(3 * rows * cols, 2 * rows * cols),
        name="square_sum",
    )(q_values, scales)


def split_roots(left, right):
    size = left.shape[0]

    def body(l_ref, r_ref, l1_ref, l2_ref, r1_ref, r2_ref):
        @pl.loop(0, size // FINE)
        def _(k):
            at = pl.ds(pl.multiple_of(k * FINE, FINE), FINE)
            l1_ref[at, :], l2_ref[at, :] = two(l_ref[at, :])
            r1_ref[at, :], r2_ref[at, :] = two(r_ref[at, :])

    return pl.pallas_call(
        body,
        out_shape=[jax.ShapeDtypeStruct((size, size), BF16)] * 4,
        in_specs=[VMEM] * 2,
        out_specs=[VMEM] * 4,
        compiler_params=grant(20),
        cost_estimate=cost(4 * size * size, 16 * size * size),
        name="split_roots",
    )(left, right)


def dequant(a_ref, band, pieces, rows, group, grad_ref, h1, h2):
    tall = a_ref.shape[1]
    here = (tall - EXTRA) // rows

    @pl.loop(0, pieces)
    def _(piece):
        source = band * pieces + piece
        scales = a_ref[source, here * rows :, :].astype(F32).T
        at = pl.ds(pl.multiple_of(piece * rows, rows), rows)
        for j in range(here):
            column = EXTRA - 8 + group + j
            grad = a_ref[source, j * rows : (j + 1) * rows, :].astype(F32) * scales[:rows, column : column + 1]
            lanes = slice(j * LANES, (j + 1) * LANES)
            grad_ref[at, lanes] = grad
            h1[at, lanes], h2[at, lanes] = two(grad)


def products(slots, arrived, l1, l2, r1, r2, rows, columns):
    size = l1.shape[0]
    _, tall, _ = arrived.shape
    pieces = size // rows
    part = tall // rows * LANES
    block = size // STEPS

    def body(slots_ref, a_ref, l1_ref, l2_ref, r1_ref, r2_ref, p_ref, grad_ref, h1, h2, t1, t2):
        dequant(a_ref, own_band(slots_ref, columns), pieces, rows, 0, grad_ref, h1, h2)

        @pl.loop(0, part // block)
        def _(n):
            at = pl.ds(pl.multiple_of(n * block, block), block)
            half = dot(l1_ref[...], h1[:, at]) + (dot(l1_ref[...], h2[:, at]) + dot(l2_ref[...], h1[:, at]))
            t1[:, at], t2[:, at] = two(half)

        @pl.loop(0, STEPS)
        def _(n):
            at = pl.ds(pl.multiple_of(n * block, block), block)
            r1_at, r2_at = r1_ref[:part, at], r2_ref[:part, at]
            p_ref[:, at] = dot(t1[...], r1_at) + (dot(t1[...], r2_at) + dot(t2[...], r1_at))

    square = (size, size)
    narrow = (size, part)
    return pl.pallas_call(
        body,
        out_shape=[jax.ShapeDtypeStruct(square, F32), jax.ShapeDtypeStruct(narrow, F32)],
        in_specs=[SMEM] + [VMEM] * 5,
        out_specs=[VMEM] * 2,
        scratch_shapes=[pltpu.VMEM(narrow, BF16)] * 4,
        compiler_params=grant(26),
        cost_estimate=cost(12 * size * size * part, 20 * size * size),
        name="products",
    )(slots, arrived, l1, l2, r1, r2)


def graft(slots, arrived, l1, l2, r1, r2, earlier, grad, moment, rows, columns, entries):
    size = moment.shape[0]
    owners, tall, _ = arrived.shape
    pieces = size // rows
    block = size // STEPS
    done = grad.shape[1]
    part = size - done
    thin = size // FINE

    def body(
        slots_ref, a_ref, l1_ref, l2_ref, r1_ref, r2_ref, p_ref, old_ref, m_hbm, out_hbm, fresh_hbm,
        new_ref, h1, h2, t1, t2, all_ref, m_ref, out_ref, asum, psum, outs,
    ):
        band = own_band(slots_ref, columns)

        def cut(n):
            return pl.ds(pl.multiple_of(n * block, block), block)

        m_read = pltpu.make_async_copy(m_hbm, m_ref, outs.at[2, 0])
        m_read.start()
        dequant(a_ref, band, pieces, rows, done // LANES, new_ref, h1, h2)
        heads = jnp.sum(a_ref[:, tall - EXTRA :, :].astype(F32), axis=0)[: EXTRA - 8]
        total = jnp.sum(heads, axis=0, keepdims=True)[:, :1]
        bound = 0.5 * jnp.sqrt(jnp.full((1, 1), entries, F32)) / jnp.sqrt(jnp.where(total > 0, total, 1.0))
        clip = jnp.where(total > 0, jnp.minimum(bound, 1.0), 1.0)
        asum[...] = jnp.zeros_like(asum)
        psum[...] = jnp.zeros_like(psum)
        half = dot(l1_ref[...], h1[...]) + (dot(l1_ref[...], h2[...]) + dot(l2_ref[...], h1[...]))
        t1[...], t2[...] = two(half)

        m_read.wait()

        def fresh_copy(n):
            return pltpu.make_async_copy(m_ref.at[cut(n)], fresh_hbm.at[cut(n)], outs.at[0, n])

        def out_copy(n):
            to = pl.ds(pl.multiple_of(band * size + n * block, block), block)
            return pltpu.make_async_copy(out_ref.at[cut(n)], out_hbm.at[to], outs.at[1, n])

        def adam(line, lanes, grads):
            held = grads * clip
            square = held * held
            fresh = 0.9 * m_ref[line, lanes] + 0.1 * square
            m_ref[line, lanes] = fresh
            root = fresh * lax.rsqrt(fresh) + 1e-08
            asum[...] += fold(square / (root * root))

        @pl.loop(0, STEPS)
        def _(n):
            at = cut(n)
            r1_at, r2_at = r1_ref[done:, at], r2_ref[done:, at]
            more = dot(t1[...], r1_at) + (dot(t1[...], r2_at) + dot(t2[...], r1_at))
            product = p_ref[:, at] + more
            all_ref[:, at] = product
            psum[...] += fold(product * product)

            @pl.loop(0, block // thin)
            def _(k):
                line = pl.ds(pl.multiple_of(n * block + k * thin, thin), thin)
                adam(line, slice(0, done), old_ref[line, :])
                adam(line, slice(done, size), new_ref[line, :])

            fresh_copy(n).start()

        norm = jnp.sqrt(everywhere(psum[...]) * (clip * clip) + 1e-12)
        ratio = clip * (jnp.sqrt(everywhere(asum[...])) / norm)

        @pl.loop(0, STEPS)
        def _(n):
            out_ref[cut(n), :] = (all_ref[cut(n), :] * ratio).astype(BF16)
            out_copy(n).start()

        for n in range(STEPS):
            fresh_copy(n).wait()
            out_copy(n).wait()

    square = (size, size)
    return pl.pallas_call(
        body,
        out_shape=[
            jax.ShapeDtypeStruct((owners * rows, size), BF16),
            jax.ShapeDtypeStruct(square, F32),
        ],
        in_specs=[SMEM] + [VMEM] * 7 + [HBM],
        out_specs=[HBM, HBM],
        scratch_shapes=[pltpu.VMEM((size, part), F32)]
        + [pltpu.VMEM((size, part), BF16)] * 4
        + [
            pltpu.VMEM(square, F32),
            pltpu.VMEM(square, F32),
            pltpu.VMEM(square, BF16),
            pltpu.VMEM((8, LANES), F32),
            pltpu.VMEM((8, LANES), F32),
            DMA((3, STEPS)),
        ],
        compiler_params=grant(24),
        cost_estimate=cost(12 * size * size * part, 24 * size * size),
        name="graft",
    )(slots, arrived, l1, l2, r1, r2, earlier, grad, moment)


def place(slots, returned, cols):
    owners, rows, width = returned.shape
    columns = cols // width

    def body(slots_ref, r_hbm, out_hbm, inverse, out_ref, ins, outs):
        first = lax.div(lax.axis_index("fsdp") * rows, width) * columns
        invert(slots_ref, inverse)

        def here(k):
            return pl.ds(pl.multiple_of(k * width, width), width)

        def read(k):
            return pltpu.make_async_copy(r_hbm.at[inverse[first + k]], out_ref.at[:, here(k)], ins.at[k])

        def write(k):
            return pltpu.make_async_copy(out_ref.at[:, here(k)], out_hbm.at[:, here(k)], outs.at[k])

        @pl.loop(0, columns)
        def _(k):
            read(k).start()

        @pl.loop(0, columns)
        def _(k):
            read(k).wait()
            write(k).start()

        @pl.loop(0, columns)
        def _(k):
            write(k).wait()

    return pl.pallas_call(
        body,
        out_shape=jax.ShapeDtypeStruct((rows, cols), BF16),
        in_specs=[SMEM, HBM],
        out_specs=HBM,
        scratch_shapes=[
            pltpu.SMEM((owners,), jnp.int32),
            pltpu.VMEM((rows, cols), BF16),
            DMA((columns,)),
            DMA((columns,)),
        ],
        compiler_params=grant(60),
        cost_estimate=cost(0, 4 * rows * cols),
        name="place",
    )(slots, returned)


def on_device(q_values, scales, block_slots, left_root, right_root, second_moment):
    count = lax.axis_size("fsdp")
    planes = lax.axis_size("grp")
    rows, cols = q_values.shape
    width = left_root.shape[-1]
    columns = cols // width
    first = width * 3 // 4

    def exchange(value):
        return lax.all_to_all(value, "fsdp", split_axis=0, concat_axis=0, tiled=True)

    arrived = exchange(pack(block_slots, q_values, scales, [], width, 0, first))
    own = square_sum(q_values, scales)
    sums = [own]
    for k in range(1, planes):
        sums.append(lax.ppermute(own, "grp", [(i, (i + k) % planes) for i in range(planes)]))
    *sums, l1, l2, r1, r2 = lax.optimization_barrier((*sums, *split_roots(left_root[0, 0], right_root[0, 0])))
    roots = (l1, l2, r1, r2)
    later = exchange(pack(block_slots, q_values, scales, sums, width, first, width - first))

    product, grad = products(block_slots, arrived, *roots, rows, columns)
    outgoing, fresh = graft(
        block_slots, later, *roots, product, grad, second_moment[0, 0], rows, columns, rows * count * cols * planes
    )
    update = place(block_slots, exchange(outgoing.reshape(count, rows, width)), cols)
    return (update, fresh[None, None])


def solution(mesh):
    in_specs = (
        P("fsdp", "grp"),
        P("fsdp", "grp"),
        P("grp", None),
        P("grp", "fsdp", None, None),
        P("grp", "fsdp", None, None),
        P("grp", "fsdp", None, None),
    )
    out_specs = (P("fsdp", "grp"), P("grp", "fsdp", None, None))
    return jax.shard_map(
        on_device, mesh=mesh, in_specs=in_specs, out_specs=out_specs, check_vma=False
    )
```

```python
import jax
import jax.numpy as jnp
from jax import lax
from jax.experimental import pallas as pl
from jax.experimental.pallas import tpu as pltpu
from jax.sharding import PartitionSpec as P

LANES = 128
EXTRA = 16
STEPS = 4
FINE = 8
F32 = jnp.float32
BF16 = jnp.bfloat16
HBM = pl.BlockSpec(memory_space=pltpu.HBM)
SMEM = pl.BlockSpec(memory_space=pltpu.SMEM)
PARAMS = pltpu.CompilerParams(vmem_limit_bytes=63 * 1024 * 1024)
DMA = pltpu.SemaphoreType.DMA


def cost(flops, nbytes):
    return pl.CostEstimate(flops=flops, bytes_accessed=nbytes, transcendentals=0)


def dot(a, b):
    return jnp.dot(a, b, preferred_element_type=F32)


def two(value):
    top = value.astype(BF16)
    return top, (value - top.astype(F32)).astype(BF16)


def fold(value):
    rows, cols = value.shape
    total = value[:, :LANES]
    for j in range(1, cols // LANES):
        total = total + value[:, j * LANES : (j + 1) * LANES]
    return total.reshape(rows // 8, 8, LANES).sum(axis=0)


def everywhere(value):
    return jnp.sum(value, axis=(0, 1), keepdims=True)


def invert(slots_ref, inverse_ref):
    for owner in range(slots_ref.shape[1]):
        inverse_ref[slots_ref[0, owner]] = owner


def own_band(slots_ref, columns):
    return lax.div(slots_ref[0, lax.axis_index("fsdp")], columns)


def pack(slots, q_values, scales, sums_of, width, start, part):
    owners = slots.shape[1]
    rows, cols = q_values.shape
    columns = cols // width
    groups = width // LANES
    here = part // LANES
    tall = here * rows + EXTRA
    sums = EXTRA - groups

    def body(slots_hbm, q_hbm, s_hbm, *rest):
        e_hbm = rest[: len(sums_of)]
        out_hbm, slots_ref, inverse, q_ref, s_ref, e_ref, turned, out_ref, ins, outs = rest[-10:]

        def q_read(k):
            at = pl.ds(pl.multiple_of(k * width + start, LANES), part)
            return pltpu.make_async_copy(q_hbm.at[:, at], q_ref.at[k], ins.at[k])

        def write(k, band):
            at = band * columns + k
            return pltpu.make_async_copy(out_ref.at[k], out_hbm.at[inverse[at]], outs.at[at])

        reads = [
            pltpu.make_async_copy(slots_hbm, slots_ref, ins.at[columns]),
            pltpu.make_async_copy(s_hbm, s_ref, ins.at[columns + 1]),
        ]
        for k, src in enumerate(e_hbm):
            reads.append(pltpu.make_async_copy(src, e_ref.at[k], ins.at[columns + 2 + k]))
        for read in reads:
            read.start()

        @pl.loop(0, columns)
        def _(k):
            q_read(k).start()

        for read in reads:
            read.wait()
        invert(slots_ref, inverse)
        padded = jnp.concatenate([s_ref[...].astype(F32), jnp.zeros((LANES - rows, LANES), F32)], axis=0)
        turned[...] = padded.T
        head = jnp.zeros((sums, LANES), F32)
        if e_hbm:
            value = e_ref[0]
            for k in range(1, len(e_hbm)):
                value = value + e_ref[k]
            high = value.astype(BF16)
            mid, low = two(value - high.astype(F32))
            row = lax.broadcasted_iota(jnp.int32, head.shape, 0)
            for k, term in enumerate((high, mid, low)):
                head = jnp.where(row == k, jnp.broadcast_to(term[:1].astype(F32), head.shape), head)

        @pl.loop(0, columns)
        def _(k):
            scale = turned[pl.ds(pl.multiple_of(k * groups, groups), groups), :]
            out_ref[k, here * rows :, :] = jnp.concatenate([head, scale], axis=0).astype(BF16)
            q_read(k).wait()
            for j in range(here):
                out_ref[k, j * rows : (j + 1) * rows, :] = q_ref[k, :, j * LANES : (j + 1) * LANES]
            for band in range(owners // columns):
                write(k, band).start()

        @pl.loop(0, columns)
        def _(k):
            for band in range(owners // columns):
                write(k, band).wait()

    operands = [slots, q_values, scales, *sums_of]
    return pl.pallas_call(
        body,
        out_shape=jax.ShapeDtypeStruct((owners, tall, LANES), BF16),
        in_specs=[HBM] * len(operands),
        out_specs=HBM,
        scratch_shapes=[
            pltpu.SMEM(slots.shape, jnp.int32),
            pltpu.SMEM((owners,), jnp.int32),
            pltpu.VMEM((columns, rows, part), BF16),
            pltpu.VMEM(scales.shape, BF16),
            pltpu.VMEM((max(len(sums_of), 1), 8, LANES), F32),
            pltpu.VMEM((LANES, LANES), F32),
            pltpu.VMEM((columns, tall, LANES), BF16),
            DMA((columns + 2 + len(sums_of),)),
            DMA((owners,)),
        ],
        compiler_params=PARAMS,
        cost_estimate=cost(0, 2 * rows * cols + 2 * owners * tall * LANES),
        name=f"pack_{start}",
    )(*operands)


def square_sum(q_values, scales):
    rows, cols = q_values.shape
    groups = scales.shape[1]
    group = cols // groups

    def body(q_hbm, s_hbm, out_ref, q_ref, s_ref, sems):
        reads = [pltpu.make_async_copy(q_hbm, q_ref, sems.at[0]), pltpu.make_async_copy(s_hbm, s_ref, sems.at[1])]
        for read in reads:
            read.start()
        for read in reads:
            read.wait()
        total = jnp.zeros((rows, group), F32)
        for j in range(groups):
            grad = q_ref[:, j * group : (j + 1) * group].astype(F32) * s_ref[:, j : j + 1].astype(F32)
            total = total + grad * grad
        out_ref[...] = jnp.full((8, LANES), jnp.sum(total))

    return pl.pallas_call(
        body,
        out_shape=jax.ShapeDtypeStruct((8, LANES), F32),
        in_specs=[HBM] * 2,
        scratch_shapes=[pltpu.VMEM((rows, cols), BF16), pltpu.VMEM(scales.shape, BF16), DMA((2,))],
        compiler_params=PARAMS,
        cost_estimate=cost(3 * rows * cols, 2 * rows * cols),
        name="square_sum",
    )(q_values, scales)


def split_roots(left, right):
    size = left.shape[0]
    rows = size // STEPS

    def body(l_hbm, r_hbm, l1_hbm, l2_hbm, r1_hbm, r2_hbm, full, top, low, ins, outs):
        jobs = []
        for src, high_hbm, low_hbm in ((l_hbm, l1_hbm, l2_hbm), (r_hbm, r1_hbm, r2_hbm)):
            for n in range(STEPS):
                at = pl.ds(n * rows, rows)
                jobs.append((src.at[at], high_hbm.at[at], low_hbm.at[at]))
        reads = [pltpu.make_async_copy(job[0], full.at[k], ins.at[k]) for k, job in enumerate(jobs)]
        for read in reads:
            read.start()
        writes = []
        for k, (_, high_to, low_to) in enumerate(jobs):
            reads[k].wait()
            top[k], low[k] = two(full[k])
            for h, (src, to) in enumerate(((top.at[k], high_to), (low.at[k], low_to))):
                write = pltpu.make_async_copy(src, to, outs.at[2 * k + h])
                write.start()
                writes.append(write)
        for write in writes:
            write.wait()

    jobs = 2 * STEPS
    return pl.pallas_call(
        body,
        out_shape=[jax.ShapeDtypeStruct((size, size), BF16)] * 4,
        in_specs=[HBM] * 2,
        out_specs=[HBM] * 4,
        scratch_shapes=[
            pltpu.VMEM((jobs, rows, size), F32),
            pltpu.VMEM((jobs, rows, size), BF16),
            pltpu.VMEM((jobs, rows, size), BF16),
            DMA((jobs,)),
            DMA((2 * jobs,)),
        ],
        compiler_params=PARAMS,
        cost_estimate=cost(4 * size * size, 16 * size * size),
        name="split_roots",
    )(left, right)


def dequant(a_ref, turned, rows, group, at_lane, grad_ref, h1, h2):
    pieces, tall, _ = a_ref.shape
    here = (tall - EXTRA) // rows
    scales = a_ref[:, here * rows :, :].astype(F32).reshape(pieces * EXTRA, LANES)
    turned[...] = scales.T
    for piece in range(pieces):
        at = slice(piece * rows, (piece + 1) * rows)
        for j in range(here):
            column = piece * EXTRA + EXTRA - 8 + group + j
            grad = a_ref[piece, j * rows : (j + 1) * rows, :].astype(F32) * turned[:rows, column : column + 1]
            grad_ref[at, at_lane + j * LANES : at_lane + (j + 1) * LANES] = grad
            lanes = slice(j * LANES, (j + 1) * LANES)
            h1[at, lanes], h2[at, lanes] = two(grad)


def products(slots, arrived, l1, l2, r1, r2, rows, columns):
    size = l1.shape[0]
    _, tall, _ = arrived.shape
    pieces = size // rows
    part = tall // rows * LANES
    block = size // STEPS

    def body(
        slots_ref, a_hbm, l1_hbm, l2_hbm, r1_hbm, r2_hbm, p_hbm, grad_hbm,
        a_ref, l1_ref, l2_ref, r1_ref, r2_ref, grad_ref, h1, h2, t1, t2, p_ref, turned, ins, outs,
    ):
        band = own_band(slots_ref, columns)
        deep = pl.ds(0, part)
        pairs = (
            (a_hbm.at[pl.ds(band * pieces, pieces)], a_ref),
            (l1_hbm, l1_ref),
            (l2_hbm, l2_ref),
            (r1_hbm.at[deep], r1_ref),
            (r2_hbm.at[deep], r2_ref),
        )
        reads = [pltpu.make_async_copy(s, t, ins.at[k]) for k, (s, t) in enumerate(pairs)]
        for read in reads:
            read.start()
        reads[0].wait()
        dequant(a_ref, turned, rows, 0, 0, grad_ref, h1, h2)
        for read in reads[1:3]:
            read.wait()
        keep = pltpu.make_async_copy(grad_ref, grad_hbm, outs.at[STEPS])
        keep.start()

        @pl.loop(0, part // block)
        def _(n):
            at = pl.ds(pl.multiple_of(n * block, block), block)
            half = dot(l1_ref[...], h1[:, at]) + (dot(l1_ref[...], h2[:, at]) + dot(l2_ref[...], h1[:, at]))
            t1[:, at], t2[:, at] = two(half)

        for read in reads[3:]:
            read.wait()

        def p_copy(n):
            at = pl.ds(pl.multiple_of(n * block, block), block)
            return pltpu.make_async_copy(p_ref.at[:, at], p_hbm.at[:, at], outs.at[n])

        @pl.loop(0, STEPS)
        def _(n):
            at = pl.ds(pl.multiple_of(n * block, block), block)
            p_ref[:, at] = dot(t1[...], r1_ref[:, at]) + (dot(t1[...], r2_ref[:, at]) + dot(t2[...], r1_ref[:, at]))
            p_copy(n).start()

        for n in range(STEPS):
            p_copy(n).wait()
        keep.wait()

    square = (size, size)
    narrow = (size, part)
    return pl.pallas_call(
        body,
        out_shape=[jax.ShapeDtypeStruct(square, F32), jax.ShapeDtypeStruct(narrow, F32)],
        in_specs=[SMEM] + [HBM] * 5,
        out_specs=[HBM] * 2,
        scratch_shapes=[pltpu.VMEM((pieces, tall, LANES), BF16)]
        + [pltpu.VMEM(square, BF16)] * 2
        + [pltpu.VMEM((part, size), BF16)] * 2
        + [pltpu.VMEM(narrow, F32)]
        + [pltpu.VMEM(narrow, BF16)] * 4
        + [pltpu.VMEM(square, F32), pltpu.VMEM((LANES, pieces * EXTRA), F32), DMA((5,)), DMA((STEPS + 1,))],
        compiler_params=PARAMS,
        cost_estimate=cost(12 * size * size * part, 20 * size * size),
        name="products",
    )(slots, arrived, l1, l2, r1, r2)


def graft(slots, arrived, l1, l2, r1, r2, earlier, grad, moment, rows, columns, entries):
    size = moment.shape[0]
    owners, tall, _ = arrived.shape
    pieces = size // rows
    block = size // STEPS
    done = grad.shape[1]
    part = size - done
    thin = size // FINE

    def body(
        slots_ref, a_hbm, l1_hbm, l2_hbm, r1_hbm, r2_hbm, p_hbm, grad_hbm, m_hbm, out_hbm, fresh_hbm,
        sums_ref, a_ref, l1_ref, l2_ref, r1_ref, r2_ref, p_ref, grad_ref, h1, h2, t1, t2, m_ref, out_ref,
        turned, asum, psum, ins, outs,
    ):
        band = own_band(slots_ref, columns)
        deep = pl.ds(done, part)

        def cut(n):
            return pl.ds(pl.multiple_of(n * block, block), block)

        pairs = (
            (a_hbm.at[pl.ds(band * pieces, pieces)], a_ref),
            (a_hbm.at[:, pl.ds(tall - EXTRA, EXTRA)], sums_ref),
            (l1_hbm, l1_ref),
            (l2_hbm, l2_ref),
            (r1_hbm.at[deep], r1_ref),
            (r2_hbm.at[deep], r2_ref),
        )
        reads = [pltpu.make_async_copy(s, t, ins.at[3, k]) for k, (s, t) in enumerate(pairs)]

        def step_reads(n):
            at = cut(n)
            pairs = (
                (p_hbm.at[:, at], p_ref.at[:, at]),
                (grad_hbm.at[at], grad_ref.at[at, pl.ds(0, done)]),
                (m_hbm.at[at], m_ref.at[at]),
            )
            return [pltpu.make_async_copy(s, t, ins.at[k, n]) for k, (s, t) in enumerate(pairs)]

        for read in reads:
            read.start()

        @pl.loop(0, STEPS)
        def _(n):
            for read in step_reads(n):
                read.start()

        for read in reads[:2]:
            read.wait()
        dequant(a_ref, turned, rows, done // LANES, done, grad_ref, h1, h2)
        heads = jnp.sum(sums_ref[...].astype(F32), axis=0)[: EXTRA - 8]
        total = jnp.sum(heads, axis=0, keepdims=True)[:, :1]
        bound = 0.5 * jnp.sqrt(jnp.full((1, 1), entries, F32)) / jnp.sqrt(jnp.where(total > 0, total, 1.0))
        clip = jnp.where(total > 0, jnp.minimum(bound, 1.0), 1.0)
        asum[...] = jnp.zeros_like(asum)
        psum[...] = jnp.zeros_like(psum)
        for read in reads[2:4]:
            read.wait()
        half = dot(l1_ref[...], h1[...]) + (dot(l1_ref[...], h2[...]) + dot(l2_ref[...], h1[...]))
        t1[...], t2[...] = two(half)
        for read in reads[4:]:
            read.wait()

        def fresh_copy(n):
            return pltpu.make_async_copy(m_ref.at[cut(n)], fresh_hbm.at[cut(n)], outs.at[0, n])

        def out_copy(n):
            to = pl.ds(pl.multiple_of(band * size + n * block, block), block)
            return pltpu.make_async_copy(out_ref.at[cut(n)], out_hbm.at[to], outs.at[1, n])

        @pl.loop(0, STEPS)
        def _(n):
            for read in step_reads(n):
                read.wait()
            at = cut(n)
            more = dot(t1[...], r1_ref[:, at]) + (dot(t1[...], r2_ref[:, at]) + dot(t2[...], r1_ref[:, at]))
            product = p_ref[:, at] + more
            p_ref[:, at] = product
            psum[...] += fold(product * product)

            @pl.loop(0, block // thin)
            def _(k):
                line = pl.ds(pl.multiple_of(n * block + k * thin, thin), thin)
                held = grad_ref[line, :] * clip
                square = held * held
                fresh = 0.9 * m_ref[line, :] + 0.1 * square
                m_ref[line, :] = fresh
                root = fresh * lax.rsqrt(fresh) + 1e-08
                inverse = pl.reciprocal(root, approx=True)
                adam = held * (inverse * (2.0 - root * inverse))
                asum[...] += fold(adam * adam)

            fresh_copy(n).start()

        norm = jnp.sqrt(everywhere(psum[...]) * (clip * clip) + 1e-12)
        ratio = clip * (jnp.sqrt(everywhere(asum[...])) / norm)

        @pl.loop(0, STEPS)
        def _(n):
            out_ref[cut(n), :] = (p_ref[cut(n), :] * ratio).astype(BF16)
            out_copy(n).start()

        for n in range(STEPS):
            fresh_copy(n).wait()
            out_copy(n).wait()

    square = (size, size)
    return pl.pallas_call(
        body,
        out_shape=[
            jax.ShapeDtypeStruct((owners * rows, size), BF16),
            jax.ShapeDtypeStruct(square, F32),
        ],
        in_specs=[SMEM] + [HBM] * 8,
        out_specs=[HBM, HBM],
        scratch_shapes=[pltpu.VMEM((owners, EXTRA, LANES), BF16), pltpu.VMEM((pieces, tall, LANES), BF16)]
        + [pltpu.VMEM(square, BF16)] * 2
        + [pltpu.VMEM((part, size), BF16)] * 2
        + [pltpu.VMEM(square, F32)] * 2
        + [pltpu.VMEM((size, part), BF16)] * 4
        + [
            pltpu.VMEM(square, F32),
            pltpu.VMEM(square, BF16),
            pltpu.VMEM((LANES, pieces * EXTRA), F32),
            pltpu.VMEM((8, LANES), F32),
            pltpu.VMEM((8, LANES), F32),
            DMA((4, 6)),
            DMA((2, STEPS)),
        ],
        compiler_params=PARAMS,
        cost_estimate=cost(12 * size * size * part, 24 * size * size),
        name="graft",
    )(slots, arrived, l1, l2, r1, r2, earlier, grad, moment)


def place(slots, returned, cols):
    owners, rows, width = returned.shape
    columns = cols // width

    def body(slots_ref, r_hbm, out_hbm, inverse, out_ref, ins, outs):
        first = lax.div(lax.axis_index("fsdp") * rows, width) * columns
        invert(slots_ref, inverse)

        def here(k):
            return pl.ds(pl.multiple_of(k * width, width), width)

        def read(k):
            return pltpu.make_async_copy(r_hbm.at[inverse[first + k]], out_ref.at[:, here(k)], ins.at[k])

        def write(k):
            return pltpu.make_async_copy(out_ref.at[:, here(k)], out_hbm.at[:, here(k)], outs.at[k])

        @pl.loop(0, columns)
        def _(k):
            read(k).start()

        @pl.loop(0, columns)
        def _(k):
            read(k).wait()
            write(k).start()

        @pl.loop(0, columns)
        def _(k):
            write(k).wait()

    return pl.pallas_call(
        body,
        out_shape=jax.ShapeDtypeStruct((rows, cols), BF16),
        in_specs=[SMEM, HBM],
        out_specs=HBM,
        scratch_shapes=[
            pltpu.SMEM((owners,), jnp.int32),
            pltpu.VMEM((rows, cols), BF16),
            DMA((columns,)),
            DMA((columns,)),
        ],
        compiler_params=PARAMS,
        cost_estimate=cost(0, 4 * rows * cols),
        name="place",
    )(slots, returned)


def on_device(q_values, scales, block_slots, left_root, right_root, second_moment):
    count = lax.axis_size("fsdp")
    planes = lax.axis_size("grp")
    rows, cols = q_values.shape
    width = left_root.shape[-1]
    columns = cols // width
    first = width * 3 // 4

    def exchange(value):
        return lax.all_to_all(value, "fsdp", split_axis=0, concat_axis=0, tiled=True)

    arrived = exchange(pack(block_slots, q_values, scales, [], width, 0, first))
    own = square_sum(q_values, scales)
    sums = [own]
    for k in range(1, planes):
        sums.append(lax.ppermute(own, "grp", [(i, (i + k) % planes) for i in range(planes)]))
    *sums, l1, l2, r1, r2 = lax.optimization_barrier((*sums, *split_roots(left_root[0, 0], right_root[0, 0])))
    roots = (l1, l2, r1, r2)
    later = exchange(pack(block_slots, q_values, scales, sums, width, first, width - first))

    product, grad = products(block_slots, arrived, *roots, rows, columns)
    outgoing, fresh = graft(
        block_slots, later, *roots, product, grad, second_moment[0, 0], rows, columns, rows * count * cols * planes
    )
    update = place(block_slots, exchange(outgoing.reshape(count, rows, width)), cols)
    return (update, fresh[None, None])


def solution(mesh):
    in_specs = (
        P("fsdp", "grp"),
        P("fsdp", "grp"),
        P("grp", None),
        P("grp", "fsdp", None, None),
        P("grp", "fsdp", None, None),
        P("grp", "fsdp", None, None),
    )
    out_specs = (P("fsdp", "grp"), P("grp", "fsdp", None, None))
    return jax.shard_map(
        on_device, mesh=mesh, in_specs=in_specs, out_specs=out_specs, check_vma=False
    )
```

```python
import jax
import jax.numpy as jnp
from jax import lax
from jax.experimental import pallas as pl
from jax.experimental.pallas import tpu as pltpu
from jax.sharding import PartitionSpec as P

LANES = 128
EXTRA = 16
STEPS = 4
FINE = 16
F32 = jnp.float32
BF16 = jnp.bfloat16
HBM = pl.BlockSpec(memory_space=pltpu.HBM)
SMEM = pl.BlockSpec(memory_space=pltpu.SMEM)
PARAMS = pltpu.CompilerParams(vmem_limit_bytes=63 * 1024 * 1024)
DMA = pltpu.SemaphoreType.DMA


def cost(flops, nbytes):
    return pl.CostEstimate(flops=flops, bytes_accessed=nbytes, transcendentals=0)


def dot(a, b):
    return jnp.dot(a, b, preferred_element_type=F32)


def two(value):
    top = value.astype(BF16)
    return top, (value - top.astype(F32)).astype(BF16)


def fold(value):
    rows, cols = value.shape
    total = value[:, :LANES]
    for j in range(1, cols // LANES):
        total = total + value[:, j * LANES : (j + 1) * LANES]
    return total.reshape(rows // 8, 8, LANES).sum(axis=0)


def everywhere(value):
    return jnp.sum(value, axis=(0, 1), keepdims=True)


def invert(slots_ref, inverse_ref):
    for owner in range(slots_ref.shape[1]):
        inverse_ref[slots_ref[0, owner]] = owner


def own_band(slots_ref, columns):
    return lax.div(slots_ref[0, lax.axis_index("fsdp")], columns)


def pack(slots, q_values, scales, sums_of, width, start, part):
    owners = slots.shape[1]
    rows, cols = q_values.shape
    columns = cols // width
    groups = width // LANES
    here = part // LANES
    tall = here * rows + EXTRA
    sums = EXTRA - groups

    def body(slots_hbm, q_hbm, s_hbm, *rest):
        e_hbm = rest[: len(sums_of)]
        out_hbm, slots_ref, inverse, q_ref, s_ref, e_ref, turned, out_ref, ins, outs = rest[-10:]

        def q_read(k):
            at = pl.ds(pl.multiple_of(k * width + start, LANES), part)
            return pltpu.make_async_copy(q_hbm.at[:, at], q_ref.at[k], ins.at[k])

        def write(k, band):
            at = band * columns + k
            return pltpu.make_async_copy(out_ref.at[k], out_hbm.at[inverse[at]], outs.at[at])

        reads = [
            pltpu.make_async_copy(slots_hbm, slots_ref, ins.at[columns]),
            pltpu.make_async_copy(s_hbm, s_ref, ins.at[columns + 1]),
        ]
        for k, src in enumerate(e_hbm):
            reads.append(pltpu.make_async_copy(src, e_ref.at[k], ins.at[columns + 2 + k]))
        for read in reads:
            read.start()

        @pl.loop(0, columns)
        def _(k):
            q_read(k).start()

        for read in reads:
            read.wait()
        invert(slots_ref, inverse)
        padded = jnp.concatenate([s_ref[...].astype(F32), jnp.zeros((LANES - rows, LANES), F32)], axis=0)
        turned[...] = padded.T
        head = jnp.zeros((sums, LANES), F32)
        if e_hbm:
            value = e_ref[0]
            for k in range(1, len(e_hbm)):
                value = value + e_ref[k]
            high = value.astype(BF16)
            mid, low = two(value - high.astype(F32))
            row = lax.broadcasted_iota(jnp.int32, head.shape, 0)
            for k, term in enumerate((high, mid, low)):
                head = jnp.where(row == k, jnp.broadcast_to(term[:1].astype(F32), head.shape), head)

        @pl.loop(0, columns)
        def _(k):
            scale = turned[pl.ds(pl.multiple_of(k * groups, groups), groups), :]
            out_ref[k, here * rows :, :] = jnp.concatenate([head, scale], axis=0).astype(BF16)
            q_read(k).wait()
            for j in range(here):
                out_ref[k, j * rows : (j + 1) * rows, :] = q_ref[k, :, j * LANES : (j + 1) * LANES]
            for band in range(owners // columns):
                write(k, band).start()

        @pl.loop(0, columns)
        def _(k):
            for band in range(owners // columns):
                write(k, band).wait()

    operands = [slots, q_values, scales, *sums_of]
    return pl.pallas_call(
        body,
        out_shape=jax.ShapeDtypeStruct((owners, tall, LANES), BF16),
        in_specs=[HBM] * len(operands),
        out_specs=HBM,
        scratch_shapes=[
            pltpu.SMEM(slots.shape, jnp.int32),
            pltpu.SMEM((owners,), jnp.int32),
            pltpu.VMEM((columns, rows, part), BF16),
            pltpu.VMEM(scales.shape, BF16),
            pltpu.VMEM((max(len(sums_of), 1), 8, LANES), F32),
            pltpu.VMEM((LANES, LANES), F32),
            pltpu.VMEM((columns, tall, LANES), BF16),
            DMA((columns + 2 + len(sums_of),)),
            DMA((owners,)),
        ],
        compiler_params=PARAMS,
        cost_estimate=cost(0, 2 * rows * cols + 2 * owners * tall * LANES),
        name=f"pack_{start}",
    )(*operands)


def square_sum(q_values, scales):
    rows, cols = q_values.shape
    groups = scales.shape[1]
    group = cols // groups

    def body(q_hbm, s_hbm, out_ref, q_ref, s_ref, sems):
        reads = [pltpu.make_async_copy(q_hbm, q_ref, sems.at[0]), pltpu.make_async_copy(s_hbm, s_ref, sems.at[1])]
        for read in reads:
            read.start()
        for read in reads:
            read.wait()
        total = jnp.zeros((rows, group), F32)
        for j in range(groups):
            grad = q_ref[:, j * group : (j + 1) * group].astype(F32) * s_ref[:, j : j + 1].astype(F32)
            total = total + grad * grad
        out_ref[...] = jnp.full((8, LANES), jnp.sum(total))

    return pl.pallas_call(
        body,
        out_shape=jax.ShapeDtypeStruct((8, LANES), F32),
        in_specs=[HBM] * 2,
        scratch_shapes=[pltpu.VMEM((rows, cols), BF16), pltpu.VMEM(scales.shape, BF16), DMA((2,))],
        compiler_params=PARAMS,
        cost_estimate=cost(3 * rows * cols, 2 * rows * cols),
        name="square_sum",
    )(q_values, scales)


def split_roots(left, right):
    size = left.shape[0]
    rows = size // STEPS

    def body(l_hbm, r_hbm, l1_hbm, l2_hbm, r1_hbm, r2_hbm, full, top, low, ins, outs):
        jobs = []
        for src, high_hbm, low_hbm in ((l_hbm, l1_hbm, l2_hbm), (r_hbm, r1_hbm, r2_hbm)):
            for n in range(STEPS):
                at = pl.ds(n * rows, rows)
                jobs.append((src.at[at], high_hbm.at[at], low_hbm.at[at]))
        reads = [pltpu.make_async_copy(job[0], full.at[k], ins.at[k]) for k, job in enumerate(jobs)]
        for read in reads:
            read.start()
        writes = []
        for k, (_, high_to, low_to) in enumerate(jobs):
            reads[k].wait()
            top[k], low[k] = two(full[k])
            for h, (src, to) in enumerate(((top.at[k], high_to), (low.at[k], low_to))):
                write = pltpu.make_async_copy(src, to, outs.at[2 * k + h])
                write.start()
                writes.append(write)
        for write in writes:
            write.wait()

    jobs = 2 * STEPS
    return pl.pallas_call(
        body,
        out_shape=[jax.ShapeDtypeStruct((size, size), BF16)] * 4,
        in_specs=[HBM] * 2,
        out_specs=[HBM] * 4,
        scratch_shapes=[
            pltpu.VMEM((jobs, rows, size), F32),
            pltpu.VMEM((jobs, rows, size), BF16),
            pltpu.VMEM((jobs, rows, size), BF16),
            DMA((jobs,)),
            DMA((2 * jobs,)),
        ],
        compiler_params=PARAMS,
        cost_estimate=cost(4 * size * size, 16 * size * size),
        name="split_roots",
    )(left, right)


def dequant(a_ref, turned, rows, group, at_lane, grad_ref, h1, h2):
    pieces, tall, _ = a_ref.shape
    here = (tall - EXTRA) // rows
    scales = a_ref[:, here * rows :, :].astype(F32).reshape(pieces * EXTRA, LANES)
    turned[...] = scales.T
    for piece in range(pieces):
        at = slice(piece * rows, (piece + 1) * rows)
        for j in range(here):
            column = piece * EXTRA + EXTRA - 8 + group + j
            grad = a_ref[piece, j * rows : (j + 1) * rows, :].astype(F32) * turned[:rows, column : column + 1]
            grad_ref[at, at_lane + j * LANES : at_lane + (j + 1) * LANES] = grad
            lanes = slice(j * LANES, (j + 1) * LANES)
            h1[at, lanes], h2[at, lanes] = two(grad)


def products(slots, arrived, l1, l2, r1, r2, rows, columns):
    size = l1.shape[0]
    _, tall, _ = arrived.shape
    pieces = size // rows
    part = tall // rows * LANES
    block = size // STEPS

    def body(
        slots_ref, a_hbm, l1_hbm, l2_hbm, r1_hbm, r2_hbm, p_hbm, grad_hbm,
        a_ref, l1_ref, l2_ref, r1_ref, r2_ref, grad_ref, h1, h2, t1, t2, p_ref, turned, ins, outs,
    ):
        band = own_band(slots_ref, columns)
        deep = pl.ds(0, part)
        pairs = (
            (a_hbm.at[pl.ds(band * pieces, pieces)], a_ref),
            (l1_hbm, l1_ref),
            (l2_hbm, l2_ref),
            (r1_hbm.at[deep], r1_ref),
            (r2_hbm.at[deep], r2_ref),
        )
        reads = [pltpu.make_async_copy(s, t, ins.at[k]) for k, (s, t) in enumerate(pairs)]
        for read in reads[:3]:
            read.start()
        reads[0].wait()
        for read in reads[3:]:
            read.start()
        dequant(a_ref, turned, rows, 0, 0, grad_ref, h1, h2)
        for read in reads[1:3]:
            read.wait()
        keep = pltpu.make_async_copy(grad_ref, grad_hbm, outs.at[STEPS])
        keep.start()

        @pl.loop(0, part // block)
        def _(n):
            at = pl.ds(pl.multiple_of(n * block, block), block)
            half = dot(l1_ref[...], h1[:, at]) + (dot(l1_ref[...], h2[:, at]) + dot(l2_ref[...], h1[:, at]))
            t1[:, at], t2[:, at] = two(half)

        for read in reads[3:]:
            read.wait()

        def p_copy(n):
            at = pl.ds(pl.multiple_of(n * block, block), block)
            return pltpu.make_async_copy(p_ref.at[:, at], p_hbm.at[:, at], outs.at[n])

        @pl.loop(0, STEPS)
        def _(n):
            at = pl.ds(pl.multiple_of(n * block, block), block)
            p_ref[:, at] = dot(t1[...], r1_ref[:, at]) + (dot(t1[...], r2_ref[:, at]) + dot(t2[...], r1_ref[:, at]))
            p_copy(n).start()

        for n in range(STEPS):
            p_copy(n).wait()
        keep.wait()

    square = (size, size)
    narrow = (size, part)
    return pl.pallas_call(
        body,
        out_shape=[jax.ShapeDtypeStruct(square, F32), jax.ShapeDtypeStruct(narrow, F32)],
        in_specs=[SMEM] + [HBM] * 5,
        out_specs=[HBM] * 2,
        scratch_shapes=[pltpu.VMEM((pieces, tall, LANES), BF16)]
        + [pltpu.VMEM(square, BF16)] * 2
        + [pltpu.VMEM((part, size), BF16)] * 2
        + [pltpu.VMEM(narrow, F32)]
        + [pltpu.VMEM(narrow, BF16)] * 4
        + [pltpu.VMEM(square, F32), pltpu.VMEM((LANES, pieces * EXTRA), F32), DMA((5,)), DMA((STEPS + 1,))],
        compiler_params=PARAMS,
        cost_estimate=cost(12 * size * size * part, 20 * size * size),
        name="products",
    )(slots, arrived, l1, l2, r1, r2)


def graft(slots, arrived, l1, l2, r1, r2, earlier, grad, moment, rows, columns, entries):
    size = moment.shape[0]
    owners, tall, _ = arrived.shape
    pieces = size // rows
    block = size // STEPS
    done = grad.shape[1]
    part = size - done
    thin = size // FINE

    def body(
        slots_ref, a_hbm, l1_hbm, l2_hbm, r1_hbm, r2_hbm, p_hbm, grad_hbm, m_hbm, out_hbm, fresh_hbm,
        sums_ref, a_ref, l1_ref, l2_ref, r1_ref, r2_ref, p_ref, grad_ref, h1, h2, t1, t2, m_ref, out_ref,
        turned, asum, psum, ins, outs,
    ):
        band = own_band(slots_ref, columns)
        deep = pl.ds(done, part)

        def cut(n):
            return pl.ds(pl.multiple_of(n * block, block), block)

        pairs = (
            (a_hbm.at[pl.ds(band * pieces, pieces)], a_ref),
            (a_hbm.at[:, pl.ds(tall - EXTRA, EXTRA)], sums_ref),
            (l1_hbm, l1_ref),
            (l2_hbm, l2_ref),
            (r1_hbm.at[deep], r1_ref),
            (r2_hbm.at[deep], r2_ref),
        )
        reads = [pltpu.make_async_copy(s, t, ins.at[3, k]) for k, (s, t) in enumerate(pairs)]

        def step_reads(n):
            at = cut(n)
            pairs = (
                (p_hbm.at[:, at], p_ref.at[:, at]),
                (grad_hbm.at[at], grad_ref.at[at, pl.ds(0, done)]),
                (m_hbm.at[at], m_ref.at[at]),
            )
            return [pltpu.make_async_copy(s, t, ins.at[k, n]) for k, (s, t) in enumerate(pairs)]

        for read in reads[:4]:
            read.start()
        for read in reads[:2]:
            read.wait()
        for read in reads[4:]:
            read.start()

        @pl.loop(0, STEPS)
        def _(n):
            for read in step_reads(n):
                read.start()

        dequant(a_ref, turned, rows, done // LANES, done, grad_ref, h1, h2)
        heads = jnp.sum(sums_ref[...].astype(F32), axis=0)[: EXTRA - 8]
        total = jnp.sum(heads, axis=0, keepdims=True)[:, :1]
        bound = 0.5 * jnp.sqrt(jnp.full((1, 1), entries, F32)) / jnp.sqrt(jnp.where(total > 0, total, 1.0))
        clip = jnp.where(total > 0, jnp.minimum(bound, 1.0), 1.0)
        asum[...] = jnp.zeros_like(asum)
        psum[...] = jnp.zeros_like(psum)
        for read in reads[2:4]:
            read.wait()
        half = dot(l1_ref[...], h1[...]) + (dot(l1_ref[...], h2[...]) + dot(l2_ref[...], h1[...]))
        t1[...], t2[...] = two(half)
        for read in reads[4:]:
            read.wait()

        def fresh_copy(n):
            return pltpu.make_async_copy(m_ref.at[cut(n)], fresh_hbm.at[cut(n)], outs.at[0, n])

        def out_copy(n):
            to = pl.ds(pl.multiple_of(band * size + n * block, block), block)
            return pltpu.make_async_copy(out_ref.at[cut(n)], out_hbm.at[to], outs.at[1, n])

        @pl.loop(0, STEPS)
        def _(n):
            for read in step_reads(n):
                read.wait()
            at = cut(n)
            more = dot(t1[...], r1_ref[:, at]) + (dot(t1[...], r2_ref[:, at]) + dot(t2[...], r1_ref[:, at]))
            product = p_ref[:, at] + more
            p_ref[:, at] = product
            psum[...] += fold(product * product)

            steps = []
            for k in range(block // thin):
                line = pl.ds(pl.multiple_of(n * block + k * thin, thin), thin)
                held = grad_ref[line, :] * clip
                square = held * held
                fresh = 0.9 * m_ref[line, :] + 0.1 * square
                m_ref[line, :] = fresh
                root = fresh * lax.rsqrt(fresh) + 1e-08
                inverse = pl.reciprocal(root, approx=True)
                adam = held * (inverse * (2.0 - root * inverse))
                steps.append(fold(adam * adam))
            asum[...] += sum(steps)
            fresh_copy(n).start()

        norm = jnp.sqrt(everywhere(psum[...]) * (clip * clip) + 1e-12)
        ratio = clip * (jnp.sqrt(everywhere(asum[...])) / norm)

        @pl.loop(0, STEPS)
        def _(n):
            out_ref[cut(n), :] = (p_ref[cut(n), :] * ratio).astype(BF16)
            out_copy(n).start()

        for n in range(STEPS):
            fresh_copy(n).wait()
            out_copy(n).wait()

    square = (size, size)
    return pl.pallas_call(
        body,
        out_shape=[
            jax.ShapeDtypeStruct((owners * rows, size), BF16),
            jax.ShapeDtypeStruct(square, F32),
        ],
        in_specs=[SMEM] + [HBM] * 8,
        out_specs=[HBM, HBM],
        scratch_shapes=[pltpu.VMEM((owners, EXTRA, LANES), BF16), pltpu.VMEM((pieces, tall, LANES), BF16)]
        + [pltpu.VMEM(square, BF16)] * 2
        + [pltpu.VMEM((part, size), BF16)] * 2
        + [pltpu.VMEM(square, F32)] * 2
        + [pltpu.VMEM((size, part), BF16)] * 4
        + [
            pltpu.VMEM(square, F32),
            pltpu.VMEM(square, BF16),
            pltpu.VMEM((LANES, pieces * EXTRA), F32),
            pltpu.VMEM((8, LANES), F32),
            pltpu.VMEM((8, LANES), F32),
            DMA((4, 6)),
            DMA((2, STEPS)),
        ],
        compiler_params=PARAMS,
        cost_estimate=cost(12 * size * size * part, 24 * size * size),
        name="graft",
    )(slots, arrived, l1, l2, r1, r2, earlier, grad, moment)


def place(slots, returned, cols):
    owners, rows, width = returned.shape
    columns = cols // width

    def body(slots_ref, r_ref, out_hbm, inverse, outs):
        first = lax.div(lax.axis_index("fsdp") * rows, width) * columns
        invert(slots_ref, inverse)

        def write(k):
            here = pl.ds(pl.multiple_of(k * width, width), width)
            return pltpu.make_async_copy(r_ref.at[inverse[first + k]], out_hbm.at[:, here], outs.at[k])

        @pl.loop(0, columns)
        def _(k):
            write(k).start()

        @pl.loop(0, columns)
        def _(k):
            write(k).wait()

    return pl.pallas_call(
        body,
        out_shape=jax.ShapeDtypeStruct((rows, cols), BF16),
        in_specs=[SMEM, pl.BlockSpec(memory_space=pltpu.VMEM)],
        out_specs=HBM,
        scratch_shapes=[pltpu.SMEM((owners,), jnp.int32), DMA((columns,))],
        compiler_params=pltpu.CompilerParams(vmem_limit_bytes=12 * 1024 * 1024),
        cost_estimate=cost(0, 4 * rows * cols),
        name="place",
    )(slots, returned)


def on_device(q_values, scales, block_slots, left_root, right_root, second_moment):
    count = lax.axis_size("fsdp")
    planes = lax.axis_size("grp")
    rows, cols = q_values.shape
    width = left_root.shape[-1]
    columns = cols // width
    first = width * 3 // 4

    def exchange(value):
        return lax.all_to_all(value, "fsdp", split_axis=0, concat_axis=0, tiled=True)

    arrived = exchange(pack(block_slots, q_values, scales, [], width, 0, first))
    own = square_sum(q_values, scales)
    sums = [own]
    for k in range(1, planes):
        sums.append(lax.ppermute(own, "grp", [(i, (i + k) % planes) for i in range(planes)]))
    *sums, l1, l2, r1, r2 = lax.optimization_barrier((*sums, *split_roots(left_root[0, 0], right_root[0, 0])))
    roots = (l1, l2, r1, r2)
    later = exchange(pack(block_slots, q_values, scales, sums, width, first, width - first))

    product, grad = products(block_slots, arrived, *roots, rows, columns)
    outgoing, fresh = graft(
        block_slots, later, *roots, product, grad, second_moment[0, 0], rows, columns, rows * count * cols * planes
    )
    update = place(block_slots, exchange(outgoing.reshape(count, rows, width)), cols)
    return (update, fresh[None, None])


def solution(mesh):
    in_specs = (
        P("fsdp", "grp"),
        P("fsdp", "grp"),
        P("grp", None),
        P("grp", "fsdp", None, None),
        P("grp", "fsdp", None, None),
        P("grp", "fsdp", None, None),
    )
    out_specs = (P("fsdp", "grp"), P("grp", "fsdp", None, None))
    return jax.shard_map(
        on_device, mesh=mesh, in_specs=in_specs, out_specs=out_specs, check_vma=False
    )
```

```python
import jax
import jax.numpy as jnp
from jax import lax
from jax.experimental import pallas as pl
from jax.experimental.pallas import tpu as pltpu
from jax.sharding import PartitionSpec as P

LANES = 128
EXTRA = 16
STEPS = 4
FINE = 16
F32 = jnp.float32
BF16 = jnp.bfloat16
HBM = pl.BlockSpec(memory_space=pltpu.HBM)
SMEM = pl.BlockSpec(memory_space=pltpu.SMEM)
PARAMS = pltpu.CompilerParams(vmem_limit_bytes=63 * 1024 * 1024)
DMA = pltpu.SemaphoreType.DMA


def cost(flops, nbytes):
    return pl.CostEstimate(flops=flops, bytes_accessed=nbytes, transcendentals=0)


def dot(a, b):
    return jnp.dot(a, b, preferred_element_type=F32)


def two(value):
    top = value.astype(BF16)
    return top, (value - top.astype(F32)).astype(BF16)


def fold(value):
    rows, cols = value.shape
    total = value[:, :LANES]
    for j in range(1, cols // LANES):
        total = total + value[:, j * LANES : (j + 1) * LANES]
    return total.reshape(rows // 8, 8, LANES).sum(axis=0)


def everywhere(value):
    return jnp.sum(value, axis=(0, 1), keepdims=True)


def invert(slots_ref, inverse_ref):
    for owner in range(slots_ref.shape[1]):
        inverse_ref[slots_ref[0, owner]] = owner


def own_band(slots_ref, columns):
    return lax.div(slots_ref[0, lax.axis_index("fsdp")], columns)


def pack(slots, q_values, scales, sums_of, width, start, part):
    owners = slots.shape[1]
    rows, cols = q_values.shape
    columns = cols // width
    groups = width // LANES
    here = part // LANES
    tall = here * rows + EXTRA
    sums = EXTRA - groups

    def body(slots_hbm, q_hbm, s_hbm, *rest):
        e_hbm = rest[: len(sums_of)]
        out_hbm, slots_ref, inverse, q_ref, s_ref, e_ref, turned, out_ref, ins, outs = rest[-10:]

        def q_read(k):
            at = pl.ds(pl.multiple_of(k * width + start, LANES), part)
            return pltpu.make_async_copy(q_hbm.at[:, at], q_ref.at[k], ins.at[k])

        def write(k, band):
            at = band * columns + k
            return pltpu.make_async_copy(out_ref.at[k], out_hbm.at[inverse[at]], outs.at[at])

        reads = [
            pltpu.make_async_copy(slots_hbm, slots_ref, ins.at[columns]),
            pltpu.make_async_copy(s_hbm, s_ref, ins.at[columns + 1]),
        ]
        for k, src in enumerate(e_hbm):
            reads.append(pltpu.make_async_copy(src, e_ref.at[k], ins.at[columns + 2 + k]))
        for read in reads:
            read.start()

        @pl.loop(0, columns)
        def _(k):
            q_read(k).start()

        for read in reads:
            read.wait()
        invert(slots_ref, inverse)
        padded = jnp.concatenate([s_ref[...].astype(F32), jnp.zeros((LANES - rows, LANES), F32)], axis=0)
        turned[...] = padded.T
        head = jnp.zeros((sums, LANES), F32)
        if e_hbm:
            value = e_ref[0]
            for k in range(1, len(e_hbm)):
                value = value + e_ref[k]
            high = value.astype(BF16)
            mid, low = two(value - high.astype(F32))
            row = lax.broadcasted_iota(jnp.int32, head.shape, 0)
            for k, term in enumerate((high, mid, low)):
                head = jnp.where(row == k, jnp.broadcast_to(term[:1].astype(F32), head.shape), head)

        @pl.loop(0, columns)
        def _(k):
            scale = turned[pl.ds(pl.multiple_of(k * groups, groups), groups), :]
            out_ref[k, here * rows :, :] = jnp.concatenate([head, scale], axis=0).astype(BF16)
            q_read(k).wait()
            for j in range(here):
                out_ref[k, j * rows : (j + 1) * rows, :] = q_ref[k, :, j * LANES : (j + 1) * LANES]
            for band in range(owners // columns):
                write(k, band).start()

        @pl.loop(0, columns)
        def _(k):
            for band in range(owners // columns):
                write(k, band).wait()

    operands = [slots, q_values, scales, *sums_of]
    return pl.pallas_call(
        body,
        out_shape=jax.ShapeDtypeStruct((owners, tall, LANES), BF16),
        in_specs=[HBM] * len(operands),
        out_specs=HBM,
        scratch_shapes=[
            pltpu.SMEM(slots.shape, jnp.int32),
            pltpu.SMEM((owners,), jnp.int32),
            pltpu.VMEM((columns, rows, part), BF16),
            pltpu.VMEM(scales.shape, BF16),
            pltpu.VMEM((max(len(sums_of), 1), 8, LANES), F32),
            pltpu.VMEM((LANES, LANES), F32),
            pltpu.VMEM((columns, tall, LANES), BF16),
            DMA((columns + 2 + len(sums_of),)),
            DMA((owners,)),
        ],
        compiler_params=PARAMS,
        cost_estimate=cost(0, 2 * rows * cols + 2 * owners * tall * LANES),
        name=f"pack_{start}",
    )(*operands)


def square_sum(q_values, scales):
    rows, cols = q_values.shape
    groups = scales.shape[1]
    group = cols // groups

    def body(q_hbm, s_hbm, out_ref, q_ref, s_ref, sems):
        reads = [pltpu.make_async_copy(q_hbm, q_ref, sems.at[0]), pltpu.make_async_copy(s_hbm, s_ref, sems.at[1])]
        for read in reads:
            read.start()
        for read in reads:
            read.wait()
        total = jnp.zeros((rows, group), F32)
        for j in range(groups):
            grad = q_ref[:, j * group : (j + 1) * group].astype(F32) * s_ref[:, j : j + 1].astype(F32)
            total = total + grad * grad
        out_ref[...] = jnp.full((8, LANES), jnp.sum(total))

    return pl.pallas_call(
        body,
        out_shape=jax.ShapeDtypeStruct((8, LANES), F32),
        in_specs=[HBM] * 2,
        scratch_shapes=[pltpu.VMEM((rows, cols), BF16), pltpu.VMEM(scales.shape, BF16), DMA((2,))],
        compiler_params=PARAMS,
        cost_estimate=cost(3 * rows * cols, 2 * rows * cols),
        name="square_sum",
    )(q_values, scales)


def split_roots(left, right):
    size = left.shape[0]
    rows = size // STEPS

    def body(l_hbm, r_hbm, l1_hbm, l2_hbm, r1_hbm, r2_hbm, full, top, low, ins, outs):
        jobs = []
        for src, high_hbm, low_hbm in ((l_hbm, l1_hbm, l2_hbm), (r_hbm, r1_hbm, r2_hbm)):
            for n in range(STEPS):
                at = pl.ds(n * rows, rows)
                jobs.append((src.at[at], high_hbm.at[at], low_hbm.at[at]))
        reads = [pltpu.make_async_copy(job[0], full.at[k], ins.at[k]) for k, job in enumerate(jobs)]
        for read in reads:
            read.start()
        writes = []
        for k, (_, high_to, low_to) in enumerate(jobs):
            reads[k].wait()
            top[k], low[k] = two(full[k])
            for h, (src, to) in enumerate(((top.at[k], high_to), (low.at[k], low_to))):
                write = pltpu.make_async_copy(src, to, outs.at[2 * k + h])
                write.start()
                writes.append(write)
        for write in writes:
            write.wait()

    jobs = 2 * STEPS
    return pl.pallas_call(
        body,
        out_shape=[jax.ShapeDtypeStruct((size, size), BF16)] * 4,
        in_specs=[HBM] * 2,
        out_specs=[HBM] * 4,
        scratch_shapes=[
            pltpu.VMEM((jobs, rows, size), F32),
            pltpu.VMEM((jobs, rows, size), BF16),
            pltpu.VMEM((jobs, rows, size), BF16),
            DMA((jobs,)),
            DMA((2 * jobs,)),
        ],
        compiler_params=PARAMS,
        cost_estimate=cost(4 * size * size, 16 * size * size),
        name="split_roots",
    )(left, right)


def dequant(a_ref, turned, rows, group, at_lane, grad_ref, h1, h2):
    pieces, tall, _ = a_ref.shape
    here = (tall - EXTRA) // rows
    scales = a_ref[:, here * rows :, :].astype(F32).reshape(pieces * EXTRA, LANES)
    turned[...] = scales.T
    for piece in range(pieces):
        at = slice(piece * rows, (piece + 1) * rows)
        for j in range(here):
            column = piece * EXTRA + EXTRA - 8 + group + j
            grad = a_ref[piece, j * rows : (j + 1) * rows, :].astype(F32) * turned[:rows, column : column + 1]
            grad_ref[at, at_lane + j * LANES : at_lane + (j + 1) * LANES] = grad
            lanes = slice(j * LANES, (j + 1) * LANES)
            h1[at, lanes], h2[at, lanes] = two(grad)


def products(slots, arrived, l1, l2, r1, r2, rows, columns):
    size = l1.shape[0]
    _, tall, _ = arrived.shape
    pieces = size // rows
    part = tall // rows * LANES
    block = size // STEPS

    def body(
        slots_ref, a_hbm, l1_hbm, l2_hbm, r1_hbm, r2_hbm, p_hbm, grad_hbm,
        a_ref, l1_ref, l2_ref, r_ref, grad_ref, h1, h2, t_ref, p_ref, turned, ins, outs,
    ):
        band = own_band(slots_ref, columns)
        deep = pl.ds(0, part)
        pairs = (
            (a_hbm.at[pl.ds(band * pieces, pieces)], a_ref),
            (l1_hbm, l1_ref),
            (l2_hbm, l2_ref),
            *((src.at[deep], r_ref.at[pl.ds(k * part, part)]) for k, src in enumerate((r1_hbm, r2_hbm, r1_hbm))),
        )
        reads = [pltpu.make_async_copy(s, t, ins.at[k]) for k, (s, t) in enumerate(pairs)]
        for read in reads[:3]:
            read.start()
        reads[0].wait()
        for read in reads[3:]:
            read.start()
        dequant(a_ref, turned, rows, 0, 0, grad_ref, h1, h2)
        for read in reads[1:3]:
            read.wait()
        keep = pltpu.make_async_copy(grad_ref, grad_hbm, outs.at[STEPS])
        keep.start()

        @pl.loop(0, part // block)
        def _(n):
            at = pl.ds(pl.multiple_of(n * block, block), block)
            half = dot(l1_ref[...], h1[:, at]) + (dot(l1_ref[...], h2[:, at]) + dot(l2_ref[...], h1[:, at]))
            high, low = two(half)
            for k, term in enumerate((high, high, low)):
                t_ref[:, pl.ds(pl.multiple_of(k * part + n * block, block), block)] = term

        for read in reads[3:]:
            read.wait()

        def p_copy(n):
            at = pl.ds(pl.multiple_of(n * block, block), block)
            return pltpu.make_async_copy(p_ref.at[:, at], p_hbm.at[:, at], outs.at[n])

        @pl.loop(0, STEPS)
        def _(n):
            at = pl.ds(pl.multiple_of(n * block, block), block)
            p_ref[:, at] = dot(t_ref[...], r_ref[:, at])
            p_copy(n).start()

        for n in range(STEPS):
            p_copy(n).wait()
        keep.wait()

    square = (size, size)
    narrow = (size, part)
    return pl.pallas_call(
        body,
        out_shape=[jax.ShapeDtypeStruct(square, F32), jax.ShapeDtypeStruct(narrow, F32)],
        in_specs=[SMEM] + [HBM] * 5,
        out_specs=[HBM] * 2,
        scratch_shapes=[pltpu.VMEM((pieces, tall, LANES), BF16)]
        + [pltpu.VMEM(square, BF16)] * 2
        + [pltpu.VMEM((3 * part, size), BF16), pltpu.VMEM(narrow, F32)]
        + [pltpu.VMEM(narrow, BF16)] * 2
        + [pltpu.VMEM((size, 3 * part), BF16), pltpu.VMEM(square, F32)]
        + [pltpu.VMEM((LANES, pieces * EXTRA), F32), DMA((6,)), DMA((STEPS + 1,))],
        compiler_params=PARAMS,
        cost_estimate=cost(12 * size * size * part, 20 * size * size),
        name="products",
    )(slots, arrived, l1, l2, r1, r2)


def graft(slots, arrived, l1, l2, r1, r2, earlier, grad, moment, rows, columns, entries):
    size = moment.shape[0]
    owners, tall, _ = arrived.shape
    pieces = size // rows
    block = size // STEPS
    done = grad.shape[1]
    part = size - done
    thin = size // FINE

    def body(
        slots_ref, a_hbm, l1_hbm, l2_hbm, r1_hbm, r2_hbm, p_hbm, grad_hbm, m_hbm, out_hbm, fresh_hbm,
        sums_ref, a_ref, l1_ref, l2_ref, r_ref, p_ref, grad_ref, h1, h2, t_ref, m_ref, out_ref,
        turned, asum, psum, ins, outs,
    ):
        band = own_band(slots_ref, columns)
        deep = pl.ds(done, part)

        def cut(n):
            return pl.ds(pl.multiple_of(n * block, block), block)

        pairs = (
            (a_hbm.at[pl.ds(band * pieces, pieces)], a_ref),
            (a_hbm.at[:, pl.ds(tall - EXTRA, EXTRA)], sums_ref),
            (l1_hbm, l1_ref),
            (l2_hbm, l2_ref),
            *((src.at[deep], r_ref.at[pl.ds(k * part, part)]) for k, src in enumerate((r1_hbm, r2_hbm, r1_hbm))),
        )
        reads = [pltpu.make_async_copy(s, t, ins.at[3, k]) for k, (s, t) in enumerate(pairs)]

        def step_reads(n):
            at = cut(n)
            pairs = (
                (p_hbm.at[:, at], p_ref.at[:, at]),
                (grad_hbm.at[at], grad_ref.at[at, pl.ds(0, done)]),
                (m_hbm.at[at], m_ref.at[at]),
            )
            return [pltpu.make_async_copy(s, t, ins.at[k, n]) for k, (s, t) in enumerate(pairs)]

        for read in reads[:4]:
            read.start()
        for read in reads[:2]:
            read.wait()
        for read in reads[4:]:
            read.start()

        @pl.loop(0, STEPS)
        def _(n):
            for read in step_reads(n):
                read.start()

        dequant(a_ref, turned, rows, done // LANES, done, grad_ref, h1, h2)
        heads = jnp.sum(sums_ref[...].astype(F32), axis=0)[: EXTRA - 8]
        total = jnp.sum(heads, axis=0, keepdims=True)[:, :1]
        bound = 0.5 * jnp.sqrt(jnp.full((1, 1), entries, F32)) / jnp.sqrt(jnp.where(total > 0, total, 1.0))
        clip = jnp.where(total > 0, jnp.minimum(bound, 1.0), 1.0)
        asum[...] = jnp.zeros_like(asum)
        psum[...] = jnp.zeros_like(psum)
        for read in reads[2:4]:
            read.wait()
        half = dot(l1_ref[...], h1[...]) + (dot(l1_ref[...], h2[...]) + dot(l2_ref[...], h1[...]))
        high, low = two(half)
        for k, term in enumerate((high, high, low)):
            t_ref[:, k * part : (k + 1) * part] = term
        for read in reads[4:]:
            read.wait()

        def fresh_copy(n):
            return pltpu.make_async_copy(m_ref.at[cut(n)], fresh_hbm.at[cut(n)], outs.at[0, n])

        def out_copy(n):
            to = pl.ds(pl.multiple_of(band * size + n * block, block), block)
            return pltpu.make_async_copy(out_ref.at[cut(n)], out_hbm.at[to], outs.at[1, n])

        @pl.loop(0, STEPS)
        def _(n):
            for read in step_reads(n):
                read.wait()
            at = cut(n)
            product = p_ref[:, at] + dot(t_ref[...], r_ref[:, at])
            p_ref[:, at] = product
            psum[...] += fold(product * product)

            steps = []
            for k in range(block // thin):
                line = pl.ds(pl.multiple_of(n * block + k * thin, thin), thin)
                held = grad_ref[line, :] * clip
                square = held * held
                fresh = 0.9 * m_ref[line, :] + 0.1 * square
                m_ref[line, :] = fresh
                root = fresh * lax.rsqrt(fresh) + 1e-08
                inverse = pl.reciprocal(root, approx=True)
                adam = held * (inverse * (2.0 - root * inverse))
                steps.append(fold(adam * adam))
            asum[...] += sum(steps)
            fresh_copy(n).start()

        norm = jnp.sqrt(everywhere(psum[...]) * (clip * clip) + 1e-12)
        ratio = clip * (jnp.sqrt(everywhere(asum[...])) / norm)

        @pl.loop(0, STEPS)
        def _(n):
            out_ref[cut(n), :] = (p_ref[cut(n), :] * ratio).astype(BF16)
            out_copy(n).start()

        for n in range(STEPS):
            fresh_copy(n).wait()
            out_copy(n).wait()

    square = (size, size)
    return pl.pallas_call(
        body,
        out_shape=[
            jax.ShapeDtypeStruct((owners * rows, size), BF16),
            jax.ShapeDtypeStruct(square, F32),
        ],
        in_specs=[SMEM] + [HBM] * 8,
        out_specs=[HBM, HBM],
        scratch_shapes=[pltpu.VMEM((owners, EXTRA, LANES), BF16), pltpu.VMEM((pieces, tall, LANES), BF16)]
        + [pltpu.VMEM(square, BF16)] * 2
        + [pltpu.VMEM((3 * part, size), BF16)]
        + [pltpu.VMEM(square, F32)] * 2
        + [pltpu.VMEM((size, part), BF16)] * 2
        + [pltpu.VMEM((size, 3 * part), BF16)]
        + [
            pltpu.VMEM(square, F32),
            pltpu.VMEM(square, BF16),
            pltpu.VMEM((LANES, pieces * EXTRA), F32),
            pltpu.VMEM((8, LANES), F32),
            pltpu.VMEM((8, LANES), F32),
            DMA((4, 7)),
            DMA((2, STEPS)),
        ],
        compiler_params=PARAMS,
        cost_estimate=cost(12 * size * size * part, 24 * size * size),
        name="graft",
    )(slots, arrived, l1, l2, r1, r2, earlier, grad, moment)


def place(slots, returned, cols):
    owners, rows, width = returned.shape
    columns = cols // width

    def body(slots_ref, r_ref, out_hbm, inverse, outs):
        first = lax.div(lax.axis_index("fsdp") * rows, width) * columns
        invert(slots_ref, inverse)

        def write(k):
            here = pl.ds(pl.multiple_of(k * width, width), width)
            return pltpu.make_async_copy(r_ref.at[inverse[first + k]], out_hbm.at[:, here], outs.at[k])

        @pl.loop(0, columns)
        def _(k):
            write(k).start()

        @pl.loop(0, columns)
        def _(k):
            write(k).wait()

    return pl.pallas_call(
        body,
        out_shape=jax.ShapeDtypeStruct((rows, cols), BF16),
        in_specs=[SMEM, pl.BlockSpec(memory_space=pltpu.VMEM)],
        out_specs=HBM,
        scratch_shapes=[pltpu.SMEM((owners,), jnp.int32), DMA((columns,))],
        compiler_params=pltpu.CompilerParams(vmem_limit_bytes=12 * 1024 * 1024),
        cost_estimate=cost(0, 4 * rows * cols),
        name="place",
    )(slots, returned)


def on_device(q_values, scales, block_slots, left_root, right_root, second_moment):
    count = lax.axis_size("fsdp")
    planes = lax.axis_size("grp")
    rows, cols = q_values.shape
    width = left_root.shape[-1]
    columns = cols // width
    first = width * 3 // 4

    def exchange(value):
        return lax.all_to_all(value, "fsdp", split_axis=0, concat_axis=0, tiled=True)

    arrived = exchange(pack(block_slots, q_values, scales, [], width, 0, first))
    own = square_sum(q_values, scales)
    sums = [own]
    for k in range(1, planes):
        sums.append(lax.ppermute(own, "grp", [(i, (i + k) % planes) for i in range(planes)]))
    *sums, l1, l2, r1, r2 = lax.optimization_barrier((*sums, *split_roots(left_root[0, 0], right_root[0, 0])))
    roots = (l1, l2, r1, r2)
    later = exchange(pack(block_slots, q_values, scales, sums, width, first, width - first))

    product, grad = products(block_slots, arrived, *roots, rows, columns)
    outgoing, fresh = graft(
        block_slots, later, *roots, product, grad, second_moment[0, 0], rows, columns, rows * count * cols * planes
    )
    update = place(block_slots, exchange(outgoing.reshape(count, rows, width)), cols)
    return (update, fresh[None, None])


def solution(mesh):
    in_specs = (
        P("fsdp", "grp"),
        P("fsdp", "grp"),
        P("grp", None),
        P("grp", "fsdp", None, None),
        P("grp", "fsdp", None, None),
        P("grp", "fsdp", None, None),
    )
    out_specs = (P("fsdp", "grp"), P("grp", "fsdp", None, None))
    return jax.shard_map(
        on_device, mesh=mesh, in_specs=in_specs, out_specs=out_specs, check_vma=False
    )
```

```python
import jax
import jax.numpy as jnp
from jax import lax
from jax.experimental import pallas as pl
from jax.experimental.pallas import tpu as pltpu
from jax.sharding import PartitionSpec as P

LANES = 128
EXTRA = 16
STEPS = 4
FINE = 16
F32 = jnp.float32
BF16 = jnp.bfloat16
HBM = pl.BlockSpec(memory_space=pltpu.HBM)
SMEM = pl.BlockSpec(memory_space=pltpu.SMEM)
PARAMS = pltpu.CompilerParams(vmem_limit_bytes=63 * 1024 * 1024)
DMA = pltpu.SemaphoreType.DMA


def cost(flops, nbytes):
    return pl.CostEstimate(flops=flops, bytes_accessed=nbytes, transcendentals=0)


def dot(a, b):
    return jnp.dot(a, b, preferred_element_type=F32)


def two(value):
    top = value.astype(BF16)
    return top, (value - top.astype(F32)).astype(BF16)


def fold(value):
    rows, cols = value.shape
    total = value[:, :LANES]
    for j in range(1, cols // LANES):
        total = total + value[:, j * LANES : (j + 1) * LANES]
    return total.reshape(rows // 8, 8, LANES).sum(axis=0)


def everywhere(value):
    return jnp.sum(value, axis=(0, 1), keepdims=True)


def invert(slots_ref, inverse_ref):
    for owner in range(slots_ref.shape[1]):
        inverse_ref[slots_ref[0, owner]] = owner


def own_band(slots_ref, columns):
    return lax.div(slots_ref[0, lax.axis_index("fsdp")], columns)


def pack(slots, q_values, scales, sums_of, width, start, part):
    owners = slots.shape[1]
    rows, cols = q_values.shape
    columns = cols // width
    groups = width // LANES
    here = part // LANES
    tall = here * rows + EXTRA
    sums = EXTRA - groups

    def body(slots_hbm, q_hbm, s_hbm, *rest):
        e_hbm = rest[: len(sums_of)]
        out_hbm, slots_ref, inverse, q_ref, s_ref, e_ref, turned, out_ref, ins, outs = rest[-10:]

        def q_read(k):
            at = pl.ds(pl.multiple_of(k * width + start, LANES), part)
            return pltpu.make_async_copy(q_hbm.at[:, at], q_ref.at[k], ins.at[k])

        def write(k, band):
            at = band * columns + k
            return pltpu.make_async_copy(out_ref.at[k], out_hbm.at[inverse[at]], outs.at[at])

        reads = [
            pltpu.make_async_copy(slots_hbm, slots_ref, ins.at[columns]),
            pltpu.make_async_copy(s_hbm, s_ref, ins.at[columns + 1]),
        ]
        for k, src in enumerate(e_hbm):
            reads.append(pltpu.make_async_copy(src, e_ref.at[k], ins.at[columns + 2 + k]))
        for read in reads:
            read.start()

        @pl.loop(0, columns)
        def _(k):
            q_read(k).start()

        for read in reads:
            read.wait()
        invert(slots_ref, inverse)
        padded = jnp.concatenate([s_ref[...].astype(F32), jnp.zeros((LANES - rows, LANES), F32)], axis=0)
        turned[...] = padded.T
        head = jnp.zeros((sums, LANES), F32)
        if e_hbm:
            value = e_ref[0]
            for k in range(1, len(e_hbm)):
                value = value + e_ref[k]
            high = value.astype(BF16)
            mid, low = two(value - high.astype(F32))
            row = lax.broadcasted_iota(jnp.int32, head.shape, 0)
            for k, term in enumerate((high, mid, low)):
                head = jnp.where(row == k, jnp.broadcast_to(term[:1].astype(F32), head.shape), head)

        @pl.loop(0, columns)
        def _(k):
            scale = turned[pl.ds(pl.multiple_of(k * groups, groups), groups), :]
            out_ref[k, here * rows :, :] = jnp.concatenate([head, scale], axis=0).astype(BF16)
            q_read(k).wait()
            for j in range(here):
                out_ref[k, j * rows : (j + 1) * rows, :] = q_ref[k, :, j * LANES : (j + 1) * LANES]
            for band in range(owners // columns):
                write(k, band).start()

        @pl.loop(0, columns)
        def _(k):
            for band in range(owners // columns):
                write(k, band).wait()

    operands = [slots, q_values, scales, *sums_of]
    return pl.pallas_call(
        body,
        out_shape=jax.ShapeDtypeStruct((owners, tall, LANES), BF16),
        in_specs=[HBM] * len(operands),
        out_specs=HBM,
        scratch_shapes=[
            pltpu.SMEM(slots.shape, jnp.int32),
            pltpu.SMEM((owners,), jnp.int32),
            pltpu.VMEM((columns, rows, part), BF16),
            pltpu.VMEM(scales.shape, BF16),
            pltpu.VMEM((max(len(sums_of), 1), 8, LANES), F32),
            pltpu.VMEM((LANES, LANES), F32),
            pltpu.VMEM((columns, tall, LANES), BF16),
            DMA((columns + 2 + len(sums_of),)),
            DMA((owners,)),
        ],
        compiler_params=PARAMS,
        cost_estimate=cost(0, 2 * rows * cols + 2 * owners * tall * LANES),
        name=f"pack_{start}",
    )(*operands)


def square_sum(q_values, scales):
    rows, cols = q_values.shape
    groups = scales.shape[1]
    group = cols // groups

    def body(q_hbm, s_hbm, out_ref, q_ref, s_ref, sems):
        reads = [pltpu.make_async_copy(q_hbm, q_ref, sems.at[0]), pltpu.make_async_copy(s_hbm, s_ref, sems.at[1])]
        for read in reads:
            read.start()
        for read in reads:
            read.wait()
        total = jnp.zeros((rows, group), F32)
        for j in range(groups):
            grad = q_ref[:, j * group : (j + 1) * group].astype(F32) * s_ref[:, j : j + 1].astype(F32)
            total = total + grad * grad
        out_ref[...] = jnp.full((8, LANES), jnp.sum(total))

    return pl.pallas_call(
        body,
        out_shape=jax.ShapeDtypeStruct((8, LANES), F32),
        in_specs=[HBM] * 2,
        scratch_shapes=[pltpu.VMEM((rows, cols), BF16), pltpu.VMEM(scales.shape, BF16), DMA((2,))],
        compiler_params=PARAMS,
        cost_estimate=cost(3 * rows * cols, 2 * rows * cols),
        name="square_sum",
    )(q_values, scales)


def split_roots(left, right):
    size = left.shape[0]
    rows = size // STEPS

    def body(l_hbm, r_hbm, l1_hbm, l2_hbm, r1_hbm, r2_hbm, full, top, low, ins, outs):
        jobs = []
        for src, high_hbm, low_hbm in ((l_hbm, l1_hbm, l2_hbm), (r_hbm, r1_hbm, r2_hbm)):
            for n in range(STEPS):
                at = pl.ds(n * rows, rows)
                jobs.append((src.at[at], high_hbm.at[at], low_hbm.at[at]))
        reads = [pltpu.make_async_copy(job[0], full.at[k], ins.at[k]) for k, job in enumerate(jobs)]
        for read in reads:
            read.start()
        writes = []
        for k, (_, high_to, low_to) in enumerate(jobs):
            reads[k].wait()
            top[k], low[k] = two(full[k])
            for h, (src, to) in enumerate(((top.at[k], high_to), (low.at[k], low_to))):
                write = pltpu.make_async_copy(src, to, outs.at[2 * k + h])
                write.start()
                writes.append(write)
        for write in writes:
            write.wait()

    jobs = 2 * STEPS
    return pl.pallas_call(
        body,
        out_shape=[jax.ShapeDtypeStruct((size, size), BF16)] * 4,
        in_specs=[HBM] * 2,
        out_specs=[HBM] * 4,
        scratch_shapes=[
            pltpu.VMEM((jobs, rows, size), F32),
            pltpu.VMEM((jobs, rows, size), BF16),
            pltpu.VMEM((jobs, rows, size), BF16),
            DMA((jobs,)),
            DMA((2 * jobs,)),
        ],
        compiler_params=PARAMS,
        cost_estimate=cost(4 * size * size, 16 * size * size),
        name="split_roots",
    )(left, right)


def dequant(a_ref, base, pieces, turned, rows, group, at_lane, grad_ref, h1, h2):
    tall = a_ref.shape[1]
    here = (tall - EXTRA) // rows
    scales = a_ref[pl.ds(base, pieces), here * rows :, :].astype(F32).reshape(pieces * EXTRA, LANES)
    turned[...] = scales.T
    for piece in range(pieces):
        at = slice(piece * rows, (piece + 1) * rows)
        for j in range(here):
            column = piece * EXTRA + EXTRA - 8 + group + j
            grad = a_ref[base + piece, j * rows : (j + 1) * rows, :].astype(F32) * turned[:rows, column : column + 1]
            grad_ref[at, at_lane + j * LANES : at_lane + (j + 1) * LANES] = grad
            lanes = slice(j * LANES, (j + 1) * LANES)
            h1[at, lanes], h2[at, lanes] = two(grad)


def products(slots, arrived, l1, l2, r1, r2, rows, columns):
    size = l1.shape[0]
    _, tall, _ = arrived.shape
    pieces = size // rows
    part = tall // rows * LANES
    block = size // STEPS

    def body(
        slots_ref, a_hbm, l1_hbm, l2_hbm, r1_hbm, r2_hbm, p_hbm, grad_hbm,
        a_ref, l1_ref, l2_ref, r1_ref, r2_ref, grad_ref, h1, h2, t1, t2, p_ref, turned, ins, outs,
    ):
        band = own_band(slots_ref, columns)
        deep = pl.ds(0, part)
        pairs = (
            (a_hbm.at[pl.ds(band * pieces, pieces)], a_ref),
            (l1_hbm, l1_ref),
            (l2_hbm, l2_ref),
            (r1_hbm.at[deep], r1_ref),
            (r2_hbm.at[deep], r2_ref),
        )
        reads = [pltpu.make_async_copy(s, t, ins.at[k]) for k, (s, t) in enumerate(pairs)]
        for read in reads[:3]:
            read.start()
        reads[0].wait()
        for read in reads[3:]:
            read.start()
        dequant(a_ref, 0, pieces, turned, rows, 0, 0, grad_ref, h1, h2)
        for read in reads[1:3]:
            read.wait()
        keep = pltpu.make_async_copy(grad_ref, grad_hbm, outs.at[STEPS])
        keep.start()

        @pl.loop(0, part // block)
        def _(n):
            at = pl.ds(pl.multiple_of(n * block, block), block)
            half = dot(l1_ref[...], h1[:, at]) + (dot(l1_ref[...], h2[:, at]) + dot(l2_ref[...], h1[:, at]))
            t1[:, at], t2[:, at] = two(half)

        for read in reads[3:]:
            read.wait()

        def p_copy(n):
            at = pl.ds(pl.multiple_of(n * block, block), block)
            return pltpu.make_async_copy(p_ref.at[:, at], p_hbm.at[:, at], outs.at[n])

        @pl.loop(0, STEPS)
        def _(n):
            at = pl.ds(pl.multiple_of(n * block, block), block)
            p_ref[:, at] = dot(t1[...], r1_ref[:, at]) + (dot(t1[...], r2_ref[:, at]) + dot(t2[...], r1_ref[:, at]))
            p_copy(n).start()

        for n in range(STEPS):
            p_copy(n).wait()
        keep.wait()

    square = (size, size)
    narrow = (size, part)
    return pl.pallas_call(
        body,
        out_shape=[jax.ShapeDtypeStruct(square, F32), jax.ShapeDtypeStruct(narrow, F32)],
        in_specs=[SMEM] + [HBM] * 5,
        out_specs=[HBM] * 2,
        scratch_shapes=[pltpu.VMEM((pieces, tall, LANES), BF16)]
        + [pltpu.VMEM(square, BF16)] * 2
        + [pltpu.VMEM((part, size), BF16)] * 2
        + [pltpu.VMEM(narrow, F32)]
        + [pltpu.VMEM(narrow, BF16)] * 4
        + [pltpu.VMEM(square, F32), pltpu.VMEM((LANES, pieces * EXTRA), F32), DMA((5,)), DMA((STEPS + 1,))],
        compiler_params=PARAMS,
        cost_estimate=cost(12 * size * size * part, 20 * size * size),
        name="products",
    )(slots, arrived, l1, l2, r1, r2)


def graft(slots, arrived, l1, l2, r1, r2, earlier, grad, moment, rows, columns, entries):
    size = moment.shape[0]
    owners, tall, _ = arrived.shape
    pieces = size // rows
    block = size // STEPS
    done = grad.shape[1]
    part = size - done
    thin = size // FINE

    def body(
        slots_hbm, a_hbm, l1_hbm, l2_hbm, r1_hbm, r2_hbm, p_hbm, grad_hbm, m_hbm, out_hbm, fresh_hbm,
        slots_ref, a_ref, l1_ref, l2_ref, r1_ref, r2_ref, p_ref, grad_ref, h1, h2, t1, t2, m_ref, out_ref,
        turned, asum, psum, ins, outs,
    ):
        deep = pl.ds(done, part)

        def cut(n):
            return pl.ds(pl.multiple_of(n * block, block), block)

        pairs = (
            (slots_hbm, slots_ref),
            (a_hbm, a_ref),
            (l1_hbm, l1_ref),
            (l2_hbm, l2_ref),
            (r1_hbm.at[deep], r1_ref),
            (r2_hbm.at[deep], r2_ref),
        )
        reads = [pltpu.make_async_copy(s, t, ins.at[3, k]) for k, (s, t) in enumerate(pairs)]

        def p_read(n):
            at = cut(n)
            return pltpu.make_async_copy(p_hbm.at[:, at], p_ref.at[:, at], ins.at[0, n])

        def adam_reads(n):
            at = cut(n)
            pairs = ((grad_hbm.at[at], grad_ref.at[at, pl.ds(0, done)]), (m_hbm.at[at], m_ref.at[at]))
            return [pltpu.make_async_copy(s, t, ins.at[1 + k, n]) for k, (s, t) in enumerate(pairs)]

        for read in reads[:4]:
            read.start()
        for read in reads[:2]:
            read.wait()
        band = own_band(slots_ref, columns)
        base = band * pieces

        for read in reads[4:] + adam_reads(0):
            read.start()

        @pl.loop(1, STEPS)
        def _(n):
            for read in [p_read(n), *adam_reads(n)]:
                read.start()

        p_read(0).start()
        dequant(a_ref, base, pieces, turned, rows, done // LANES, done, grad_ref, h1, h2)
        heads = jnp.sum(a_ref[:, tall - EXTRA :, :].astype(F32), axis=0)[: EXTRA - 8]
        total = jnp.sum(heads, axis=0, keepdims=True)[:, :1]
        bound = 0.5 * jnp.sqrt(jnp.full((1, 1), entries, F32)) / jnp.sqrt(jnp.where(total > 0, total, 1.0))
        clip = jnp.where(total > 0, jnp.minimum(bound, 1.0), 1.0)
        asum[...] = jnp.zeros_like(asum)
        psum[...] = jnp.zeros_like(psum)
        for read in reads[2:4]:
            read.wait()

        def fresh_copy(n):
            return pltpu.make_async_copy(m_ref.at[cut(n)], fresh_hbm.at[cut(n)], outs.at[0, n])

        def out_copy(n):
            to = pl.ds(pl.multiple_of(band * size + n * block, block), block)
            return pltpu.make_async_copy(out_ref.at[cut(n)], out_hbm.at[to], outs.at[1, n])

        def adam(n):
            for read in adam_reads(n):
                read.wait()
            steps = []
            for k in range(block // thin):
                line = pl.ds(pl.multiple_of(n * block + k * thin, thin), thin)
                held = grad_ref[line, :] * clip
                square = held * held
                fresh = 0.9 * m_ref[line, :] + 0.1 * square
                m_ref[line, :] = fresh
                root = fresh * lax.rsqrt(fresh) + 1e-08
                inverse = pl.reciprocal(root, approx=True)
                ratios = held * (inverse * (2.0 - root * inverse))
                steps.append(fold(ratios * ratios))
            asum[...] += sum(steps)
            fresh_copy(n).start()

        half = dot(l1_ref[...], h1[...])
        adam(0)
        half = half + (dot(l1_ref[...], h2[...]) + dot(l2_ref[...], h1[...]))
        t1[...], t2[...] = two(half)
        for read in reads[4:]:
            read.wait()

        def second(n):
            p_read(n).wait()
            at = cut(n)
            more = dot(t1[...], r1_ref[:, at]) + (dot(t1[...], r2_ref[:, at]) + dot(t2[...], r1_ref[:, at]))
            product = p_ref[:, at] + more
            p_ref[:, at] = product
            psum[...] += fold(product * product)

        @pl.loop(1, STEPS)
        def _(n):
            second(n)
            adam(n)

        second(0)
        norm = jnp.sqrt(everywhere(psum[...]) * (clip * clip) + 1e-12)
        ratio = clip * (jnp.sqrt(everywhere(asum[...])) / norm)

        @pl.loop(0, STEPS)
        def _(n):
            out_ref[cut(n), :] = (p_ref[cut(n), :] * ratio).astype(BF16)
            out_copy(n).start()

        for n in range(STEPS):
            fresh_copy(n).wait()
            out_copy(n).wait()

    square = (size, size)
    return pl.pallas_call(
        body,
        out_shape=[
            jax.ShapeDtypeStruct((owners * rows, size), BF16),
            jax.ShapeDtypeStruct(square, F32),
        ],
        in_specs=[HBM] * 9,
        out_specs=[HBM, HBM],
        scratch_shapes=[pltpu.SMEM(slots.shape, jnp.int32), pltpu.VMEM((owners, tall, LANES), BF16)]
        + [pltpu.VMEM(square, BF16)] * 2
        + [pltpu.VMEM((part, size), BF16)] * 2
        + [pltpu.VMEM(square, F32)] * 2
        + [pltpu.VMEM((size, part), BF16)] * 4
        + [
            pltpu.VMEM(square, F32),
            pltpu.VMEM(square, BF16),
            pltpu.VMEM((LANES, pieces * EXTRA), F32),
            pltpu.VMEM((8, LANES), F32),
            pltpu.VMEM((8, LANES), F32),
            DMA((4, 6)),
            DMA((2, STEPS)),
        ],
        compiler_params=PARAMS,
        cost_estimate=cost(12 * size * size * part, 24 * size * size),
        name="graft",
    )(slots, arrived, l1, l2, r1, r2, earlier, grad, moment)


def place(slots, returned, cols):
    owners, rows, width = returned.shape
    columns = cols // width

    def body(slots_ref, r_ref, out_hbm, inverse, outs):
        first = lax.div(lax.axis_index("fsdp") * rows, width) * columns
        invert(slots_ref, inverse)

        def write(k):
            here = pl.ds(pl.multiple_of(k * width, width), width)
            return pltpu.make_async_copy(r_ref.at[inverse[first + k]], out_hbm.at[:, here], outs.at[k])

        @pl.loop(0, columns)
        def _(k):
            write(k).start()

        @pl.loop(0, columns)
        def _(k):
            write(k).wait()

    return pl.pallas_call(
        body,
        out_shape=jax.ShapeDtypeStruct((rows, cols), BF16),
        in_specs=[SMEM, pl.BlockSpec(memory_space=pltpu.VMEM)],
        out_specs=HBM,
        scratch_shapes=[pltpu.SMEM((owners,), jnp.int32), DMA((columns,))],
        compiler_params=pltpu.CompilerParams(vmem_limit_bytes=12 * 1024 * 1024),
        cost_estimate=cost(0, 4 * rows * cols),
        name="place",
    )(slots, returned)


def on_device(q_values, scales, block_slots, left_root, right_root, second_moment):
    count = lax.axis_size("fsdp")
    planes = lax.axis_size("grp")
    rows, cols = q_values.shape
    width = left_root.shape[-1]
    columns = cols // width
    first = width * 3 // 4

    def exchange(value):
        return lax.all_to_all(value, "fsdp", split_axis=0, concat_axis=0, tiled=True)

    arrived = exchange(pack(block_slots, q_values, scales, [], width, 0, first))
    own = square_sum(q_values, scales)
    sums = [own]
    for k in range(1, planes):
        sums.append(lax.ppermute(own, "grp", [(i, (i + k) % planes) for i in range(planes)]))
    *sums, l1, l2, r1, r2 = lax.optimization_barrier((*sums, *split_roots(left_root[0, 0], right_root[0, 0])))
    roots = (l1, l2, r1, r2)
    later = exchange(pack(block_slots, q_values, scales, sums, width, first, width - first))

    product, grad = products(block_slots, arrived, *roots, rows, columns)
    outgoing, fresh = graft(
        block_slots, later, *roots, product, grad, second_moment[0, 0], rows, columns, rows * count * cols * planes
    )
    update = place(block_slots, exchange(outgoing.reshape(count, rows, width)), cols)
    return (update, fresh[None, None])


def solution(mesh):
    in_specs = (
        P("fsdp", "grp"),
        P("fsdp", "grp"),
        P("grp", None),
        P("grp", "fsdp", None, None),
        P("grp", "fsdp", None, None),
        P("grp", "fsdp", None, None),
    )
    out_specs = (P("fsdp", "grp"), P("grp", "fsdp", None, None))
    return jax.shard_map(
        on_device, mesh=mesh, in_specs=in_specs, out_specs=out_specs, check_vma=False
    )
```

```python
import jax
import jax.numpy as jnp
from jax import lax
from jax.experimental import pallas as pl
from jax.experimental.pallas import tpu as pltpu
from jax.sharding import PartitionSpec as P

LANES = 128
EXTRA = 16
STEPS = 4
FINE = 16
F32 = jnp.float32
BF16 = jnp.bfloat16
HBM = pl.BlockSpec(memory_space=pltpu.HBM)
SMEM = pl.BlockSpec(memory_space=pltpu.SMEM)
PARAMS = pltpu.CompilerParams(vmem_limit_bytes=63 * 1024 * 1024)
DMA = pltpu.SemaphoreType.DMA


def cost(flops, nbytes):
    return pl.CostEstimate(flops=flops, bytes_accessed=nbytes, transcendentals=0)


def dot(a, b):
    return jnp.dot(a, b, preferred_element_type=F32)


def two(value):
    top = value.astype(BF16)
    return top, (value - top.astype(F32)).astype(BF16)


def fold(value):
    rows, cols = value.shape
    total = value[:, :LANES]
    for j in range(1, cols // LANES):
        total = total + value[:, j * LANES : (j + 1) * LANES]
    return total.reshape(rows // 8, 8, LANES).sum(axis=0)


def everywhere(value):
    return jnp.sum(value, axis=(0, 1), keepdims=True)


def invert(slots_ref, inverse_ref):
    for owner in range(slots_ref.shape[1]):
        inverse_ref[slots_ref[0, owner]] = owner


def own_band(slots_ref, columns):
    return lax.div(slots_ref[0, lax.axis_index("fsdp")], columns)


def pack(slots, q_values, scales, sums_of, width, start, part):
    owners = slots.shape[1]
    rows, cols = q_values.shape
    columns = cols // width
    groups = width // LANES
    here = part // LANES
    tall = here * rows + EXTRA
    sums = EXTRA - groups

    def body(slots_hbm, q_hbm, s_hbm, *rest):
        e_hbm = rest[: len(sums_of)]
        out_hbm, slots_ref, inverse, q_ref, s_ref, e_ref, turned, out_ref, ins, outs = rest[-10:]

        def q_read(k):
            at = pl.ds(pl.multiple_of(k * width + start, LANES), part)
            return pltpu.make_async_copy(q_hbm.at[:, at], q_ref.at[k], ins.at[k])

        def write(k, band):
            at = band * columns + k
            return pltpu.make_async_copy(out_ref.at[k], out_hbm.at[inverse[at]], outs.at[at])

        reads = [
            pltpu.make_async_copy(slots_hbm, slots_ref, ins.at[columns]),
            pltpu.make_async_copy(s_hbm, s_ref, ins.at[columns + 1]),
        ]
        for k, src in enumerate(e_hbm):
            reads.append(pltpu.make_async_copy(src, e_ref.at[k], ins.at[columns + 2 + k]))
        for read in reads:
            read.start()

        @pl.loop(0, columns)
        def _(k):
            q_read(k).start()

        for read in reads:
            read.wait()
        invert(slots_ref, inverse)
        padded = jnp.concatenate([s_ref[...].astype(F32), jnp.zeros((LANES - rows, LANES), F32)], axis=0)
        turned[...] = padded.T
        head = jnp.zeros((sums, LANES), F32)
        if e_hbm:
            value = e_ref[0]
            for k in range(1, len(e_hbm)):
                value = value + e_ref[k]
            high = value.astype(BF16)
            mid, low = two(value - high.astype(F32))
            row = lax.broadcasted_iota(jnp.int32, head.shape, 0)
            for k, term in enumerate((high, mid, low)):
                head = jnp.where(row == k, jnp.broadcast_to(term[:1].astype(F32), head.shape), head)

        @pl.loop(0, columns)
        def _(k):
            scale = turned[pl.ds(pl.multiple_of(k * groups, groups), groups), :]
            out_ref[k, here * rows :, :] = jnp.concatenate([head, scale], axis=0).astype(BF16)
            q_read(k).wait()
            for j in range(here):
                out_ref[k, j * rows : (j + 1) * rows, :] = q_ref[k, :, j * LANES : (j + 1) * LANES]
            for band in range(owners // columns):
                write(k, band).start()

        @pl.loop(0, columns)
        def _(k):
            for band in range(owners // columns):
                write(k, band).wait()

    operands = [slots, q_values, scales, *sums_of]
    return pl.pallas_call(
        body,
        out_shape=jax.ShapeDtypeStruct((owners, tall, LANES), BF16),
        in_specs=[HBM] * len(operands),
        out_specs=HBM,
        scratch_shapes=[
            pltpu.SMEM(slots.shape, jnp.int32),
            pltpu.SMEM((owners,), jnp.int32),
            pltpu.VMEM((columns, rows, part), BF16),
            pltpu.VMEM(scales.shape, BF16),
            pltpu.VMEM((max(len(sums_of), 1), 8, LANES), F32),
            pltpu.VMEM((LANES, LANES), F32),
            pltpu.VMEM((columns, tall, LANES), BF16),
            DMA((columns + 2 + len(sums_of),)),
            DMA((owners,)),
        ],
        compiler_params=PARAMS,
        cost_estimate=cost(0, 2 * rows * cols + 2 * owners * tall * LANES),
        name=f"pack_{start}",
    )(*operands)


def square_sum(q_values, scales):
    rows, cols = q_values.shape
    groups = scales.shape[1]
    group = cols // groups

    def body(q_hbm, s_hbm, out_ref, q_ref, s_ref, sems):
        reads = [pltpu.make_async_copy(q_hbm, q_ref, sems.at[0]), pltpu.make_async_copy(s_hbm, s_ref, sems.at[1])]
        for read in reads:
            read.start()
        for read in reads:
            read.wait()
        total = jnp.zeros((rows, group), F32)
        for j in range(groups):
            grad = q_ref[:, j * group : (j + 1) * group].astype(F32) * s_ref[:, j : j + 1].astype(F32)
            total = total + grad * grad
        out_ref[...] = jnp.full((8, LANES), jnp.sum(total))

    return pl.pallas_call(
        body,
        out_shape=jax.ShapeDtypeStruct((8, LANES), F32),
        in_specs=[HBM] * 2,
        scratch_shapes=[pltpu.VMEM((rows, cols), BF16), pltpu.VMEM(scales.shape, BF16), DMA((2,))],
        compiler_params=PARAMS,
        cost_estimate=cost(3 * rows * cols, 2 * rows * cols),
        name="square_sum",
    )(q_values, scales)


def split_roots(left, right):
    size = left.shape[0]
    rows = size // STEPS

    def body(l_hbm, r_hbm, l1_hbm, l2_hbm, r1_hbm, r2_hbm, full, top, low, ins, outs):
        jobs = []
        for src, high_hbm, low_hbm in ((l_hbm, l1_hbm, l2_hbm), (r_hbm, r1_hbm, r2_hbm)):
            for n in range(STEPS):
                at = pl.ds(n * rows, rows)
                jobs.append((src.at[at], high_hbm.at[at], low_hbm.at[at]))
        reads = [pltpu.make_async_copy(job[0], full.at[k], ins.at[k]) for k, job in enumerate(jobs)]
        for read in reads:
            read.start()
        writes = []
        for k, (_, high_to, low_to) in enumerate(jobs):
            reads[k].wait()
            top[k], low[k] = two(full[k])
            for h, (src, to) in enumerate(((top.at[k], high_to), (low.at[k], low_to))):
                write = pltpu.make_async_copy(src, to, outs.at[2 * k + h])
                write.start()
                writes.append(write)
        for write in writes:
            write.wait()

    jobs = 2 * STEPS
    return pl.pallas_call(
        body,
        out_shape=[jax.ShapeDtypeStruct((size, size), BF16)] * 4,
        in_specs=[HBM] * 2,
        out_specs=[HBM] * 4,
        scratch_shapes=[
            pltpu.VMEM((jobs, rows, size), F32),
            pltpu.VMEM((jobs, rows, size), BF16),
            pltpu.VMEM((jobs, rows, size), BF16),
            DMA((jobs,)),
            DMA((2 * jobs,)),
        ],
        compiler_params=PARAMS,
        cost_estimate=cost(4 * size * size, 16 * size * size),
        name="split_roots",
    )(left, right)


def dequant(a_ref, base, pieces, turned, rows, group, at_lane, grad_ref, h1, h2):
    tall = a_ref.shape[1]
    here = (tall - EXTRA) // rows
    scales = a_ref[pl.ds(base, pieces), here * rows :, :].astype(F32).reshape(pieces * EXTRA, LANES)
    turned[...] = scales.T
    for piece in range(pieces):
        at = slice(piece * rows, (piece + 1) * rows)
        for j in range(here):
            column = piece * EXTRA + EXTRA - 8 + group + j
            grad = a_ref[base + piece, j * rows : (j + 1) * rows, :].astype(F32) * turned[:rows, column : column + 1]
            grad_ref[at, at_lane + j * LANES : at_lane + (j + 1) * LANES] = grad
            lanes = slice(j * LANES, (j + 1) * LANES)
            h1[at, lanes], h2[at, lanes] = two(grad)


def products(slots, arrived, l1, l2, r1, r2, rows, columns):
    size = l1.shape[0]
    _, tall, _ = arrived.shape
    pieces = size // rows
    part = tall // rows * LANES
    block = size // STEPS

    def body(
        slots_ref, a_hbm, l1_hbm, l2_hbm, r1_hbm, r2_hbm, p_hbm, grad_hbm,
        a_ref, l1_ref, l2_ref, r1_ref, r2_ref, grad_ref, h1, h2, t1, t2, p_ref, turned, ins, outs,
    ):
        band = own_band(slots_ref, columns)
        deep = pl.ds(0, part)
        pairs = (
            (a_hbm.at[pl.ds(band * pieces, pieces)], a_ref),
            (l1_hbm, l1_ref),
            (l2_hbm, l2_ref),
            (r1_hbm.at[deep], r1_ref),
            (r2_hbm.at[deep], r2_ref),
        )
        reads = [pltpu.make_async_copy(s, t, ins.at[k]) for k, (s, t) in enumerate(pairs)]
        for read in reads[:3]:
            read.start()
        reads[0].wait()
        for read in reads[3:]:
            read.start()
        dequant(a_ref, 0, pieces, turned, rows, 0, 0, grad_ref, h1, h2)
        for read in reads[1:3]:
            read.wait()
        keep = pltpu.make_async_copy(grad_ref, grad_hbm, outs.at[STEPS])
        keep.start()

        @pl.loop(0, part // block)
        def _(n):
            at = pl.ds(pl.multiple_of(n * block, block), block)
            half = dot(l1_ref[...], h1[:, at]) + (dot(l1_ref[...], h2[:, at]) + dot(l2_ref[...], h1[:, at]))
            t1[:, at], t2[:, at] = two(half)

        for read in reads[3:]:
            read.wait()

        def p_copy(n):
            at = pl.ds(pl.multiple_of(n * block, block), block)
            return pltpu.make_async_copy(p_ref.at[:, at], p_hbm.at[:, at], outs.at[n])

        @pl.loop(0, STEPS)
        def _(n):
            at = pl.ds(pl.multiple_of(n * block, block), block)
            p_ref[:, at] = dot(t1[...], r1_ref[:, at]) + (dot(t1[...], r2_ref[:, at]) + dot(t2[...], r1_ref[:, at]))
            p_copy(n).start()

        for n in range(STEPS):
            p_copy(n).wait()
        keep.wait()

    square = (size, size)
    narrow = (size, part)
    return pl.pallas_call(
        body,
        out_shape=[jax.ShapeDtypeStruct(square, F32), jax.ShapeDtypeStruct(narrow, F32)],
        in_specs=[SMEM] + [HBM] * 5,
        out_specs=[HBM] * 2,
        scratch_shapes=[pltpu.VMEM((pieces, tall, LANES), BF16)]
        + [pltpu.VMEM(square, BF16)] * 2
        + [pltpu.VMEM((part, size), BF16)] * 2
        + [pltpu.VMEM(narrow, F32)]
        + [pltpu.VMEM(narrow, BF16)] * 4
        + [pltpu.VMEM(square, F32), pltpu.VMEM((LANES, pieces * EXTRA), F32), DMA((5,)), DMA((STEPS + 1,))],
        compiler_params=PARAMS,
        cost_estimate=cost(12 * size * size * part, 20 * size * size),
        name="products",
    )(slots, arrived, l1, l2, r1, r2)


def graft(slots, arrived, l1, l2, r1, r2, earlier, grad, moment, rows, columns, entries):
    size = moment.shape[0]
    owners, tall, _ = arrived.shape
    pieces = size // rows
    block = size // STEPS
    done = grad.shape[1]
    part = size - done
    thin = size // FINE

    def body(
        slots_hbm, a_hbm, l1_hbm, l2_hbm, r1_hbm, r2_hbm, p_hbm, grad_hbm, m_hbm, out_hbm, fresh_hbm,
        slots_ref, a_ref, l1_ref, l2_ref, r1_ref, r2_ref, p_ref, grad_ref, h1, h2, t1, t2, m_ref, out_ref,
        turned, asum, psum, ins, outs,
    ):
        deep = pl.ds(done, part)

        def cut(n):
            return pl.ds(pl.multiple_of(n * block, block), block)

        pairs = (
            (slots_hbm, slots_ref),
            (a_hbm, a_ref),
            (l1_hbm, l1_ref),
            (l2_hbm, l2_ref),
            (r1_hbm.at[deep], r1_ref),
            (r2_hbm.at[deep], r2_ref),
        )
        reads = [pltpu.make_async_copy(s, t, ins.at[3, k]) for k, (s, t) in enumerate(pairs)]

        def p_read(n):
            at = cut(n)
            return pltpu.make_async_copy(p_hbm.at[:, at], p_ref.at[:, at], ins.at[0, n])

        def adam_reads(n):
            at = cut(n)
            pairs = ((grad_hbm.at[at], grad_ref.at[at, pl.ds(0, done)]), (m_hbm.at[at], m_ref.at[at]))
            return [pltpu.make_async_copy(s, t, ins.at[1 + k, n]) for k, (s, t) in enumerate(pairs)]

        for read in reads[:4]:
            read.start()
        for read in reads[:2]:
            read.wait()
        band = own_band(slots_ref, columns)
        base = band * pieces

        for read in reads[4:]:
            read.start()

        @pl.loop(0, STEPS)
        def _(n):
            for read in [p_read(n), *adam_reads(n)]:
                read.start()

        dequant(a_ref, base, pieces, turned, rows, done // LANES, done, grad_ref, h1, h2)
        heads = jnp.sum(a_ref[:, tall - EXTRA :, :].astype(F32), axis=0)[: EXTRA - 8]
        total = jnp.sum(heads, axis=0, keepdims=True)[:, :1]
        bound = 0.5 * jnp.sqrt(jnp.full((1, 1), entries, F32)) / jnp.sqrt(jnp.where(total > 0, total, 1.0))
        clip = jnp.where(total > 0, jnp.minimum(bound, 1.0), 1.0)
        asum[...] = jnp.zeros_like(asum)
        psum[...] = jnp.zeros_like(psum)
        for read in reads[2:4]:
            read.wait()

        def fresh_copy(n):
            return pltpu.make_async_copy(m_ref.at[cut(n)], fresh_hbm.at[cut(n)], outs.at[0, n])

        def out_copy(n):
            to = pl.ds(pl.multiple_of(band * size + n * block, block), block)
            return pltpu.make_async_copy(out_ref.at[cut(n)], out_hbm.at[to], outs.at[1, n])

        def adam(n):
            for read in adam_reads(n):
                read.wait()
            steps = []
            for k in range(block // thin):
                line = pl.ds(pl.multiple_of(n * block + k * thin, thin), thin)
                held = grad_ref[line, :] * clip
                square = held * held
                fresh = 0.9 * m_ref[line, :] + 0.1 * square
                m_ref[line, :] = fresh
                root = fresh * lax.rsqrt(fresh) + 1e-08
                inverse = pl.reciprocal(root, approx=True)
                ratios = held * (inverse * (2.0 - root * inverse))
                steps.append(fold(ratios * ratios))
            asum[...] += sum(steps)
            fresh_copy(n).start()

        half = dot(l1_ref[...], h1[...]) + (dot(l1_ref[...], h2[...]) + dot(l2_ref[...], h1[...]))
        t1[...], t2[...] = two(half)
        for read in reads[4:]:
            read.wait()

        @pl.loop(0, STEPS)
        def _(n):
            p_read(n).wait()
            at = cut(n)
            more = dot(t1[...], r1_ref[:, at]) + (dot(t1[...], r2_ref[:, at]) + dot(t2[...], r1_ref[:, at]))
            product = p_ref[:, at] + more
            p_ref[:, at] = product
            psum[...] += fold(product * product)
            adam(n)

        norm = jnp.sqrt(everywhere(psum[...]) * (clip * clip) + 1e-12)
        ratio = clip * (jnp.sqrt(everywhere(asum[...])) / norm)

        @pl.loop(0, STEPS)
        def _(n):
            out_ref[cut(n), :] = (p_ref[cut(n), :] * ratio).astype(BF16)
            out_copy(n).start()

        for n in range(STEPS):
            fresh_copy(n).wait()
            out_copy(n).wait()

    square = (size, size)
    return pl.pallas_call(
        body,
        out_shape=[
            jax.ShapeDtypeStruct((owners * rows, size), BF16),
            jax.ShapeDtypeStruct(square, F32),
        ],
        in_specs=[HBM] * 9,
        out_specs=[HBM, HBM],
        scratch_shapes=[pltpu.SMEM(slots.shape, jnp.int32), pltpu.VMEM((owners, tall, LANES), BF16)]
        + [pltpu.VMEM(square, BF16)] * 2
        + [pltpu.VMEM((part, size), BF16)] * 2
        + [pltpu.VMEM(square, F32)] * 2
        + [pltpu.VMEM((size, part), BF16)] * 4
        + [
            pltpu.VMEM(square, F32),
            pltpu.VMEM(square, BF16),
            pltpu.VMEM((LANES, pieces * EXTRA), F32),
            pltpu.VMEM((8, LANES), F32),
            pltpu.VMEM((8, LANES), F32),
            DMA((4, 6)),
            DMA((2, STEPS)),
        ],
        compiler_params=PARAMS,
        cost_estimate=cost(12 * size * size * part, 24 * size * size),
        name="graft",
    )(slots, arrived, l1, l2, r1, r2, earlier, grad, moment)


def place(slots, returned, cols):
    owners, rows, width = returned.shape
    columns = cols // width

    def body(slots_ref, r_ref, out_hbm, inverse, outs):
        first = lax.div(lax.axis_index("fsdp") * rows, width) * columns
        invert(slots_ref, inverse)

        def write(k):
            here = pl.ds(pl.multiple_of(k * width, width), width)
            return pltpu.make_async_copy(r_ref.at[inverse[first + k]], out_hbm.at[:, here], outs.at[k])

        @pl.loop(0, columns)
        def _(k):
            write(k).start()

        @pl.loop(0, columns)
        def _(k):
            write(k).wait()

    return pl.pallas_call(
        body,
        out_shape=jax.ShapeDtypeStruct((rows, cols), BF16),
        in_specs=[SMEM, pl.BlockSpec(memory_space=pltpu.VMEM)],
        out_specs=HBM,
        scratch_shapes=[pltpu.SMEM((owners,), jnp.int32), DMA((columns,))],
        compiler_params=pltpu.CompilerParams(vmem_limit_bytes=12 * 1024 * 1024),
        cost_estimate=cost(0, 4 * rows * cols),
        name="place",
    )(slots, returned)


def on_device(q_values, scales, block_slots, left_root, right_root, second_moment):
    count = lax.axis_size("fsdp")
    planes = lax.axis_size("grp")
    rows, cols = q_values.shape
    width = left_root.shape[-1]
    columns = cols // width
    first = width * 3 // 4

    def exchange(value):
        return lax.all_to_all(value, "fsdp", split_axis=0, concat_axis=0, tiled=True)

    arrived = exchange(pack(block_slots, q_values, scales, [], width, 0, first))
    own = square_sum(q_values, scales)
    sums = [own]
    for k in range(1, planes):
        sums.append(lax.ppermute(own, "grp", [(i, (i + k) % planes) for i in range(planes)]))
    *sums, l1, l2, r1, r2 = lax.optimization_barrier((*sums, *split_roots(left_root[0, 0], right_root[0, 0])))
    roots = (l1, l2, r1, r2)
    later = exchange(pack(block_slots, q_values, scales, sums, width, first, width - first))

    product, grad = products(block_slots, arrived, *roots, rows, columns)
    outgoing, fresh = graft(
        block_slots, later, *roots, product, grad, second_moment[0, 0], rows, columns, rows * count * cols * planes
    )
    update = place(block_slots, exchange(outgoing.reshape(count, rows, width)), cols)
    return (update, fresh[None, None])


def solution(mesh):
    in_specs = (
        P("fsdp", "grp"),
        P("fsdp", "grp"),
        P("grp", None),
        P("grp", "fsdp", None, None),
        P("grp", "fsdp", None, None),
        P("grp", "fsdp", None, None),
    )
    out_specs = (P("fsdp", "grp"), P("grp", "fsdp", None, None))
    return jax.shard_map(
        on_device, mesh=mesh, in_specs=in_specs, out_specs=out_specs, check_vma=False
    )
```

```python
import jax
import jax.numpy as jnp
from jax import lax
from jax.experimental import pallas as pl
from jax.experimental.pallas import tpu as pltpu
from jax.sharding import PartitionSpec as P

LANES = 128
EXTRA = 16
STEPS = 4
FINE = 16
F32 = jnp.float32
BF16 = jnp.bfloat16
HBM = pl.BlockSpec(memory_space=pltpu.HBM)
SMEM = pl.BlockSpec(memory_space=pltpu.SMEM)
PARAMS = pltpu.CompilerParams(vmem_limit_bytes=63 * 1024 * 1024)
DMA = pltpu.SemaphoreType.DMA


def cost(flops, nbytes):
    return pl.CostEstimate(flops=flops, bytes_accessed=nbytes, transcendentals=0)


def dot(a, b):
    return jnp.dot(a, b, preferred_element_type=F32)


def two(value):
    top = value.astype(BF16)
    return top, (value - top.astype(F32)).astype(BF16)


def fold(value):
    rows, cols = value.shape
    total = value[:, :LANES]
    for j in range(1, cols // LANES):
        total = total + value[:, j * LANES : (j + 1) * LANES]
    return total.reshape(rows // 8, 8, LANES).sum(axis=0)


def everywhere(value):
    return jnp.sum(value, axis=(0, 1), keepdims=True)


def invert(slots_ref, inverse_ref):
    for owner in range(slots_ref.shape[1]):
        inverse_ref[slots_ref[0, owner]] = owner


def own_band(slots_ref, columns):
    return lax.div(slots_ref[0, lax.axis_index("fsdp")], columns)


def pack(slots, q_values, scales, sums_of, width, start, part):
    owners = slots.shape[1]
    rows, cols = q_values.shape
    columns = cols // width
    groups = width // LANES
    here = part // LANES
    tall = here * rows + EXTRA
    sums = EXTRA - groups

    def body(slots_hbm, q_hbm, s_hbm, *rest):
        e_hbm = rest[: len(sums_of)]
        out_hbm, slots_ref, inverse, q_ref, s_ref, e_ref, turned, out_ref, ins, outs = rest[-10:]

        def q_read(k):
            at = pl.ds(pl.multiple_of(k * width + start, LANES), part)
            return pltpu.make_async_copy(q_hbm.at[:, at], q_ref.at[k], ins.at[k])

        def write(k, band):
            at = band * columns + k
            return pltpu.make_async_copy(out_ref.at[k], out_hbm.at[inverse[at]], outs.at[at])

        reads = [
            pltpu.make_async_copy(slots_hbm, slots_ref, ins.at[columns]),
            pltpu.make_async_copy(s_hbm, s_ref, ins.at[columns + 1]),
        ]
        for k, src in enumerate(e_hbm):
            reads.append(pltpu.make_async_copy(src, e_ref.at[k], ins.at[columns + 2 + k]))
        for read in reads:
            read.start()

        @pl.loop(0, columns)
        def _(k):
            q_read(k).start()

        bands = range(owners // columns) if e_hbm else [lax.div(lax.axis_index("fsdp") * rows, width)]
        for read in reads:
            read.wait()
        invert(slots_ref, inverse)
        padded = jnp.concatenate([s_ref[...].astype(F32), jnp.zeros((LANES - rows, LANES), F32)], axis=0)
        turned[...] = padded.T
        head = jnp.zeros((sums, LANES), F32)
        if e_hbm:
            value = e_ref[0]
            for k in range(1, len(e_hbm)):
                value = value + e_ref[k]
            high = value.astype(BF16)
            mid, low = two(value - high.astype(F32))
            row = lax.broadcasted_iota(jnp.int32, head.shape, 0)
            for k, term in enumerate((high, mid, low)):
                head = jnp.where(row == k, jnp.broadcast_to(term[:1].astype(F32), head.shape), head)

        @pl.loop(0, columns)
        def _(k):
            scale = turned[pl.ds(pl.multiple_of(k * groups, groups), groups), :]
            out_ref[k, here * rows :, :] = jnp.concatenate([head, scale], axis=0).astype(BF16)
            q_read(k).wait()
            for j in range(here):
                out_ref[k, j * rows : (j + 1) * rows, :] = q_ref[k, :, j * LANES : (j + 1) * LANES]
            for band in bands:
                write(k, band).start()

        @pl.loop(0, columns)
        def _(k):
            for band in bands:
                write(k, band).wait()

    operands = [slots, q_values, scales, *sums_of]
    return pl.pallas_call(
        body,
        out_shape=jax.ShapeDtypeStruct((owners, tall, LANES), BF16),
        in_specs=[HBM] * len(operands),
        out_specs=HBM,
        scratch_shapes=[
            pltpu.SMEM(slots.shape, jnp.int32),
            pltpu.SMEM((owners,), jnp.int32),
            pltpu.VMEM((columns, rows, part), BF16),
            pltpu.VMEM(scales.shape, BF16),
            pltpu.VMEM((max(len(sums_of), 1), 8, LANES), F32),
            pltpu.VMEM((LANES, LANES), F32),
            pltpu.VMEM((columns, tall, LANES), BF16),
            DMA((columns + 2 + len(sums_of),)),
            DMA((owners,)),
        ],
        compiler_params=PARAMS,
        cost_estimate=cost(0, 2 * rows * cols + 2 * owners * tall * LANES),
        name=f"pack_{start}",
    )(*operands)


def square_sum(q_values, scales):
    rows, cols = q_values.shape
    groups = scales.shape[1]
    group = cols // groups

    def body(q_hbm, s_hbm, out_ref, q_ref, s_ref, sems):
        reads = [pltpu.make_async_copy(q_hbm, q_ref, sems.at[0]), pltpu.make_async_copy(s_hbm, s_ref, sems.at[1])]
        for read in reads:
            read.start()
        for read in reads:
            read.wait()
        total = jnp.zeros((rows, group), F32)
        for j in range(groups):
            grad = q_ref[:, j * group : (j + 1) * group].astype(F32) * s_ref[:, j : j + 1].astype(F32)
            total = total + grad * grad
        out_ref[...] = jnp.full((8, LANES), jnp.sum(total))

    return pl.pallas_call(
        body,
        out_shape=jax.ShapeDtypeStruct((8, LANES), F32),
        in_specs=[HBM] * 2,
        scratch_shapes=[pltpu.VMEM((rows, cols), BF16), pltpu.VMEM(scales.shape, BF16), DMA((2,))],
        compiler_params=PARAMS,
        cost_estimate=cost(3 * rows * cols, 2 * rows * cols),
        name="square_sum",
    )(q_values, scales)


def split_roots(left, right):
    size = left.shape[0]
    rows = size // STEPS

    def body(l_hbm, r_hbm, l1_hbm, l2_hbm, r1_hbm, r2_hbm, full, top, low, ins, outs):
        jobs = []
        for src, high_hbm, low_hbm in ((l_hbm, l1_hbm, l2_hbm), (r_hbm, r1_hbm, r2_hbm)):
            for n in range(STEPS):
                at = pl.ds(n * rows, rows)
                jobs.append((src.at[at], high_hbm.at[at], low_hbm.at[at]))
        reads = [pltpu.make_async_copy(job[0], full.at[k], ins.at[k]) for k, job in enumerate(jobs)]
        for read in reads:
            read.start()
        writes = []
        for k, (_, high_to, low_to) in enumerate(jobs):
            reads[k].wait()
            top[k], low[k] = two(full[k])
            for h, (src, to) in enumerate(((top.at[k], high_to), (low.at[k], low_to))):
                write = pltpu.make_async_copy(src, to, outs.at[2 * k + h])
                write.start()
                writes.append(write)
        for write in writes:
            write.wait()

    jobs = 2 * STEPS
    return pl.pallas_call(
        body,
        out_shape=[jax.ShapeDtypeStruct((size, size), BF16)] * 4,
        in_specs=[HBM] * 2,
        out_specs=[HBM] * 4,
        scratch_shapes=[
            pltpu.VMEM((jobs, rows, size), F32),
            pltpu.VMEM((jobs, rows, size), BF16),
            pltpu.VMEM((jobs, rows, size), BF16),
            DMA((jobs,)),
            DMA((2 * jobs,)),
        ],
        compiler_params=PARAMS,
        cost_estimate=cost(4 * size * size, 16 * size * size),
        name="split_roots",
    )(left, right)


def dequant(a_ref, base, pieces, turned, rows, group, at_lane, grad_ref, h1, h2):
    tall = a_ref.shape[1]
    here = (tall - EXTRA) // rows
    scales = a_ref[pl.ds(base, pieces), here * rows :, :].astype(F32).reshape(pieces * EXTRA, LANES)
    turned[...] = scales.T
    for piece in range(pieces):
        at = slice(piece * rows, (piece + 1) * rows)
        for j in range(here):
            column = piece * EXTRA + EXTRA - 8 + group + j
            grad = a_ref[base + piece, j * rows : (j + 1) * rows, :].astype(F32) * turned[:rows, column : column + 1]
            grad_ref[at, at_lane + j * LANES : at_lane + (j + 1) * LANES] = grad
            lanes = slice(j * LANES, (j + 1) * LANES)
            h1[at, lanes], h2[at, lanes] = two(grad)


def products(slots, arrived, l1, l2, r1, r2, rows, columns):
    size = l1.shape[0]
    _, tall, _ = arrived.shape
    pieces = size // rows
    part = tall // rows * LANES
    block = size // STEPS

    def body(
        slots_ref, a_hbm, l1_hbm, l2_hbm, r1_hbm, r2_hbm, p_hbm, grad_hbm,
        a_ref, l1_ref, l2_ref, r1_ref, r2_ref, grad_ref, h1, h2, t1, t2, p_ref, turned, ins, outs,
    ):
        band = own_band(slots_ref, columns)
        deep = pl.ds(0, part)
        pairs = (
            (a_hbm.at[pl.ds(band * pieces, pieces)], a_ref),
            (l1_hbm, l1_ref),
            (l2_hbm, l2_ref),
            (r1_hbm.at[deep], r1_ref),
            (r2_hbm.at[deep], r2_ref),
        )
        reads = [pltpu.make_async_copy(s, t, ins.at[k]) for k, (s, t) in enumerate(pairs)]
        for read in reads[:3]:
            read.start()
        reads[0].wait()
        for read in reads[3:]:
            read.start()
        dequant(a_ref, 0, pieces, turned, rows, 0, 0, grad_ref, h1, h2)
        for read in reads[1:3]:
            read.wait()
        keep = pltpu.make_async_copy(grad_ref, grad_hbm, outs.at[STEPS])
        keep.start()

        @pl.loop(0, part // block)
        def _(n):
            at = pl.ds(pl.multiple_of(n * block, block), block)
            half = dot(l1_ref[...], h1[:, at]) + (dot(l1_ref[...], h2[:, at]) + dot(l2_ref[...], h1[:, at]))
            t1[:, at], t2[:, at] = two(half)

        for read in reads[3:]:
            read.wait()

        def p_copy(n):
            at = pl.ds(pl.multiple_of(n * block, block), block)
            return pltpu.make_async_copy(p_ref.at[:, at], p_hbm.at[:, at], outs.at[n])

        @pl.loop(0, STEPS)
        def _(n):
            at = pl.ds(pl.multiple_of(n * block, block), block)
            p_ref[:, at] = dot(t1[...], r1_ref[:, at]) + (dot(t1[...], r2_ref[:, at]) + dot(t2[...], r1_ref[:, at]))
            p_copy(n).start()

        for n in range(STEPS):
            p_copy(n).wait()
        keep.wait()

    square = (size, size)
    narrow = (size, part)
    return pl.pallas_call(
        body,
        out_shape=[jax.ShapeDtypeStruct(square, F32), jax.ShapeDtypeStruct(narrow, F32)],
        in_specs=[SMEM] + [HBM] * 5,
        out_specs=[HBM] * 2,
        scratch_shapes=[pltpu.VMEM((pieces, tall, LANES), BF16)]
        + [pltpu.VMEM(square, BF16)] * 2
        + [pltpu.VMEM((part, size), BF16)] * 2
        + [pltpu.VMEM(narrow, F32)]
        + [pltpu.VMEM(narrow, BF16)] * 4
        + [pltpu.VMEM(square, F32), pltpu.VMEM((LANES, pieces * EXTRA), F32), DMA((5,)), DMA((STEPS + 1,))],
        compiler_params=PARAMS,
        cost_estimate=cost(12 * size * size * part, 20 * size * size),
        name="products",
    )(slots, arrived, l1, l2, r1, r2)


def graft(slots, arrived, l1, l2, r1, r2, earlier, grad, moment, rows, columns, entries):
    size = moment.shape[0]
    owners, tall, _ = arrived.shape
    pieces = size // rows
    block = size // STEPS
    done = grad.shape[1]
    part = size - done
    thin = size // FINE

    def body(
        slots_hbm, a_hbm, l1_hbm, l2_hbm, r1_hbm, r2_hbm, p_hbm, grad_hbm, m_hbm, out_hbm, fresh_hbm,
        slots_ref, a_ref, l1_ref, l2_ref, r1_ref, r2_ref, p_ref, grad_ref, h1, h2, t1, t2, m_ref, out_ref,
        turned, asum, psum, ins, outs,
    ):
        deep = pl.ds(done, part)

        def cut(n):
            return pl.ds(pl.multiple_of(n * block, block), block)

        pairs = (
            (slots_hbm, slots_ref),
            (a_hbm, a_ref),
            (l1_hbm, l1_ref),
            (l2_hbm, l2_ref),
            (r1_hbm.at[deep], r1_ref),
            (r2_hbm.at[deep], r2_ref),
        )
        reads = [pltpu.make_async_copy(s, t, ins.at[3, k]) for k, (s, t) in enumerate(pairs)]

        def p_read(n):
            at = cut(n)
            return pltpu.make_async_copy(p_hbm.at[:, at], p_ref.at[:, at], ins.at[0, n])

        def adam_reads(n):
            at = cut(n)
            pairs = ((grad_hbm.at[at], grad_ref.at[at, pl.ds(0, done)]), (m_hbm.at[at], m_ref.at[at]))
            return [pltpu.make_async_copy(s, t, ins.at[1 + k, n]) for k, (s, t) in enumerate(pairs)]

        for read in reads[:4]:
            read.start()
        for read in reads[:2]:
            read.wait()
        band = own_band(slots_ref, columns)
        base = band * pieces

        for read in reads[4:]:
            read.start()

        @pl.loop(0, STEPS)
        def _(n):
            for read in [p_read(n), *adam_reads(n)]:
                read.start()

        dequant(a_ref, base, pieces, turned, rows, done // LANES, done, grad_ref, h1, h2)
        heads = jnp.sum(a_ref[:, tall - EXTRA :, :].astype(F32), axis=0)[: EXTRA - 8]
        total = jnp.sum(heads, axis=0, keepdims=True)[:, :1]
        bound = 0.5 * jnp.sqrt(jnp.full((1, 1), entries, F32)) / jnp.sqrt(jnp.where(total > 0, total, 1.0))
        clip = jnp.where(total > 0, jnp.minimum(bound, 1.0), 1.0)
        asum[...] = jnp.zeros_like(asum)
        psum[...] = jnp.zeros_like(psum)
        for read in reads[2:4]:
            read.wait()

        def fresh_copy(n):
            return pltpu.make_async_copy(m_ref.at[cut(n)], fresh_hbm.at[cut(n)], outs.at[0, n])

        def out_copy(n):
            to = pl.ds(pl.multiple_of(band * size + n * block, block), block)
            return pltpu.make_async_copy(out_ref.at[cut(n)], out_hbm.at[to], outs.at[1, n])

        def adam(n):
            for read in adam_reads(n):
                read.wait()
            steps = []
            for k in range(block // thin):
                line = pl.ds(pl.multiple_of(n * block + k * thin, thin), thin)
                held = grad_ref[line, :] * clip
                square = held * held
                fresh = 0.9 * m_ref[line, :] + 0.1 * square
                m_ref[line, :] = fresh
                root = fresh * lax.rsqrt(fresh) + 1e-08
                inverse = pl.reciprocal(root, approx=True)
                ratios = held * (inverse * (2.0 - root * inverse))
                steps.append(fold(ratios * ratios))
            asum[...] += sum(steps)
            fresh_copy(n).start()


        @pl.loop(0, STEPS)
        def _(n):
            at = cut(n)
            half = dot(l1_ref[at, :], h1[...]) + (dot(l1_ref[at, :], h2[...]) + dot(l2_ref[at, :], h1[...]))
            t1[at, :], t2[at, :] = two(half)

        for read in reads[4:]:
            read.wait()

        @pl.loop(0, STEPS)
        def _(n):
            p_read(n).wait()
            at = cut(n)
            more = dot(t1[...], r1_ref[:, at]) + (dot(t1[...], r2_ref[:, at]) + dot(t2[...], r1_ref[:, at]))
            product = p_ref[:, at] + more
            p_ref[:, at] = product
            psum[...] += fold(product * product)
            adam(n)

        norm = jnp.sqrt(everywhere(psum[...]) * (clip * clip) + 1e-12)
        ratio = clip * (jnp.sqrt(everywhere(asum[...])) / norm)

        @pl.loop(0, STEPS)
        def _(n):
            out_ref[cut(n), :] = (p_ref[cut(n), :] * ratio).astype(BF16)
            out_copy(n).start()

        for n in range(STEPS):
            fresh_copy(n).wait()
            out_copy(n).wait()

    square = (size, size)
    return pl.pallas_call(
        body,
        out_shape=[
            jax.ShapeDtypeStruct((owners * rows, size), BF16),
            jax.ShapeDtypeStruct(square, F32),
        ],
        in_specs=[HBM] * 9,
        out_specs=[HBM, HBM],
        scratch_shapes=[pltpu.SMEM(slots.shape, jnp.int32), pltpu.VMEM((owners, tall, LANES), BF16)]
        + [pltpu.VMEM(square, BF16)] * 2
        + [pltpu.VMEM((part, size), BF16)] * 2
        + [pltpu.VMEM(square, F32)] * 2
        + [pltpu.VMEM((size, part), BF16)] * 4
        + [
            pltpu.VMEM(square, F32),
            pltpu.VMEM(square, BF16),
            pltpu.VMEM((LANES, pieces * EXTRA), F32),
            pltpu.VMEM((8, LANES), F32),
            pltpu.VMEM((8, LANES), F32),
            DMA((4, 6)),
            DMA((2, STEPS)),
        ],
        compiler_params=PARAMS,
        cost_estimate=cost(12 * size * size * part, 24 * size * size),
        name="graft",
    )(slots, arrived, l1, l2, r1, r2, earlier, grad, moment)


def place(slots, returned, cols):
    owners, rows, width = returned.shape
    columns = cols // width

    def body(slots_ref, r_ref, out_hbm, inverse, outs):
        first = lax.div(lax.axis_index("fsdp") * rows, width) * columns
        invert(slots_ref, inverse)

        def write(k):
            here = pl.ds(pl.multiple_of(k * width, width), width)
            return pltpu.make_async_copy(r_ref.at[inverse[first + k]], out_hbm.at[:, here], outs.at[k])

        @pl.loop(0, columns)
        def _(k):
            write(k).start()

        @pl.loop(0, columns)
        def _(k):
            write(k).wait()

    return pl.pallas_call(
        body,
        out_shape=jax.ShapeDtypeStruct((rows, cols), BF16),
        in_specs=[SMEM, pl.BlockSpec(memory_space=pltpu.VMEM)],
        out_specs=HBM,
        scratch_shapes=[pltpu.SMEM((owners,), jnp.int32), DMA((columns,))],
        compiler_params=pltpu.CompilerParams(vmem_limit_bytes=12 * 1024 * 1024),
        cost_estimate=cost(0, 4 * rows * cols),
        name="place",
    )(slots, returned)


def on_device(q_values, scales, block_slots, left_root, right_root, second_moment):
    count = lax.axis_size("fsdp")
    planes = lax.axis_size("grp")
    rows, cols = q_values.shape
    width = left_root.shape[-1]
    columns = cols // width
    first = width * 3 // 4

    def exchange(value):
        return lax.all_to_all(value, "fsdp", split_axis=0, concat_axis=0, tiled=True)

    arrived = exchange(pack(block_slots, q_values, scales, [], width, 0, first))
    own = square_sum(q_values, scales)
    sums = [own]
    for k in range(1, planes):
        sums.append(lax.ppermute(own, "grp", [(i, (i + k) % planes) for i in range(planes)]))
    *sums, l1, l2, r1, r2 = lax.optimization_barrier((*sums, *split_roots(left_root[0, 0], right_root[0, 0])))
    roots = (l1, l2, r1, r2)
    later = exchange(pack(block_slots, q_values, scales, sums, width, first, width - first))

    product, grad = products(block_slots, arrived, *roots, rows, columns)
    outgoing, fresh = graft(
        block_slots, later, *roots, product, grad, second_moment[0, 0], rows, columns, rows * count * cols * planes
    )
    update = place(block_slots, exchange(outgoing.reshape(count, rows, width)), cols)
    return (update, fresh[None, None])


def solution(mesh):
    in_specs = (
        P("fsdp", "grp"),
        P("fsdp", "grp"),
        P("grp", None),
        P("grp", "fsdp", None, None),
        P("grp", "fsdp", None, None),
        P("grp", "fsdp", None, None),
    )
    out_specs = (P("fsdp", "grp"), P("grp", "fsdp", None, None))
    return jax.shard_map(
        on_device, mesh=mesh, in_specs=in_specs, out_specs=out_specs, check_vma=False
    )
```

```python
import jax
import jax.numpy as jnp
from jax import lax
from jax.experimental import pallas as pl
from jax.experimental.pallas import tpu as pltpu
from jax.sharding import PartitionSpec as P

LANES = 128
EXTRA = 16
STEPS = 4
FINE = 16
F32 = jnp.float32
BF16 = jnp.bfloat16
HBM = pl.BlockSpec(memory_space=pltpu.HBM)
SMEM = pl.BlockSpec(memory_space=pltpu.SMEM)
PARAMS = pltpu.CompilerParams(vmem_limit_bytes=63 * 1024 * 1024)
DMA = pltpu.SemaphoreType.DMA


def cost(flops, nbytes):
    return pl.CostEstimate(flops=flops, bytes_accessed=nbytes, transcendentals=0)


def dot(a, b):
    return jnp.dot(a, b, preferred_element_type=F32)


def two(value):
    top = value.astype(BF16)
    return top, (value - top.astype(F32)).astype(BF16)


def fold(value):
    rows, cols = value.shape
    total = value[:, :LANES]
    for j in range(1, cols // LANES):
        total = total + value[:, j * LANES : (j + 1) * LANES]
    return total.reshape(rows // 8, 8, LANES).sum(axis=0)


def everywhere(value):
    return jnp.sum(value, axis=(0, 1), keepdims=True)


def invert(slots_ref, inverse_ref):
    for owner in range(slots_ref.shape[1]):
        inverse_ref[slots_ref[0, owner]] = owner


def own_band(slots_ref, columns):
    return lax.div(slots_ref[0, lax.axis_index("fsdp")], columns)


def pack(slots, q_values, scales, sums_of, width, start, part):
    owners = slots.shape[1]
    rows, cols = q_values.shape
    columns = cols // width
    groups = width // LANES
    here = part // LANES
    tall = here * rows + EXTRA
    sums = EXTRA - groups

    def body(slots_hbm, q_hbm, s_hbm, *rest):
        e_hbm = rest[: len(sums_of)]
        out_hbm, slots_ref, inverse, q_ref, s_ref, e_ref, turned, out_ref, ins, outs = rest[-10:]

        def q_read(k):
            at = pl.ds(pl.multiple_of(k * width + start, LANES), part)
            return pltpu.make_async_copy(q_hbm.at[:, at], q_ref.at[k], ins.at[k])

        def write(k, band):
            at = band * columns + k
            return pltpu.make_async_copy(out_ref.at[k], out_hbm.at[inverse[at]], outs.at[at])

        reads = [
            pltpu.make_async_copy(slots_hbm, slots_ref, ins.at[columns]),
            pltpu.make_async_copy(s_hbm, s_ref, ins.at[columns + 1]),
        ]
        for k, src in enumerate(e_hbm):
            reads.append(pltpu.make_async_copy(src, e_ref.at[k], ins.at[columns + 2 + k]))
        for read in reads:
            read.start()

        @pl.loop(0, columns)
        def _(k):
            q_read(k).start()

        bands = range(owners // columns) if e_hbm else [lax.div(lax.axis_index("fsdp") * rows, width)]
        for read in reads:
            read.wait()
        invert(slots_ref, inverse)
        padded = jnp.concatenate([s_ref[...].astype(F32), jnp.zeros((LANES - rows, LANES), F32)], axis=0)
        turned[...] = padded.T
        head = jnp.zeros((sums, LANES), F32)
        if e_hbm:
            value = e_ref[0]
            for k in range(1, len(e_hbm)):
                value = value + e_ref[k]
            high = value.astype(BF16)
            mid, low = two(value - high.astype(F32))
            row = lax.broadcasted_iota(jnp.int32, head.shape, 0)
            for k, term in enumerate((high, mid, low)):
                head = jnp.where(row == k, jnp.broadcast_to(term[:1].astype(F32), head.shape), head)

        @pl.loop(0, columns)
        def _(k):
            scale = turned[pl.ds(pl.multiple_of(k * groups, groups), groups), :]
            out_ref[k, here * rows :, :] = jnp.concatenate([head, scale], axis=0).astype(BF16)
            q_read(k).wait()
            for j in range(here):
                out_ref[k, j * rows : (j + 1) * rows, :] = q_ref[k, :, j * LANES : (j + 1) * LANES]
            for band in bands:
                write(k, band).start()

        @pl.loop(0, columns)
        def _(k):
            for band in bands:
                write(k, band).wait()

    operands = [slots, q_values, scales, *sums_of]
    return pl.pallas_call(
        body,
        out_shape=jax.ShapeDtypeStruct((owners, tall, LANES), BF16),
        in_specs=[HBM] * len(operands),
        out_specs=HBM,
        scratch_shapes=[
            pltpu.SMEM(slots.shape, jnp.int32),
            pltpu.SMEM((owners,), jnp.int32),
            pltpu.VMEM((columns, rows, part), BF16),
            pltpu.VMEM(scales.shape, BF16),
            pltpu.VMEM((max(len(sums_of), 1), 8, LANES), F32),
            pltpu.VMEM((LANES, LANES), F32),
            pltpu.VMEM((columns, tall, LANES), BF16),
            DMA((columns + 2 + len(sums_of),)),
            DMA((owners,)),
        ],
        compiler_params=PARAMS,
        cost_estimate=cost(0, 2 * rows * cols + 2 * owners * tall * LANES),
        name=f"pack_{start}",
    )(*operands)


def square_sum(q_values, scales):
    rows, cols = q_values.shape
    groups = scales.shape[1]
    group = cols // groups

    def body(q_hbm, s_hbm, out_ref, q_ref, s_ref, sems):
        reads = [pltpu.make_async_copy(q_hbm, q_ref, sems.at[0]), pltpu.make_async_copy(s_hbm, s_ref, sems.at[1])]
        for read in reads:
            read.start()
        for read in reads:
            read.wait()
        total = jnp.zeros((rows, group), F32)
        for j in range(groups):
            grad = q_ref[:, j * group : (j + 1) * group].astype(F32) * s_ref[:, j : j + 1].astype(F32)
            total = total + grad * grad
        out_ref[...] = jnp.full((8, LANES), jnp.sum(total))

    return pl.pallas_call(
        body,
        out_shape=jax.ShapeDtypeStruct((8, LANES), F32),
        in_specs=[HBM] * 2,
        scratch_shapes=[pltpu.VMEM((rows, cols), BF16), pltpu.VMEM(scales.shape, BF16), DMA((2,))],
        compiler_params=PARAMS,
        cost_estimate=cost(3 * rows * cols, 2 * rows * cols),
        name="square_sum",
    )(q_values, scales)


def split_roots(left, right):
    size = left.shape[0]
    rows = size // STEPS

    def body(l_hbm, r_hbm, l1_hbm, l2_hbm, r1_hbm, r2_hbm, full, top, low, ins, outs):
        jobs = []
        for src, high_hbm, low_hbm in ((l_hbm, l1_hbm, l2_hbm), (r_hbm, r1_hbm, r2_hbm)):
            for n in range(STEPS):
                at = pl.ds(n * rows, rows)
                jobs.append((src.at[at], high_hbm.at[at], low_hbm.at[at]))
        reads = [pltpu.make_async_copy(job[0], full.at[k], ins.at[k]) for k, job in enumerate(jobs)]
        for read in reads:
            read.start()
        writes = []
        for k, (_, high_to, low_to) in enumerate(jobs):
            reads[k].wait()
            top[k], low[k] = two(full[k])
            for h, (src, to) in enumerate(((top.at[k], high_to), (low.at[k], low_to))):
                write = pltpu.make_async_copy(src, to, outs.at[2 * k + h])
                write.start()
                writes.append(write)
        for write in writes:
            write.wait()

    jobs = 2 * STEPS
    return pl.pallas_call(
        body,
        out_shape=[jax.ShapeDtypeStruct((size, size), BF16)] * 4,
        in_specs=[HBM] * 2,
        out_specs=[HBM] * 4,
        scratch_shapes=[
            pltpu.VMEM((jobs, rows, size), F32),
            pltpu.VMEM((jobs, rows, size), BF16),
            pltpu.VMEM((jobs, rows, size), BF16),
            DMA((jobs,)),
            DMA((2 * jobs,)),
        ],
        compiler_params=PARAMS,
        cost_estimate=cost(4 * size * size, 16 * size * size),
        name="split_roots",
    )(left, right)


def dequant(a_ref, base, pieces, turned, rows, group, at_lane, grad_ref, h1, h2):
    tall = a_ref.shape[1]
    here = (tall - EXTRA) // rows
    scales = a_ref[pl.ds(base, pieces), here * rows :, :].astype(F32).reshape(pieces * EXTRA, LANES)
    turned[...] = scales.T
    for piece in range(pieces):
        at = slice(piece * rows, (piece + 1) * rows)
        for j in range(here):
            column = piece * EXTRA + EXTRA - 8 + group + j
            grad = a_ref[base + piece, j * rows : (j + 1) * rows, :].astype(F32) * turned[:rows, column : column + 1]
            grad_ref[at, at_lane + j * LANES : at_lane + (j + 1) * LANES] = grad
            lanes = slice(j * LANES, (j + 1) * LANES)
            h1[at, lanes], h2[at, lanes] = two(grad)


def products(slots, arrived, l1, l2, r1, r2, rows, columns):
    size = l1.shape[0]
    _, tall, _ = arrived.shape
    pieces = size // rows
    part = tall // rows * LANES
    block = size // STEPS

    def body(
        slots_ref, a_hbm, l1_hbm, l2_hbm, r1_hbm, r2_hbm, p_hbm, grad_hbm,
        a_ref, l1_ref, l2_ref, r1_ref, r2_ref, grad_ref, h1, h2, t1, t2, p_ref, turned, ins, outs,
    ):
        band = own_band(slots_ref, columns)
        deep = pl.ds(0, part)
        pairs = (
            (a_hbm.at[pl.ds(band * pieces, pieces)], a_ref),
            (l1_hbm, l1_ref),
            (l2_hbm, l2_ref),
            (r1_hbm.at[deep], r1_ref),
            (r2_hbm.at[deep], r2_ref),
        )
        reads = [pltpu.make_async_copy(s, t, ins.at[k]) for k, (s, t) in enumerate(pairs)]
        for read in reads[:3]:
            read.start()
        reads[0].wait()
        for read in reads[3:]:
            read.start()
        dequant(a_ref, 0, pieces, turned, rows, 0, 0, grad_ref, h1, h2)
        for read in reads[1:3]:
            read.wait()
        keep = pltpu.make_async_copy(grad_ref, grad_hbm, outs.at[STEPS])
        keep.start()

        @pl.loop(0, part // block)
        def _(n):
            at = pl.ds(pl.multiple_of(n * block, block), block)
            half = dot(l1_ref[...], h1[:, at]) + (dot(l1_ref[...], h2[:, at]) + dot(l2_ref[...], h1[:, at]))
            t1[:, at], t2[:, at] = two(half)

        for read in reads[3:]:
            read.wait()

        def p_copy(n):
            at = pl.ds(pl.multiple_of(n * block, block), block)
            return pltpu.make_async_copy(p_ref.at[:, at], p_hbm.at[:, at], outs.at[n])

        @pl.loop(0, STEPS)
        def _(n):
            at = pl.ds(pl.multiple_of(n * block, block), block)
            p_ref[:, at] = dot(t1[...], r1_ref[:, at]) + (dot(t1[...], r2_ref[:, at]) + dot(t2[...], r1_ref[:, at]))
            p_copy(n).start()

        for n in range(STEPS):
            p_copy(n).wait()
        keep.wait()

    square = (size, size)
    narrow = (size, part)
    return pl.pallas_call(
        body,
        out_shape=[jax.ShapeDtypeStruct(square, F32), jax.ShapeDtypeStruct(narrow, F32)],
        in_specs=[SMEM] + [HBM] * 5,
        out_specs=[HBM] * 2,
        scratch_shapes=[pltpu.VMEM((pieces, tall, LANES), BF16)]
        + [pltpu.VMEM(square, BF16)] * 2
        + [pltpu.VMEM((part, size), BF16)] * 2
        + [pltpu.VMEM(narrow, F32)]
        + [pltpu.VMEM(narrow, BF16)] * 4
        + [pltpu.VMEM(square, F32), pltpu.VMEM((LANES, pieces * EXTRA), F32), DMA((5,)), DMA((STEPS + 1,))],
        compiler_params=PARAMS,
        cost_estimate=cost(12 * size * size * part, 20 * size * size),
        name="products",
    )(slots, arrived, l1, l2, r1, r2)


def graft(slots, arrived, l1, l2, r1, r2, earlier, grad, moment, rows, columns, entries):
    size = moment.shape[0]
    owners, tall, _ = arrived.shape
    pieces = size // rows
    block = size // STEPS
    done = grad.shape[1]
    part = size - done
    thin = size // FINE

    def body(
        slots_hbm, a_hbm, l1_hbm, l2_hbm, r1_hbm, r2_hbm, p_hbm, grad_hbm, m_hbm, out_hbm, fresh_hbm,
        slots_ref, a_ref, l1_ref, l2_ref, r1_ref, r2_ref, p_ref, grad_ref, h1, h2, t1, t2, m_ref, out_ref,
        turned, asum, psum, ins, outs,
    ):
        deep = pl.ds(done, part)

        def cut(n):
            return pl.ds(pl.multiple_of(n * block, block), block)

        pairs = (
            (slots_hbm, slots_ref),
            (a_hbm, a_ref),
            (l1_hbm, l1_ref),
            (l2_hbm, l2_ref),
            (r1_hbm.at[deep], r1_ref),
            (r2_hbm.at[deep], r2_ref),
        )
        reads = [pltpu.make_async_copy(s, t, ins.at[3, k]) for k, (s, t) in enumerate(pairs)]

        def p_read(n):
            at = cut(n)
            return pltpu.make_async_copy(p_hbm.at[:, at], p_ref.at[:, at], ins.at[0, n])

        def adam_reads(n):
            at = cut(n)
            pairs = ((grad_hbm.at[at], grad_ref.at[at, pl.ds(0, done)]), (m_hbm.at[at], m_ref.at[at]))
            return [pltpu.make_async_copy(s, t, ins.at[1 + k, n]) for k, (s, t) in enumerate(pairs)]

        for read in reads[:3]:
            read.start()
        for read in reads[:2]:
            read.wait()
        band = own_band(slots_ref, columns)
        base = band * pieces

        for read in reads[3:]:
            read.start()

        @pl.loop(0, STEPS)
        def _(n):
            for read in [p_read(n), *adam_reads(n)]:
                read.start()

        dequant(a_ref, base, pieces, turned, rows, done // LANES, done, grad_ref, h1, h2)
        heads = jnp.sum(a_ref[:, tall - EXTRA :, :].astype(F32), axis=0)[: EXTRA - 8]
        total = jnp.sum(heads, axis=0, keepdims=True)[:, :1]
        bound = 0.5 * jnp.sqrt(jnp.full((1, 1), entries, F32)) / jnp.sqrt(jnp.where(total > 0, total, 1.0))
        clip = jnp.where(total > 0, jnp.minimum(bound, 1.0), 1.0)
        asum[...] = jnp.zeros_like(asum)
        psum[...] = jnp.zeros_like(psum)
        reads[2].wait()

        def fresh_copy(n):
            return pltpu.make_async_copy(m_ref.at[cut(n)], fresh_hbm.at[cut(n)], outs.at[0, n])

        def out_copy(n):
            to = pl.ds(pl.multiple_of(band * size + n * block, block), block)
            return pltpu.make_async_copy(out_ref.at[cut(n)], out_hbm.at[to], outs.at[1, n])

        def adam(n):
            for read in adam_reads(n):
                read.wait()
            steps = []
            for k in range(block // thin):
                line = pl.ds(pl.multiple_of(n * block + k * thin, thin), thin)
                held = grad_ref[line, :] * clip
                square = held * held
                fresh = 0.9 * m_ref[line, :] + 0.1 * square
                m_ref[line, :] = fresh
                root = fresh * lax.rsqrt(fresh) + 1e-08
                inverse = pl.reciprocal(root, approx=True)
                ratios = held * (inverse * (2.0 - root * inverse))
                steps.append(fold(ratios * ratios))
            asum[...] += sum(steps)
            fresh_copy(n).start()

        half = dot(l1_ref[...], h1[...]) + dot(l1_ref[...], h2[...])
        reads[3].wait()
        t1[...], t2[...] = two(half + dot(l2_ref[...], h1[...]))
        for read in reads[4:]:
            read.wait()

        @pl.loop(0, STEPS)
        def _(n):
            p_read(n).wait()
            at = cut(n)
            more = dot(t1[...], r1_ref[:, at]) + (dot(t1[...], r2_ref[:, at]) + dot(t2[...], r1_ref[:, at]))
            product = p_ref[:, at] + more
            p_ref[:, at] = product
            psum[...] += fold(product * product)
            adam(n)

        norm = jnp.sqrt(everywhere(psum[...]) * (clip * clip) + 1e-12)
        ratio = clip * (jnp.sqrt(everywhere(asum[...])) / norm)

        @pl.loop(0, STEPS)
        def _(n):
            out_ref[cut(n), :] = (p_ref[cut(n), :] * ratio).astype(BF16)
            out_copy(n).start()

        for n in range(STEPS):
            fresh_copy(n).wait()
            out_copy(n).wait()

    square = (size, size)
    return pl.pallas_call(
        body,
        out_shape=[
            jax.ShapeDtypeStruct((owners * rows, size), BF16),
            jax.ShapeDtypeStruct(square, F32),
        ],
        in_specs=[HBM] * 9,
        out_specs=[HBM, HBM],
        scratch_shapes=[pltpu.SMEM(slots.shape, jnp.int32), pltpu.VMEM((owners, tall, LANES), BF16)]
        + [pltpu.VMEM(square, BF16)] * 2
        + [pltpu.VMEM((part, size), BF16)] * 2
        + [pltpu.VMEM(square, F32)] * 2
        + [pltpu.VMEM((size, part), BF16)] * 4
        + [
            pltpu.VMEM(square, F32),
            pltpu.VMEM(square, BF16),
            pltpu.VMEM((LANES, pieces * EXTRA), F32),
            pltpu.VMEM((8, LANES), F32),
            pltpu.VMEM((8, LANES), F32),
            DMA((4, 6)),
            DMA((2, STEPS)),
        ],
        compiler_params=PARAMS,
        cost_estimate=cost(12 * size * size * part, 24 * size * size),
        name="graft",
    )(slots, arrived, l1, l2, r1, r2, earlier, grad, moment)


def place(slots, returned, cols):
    owners, rows, width = returned.shape
    columns = cols // width

    def body(slots_ref, r_ref, out_hbm, inverse, outs):
        first = lax.div(lax.axis_index("fsdp") * rows, width) * columns
        invert(slots_ref, inverse)

        def write(k):
            here = pl.ds(pl.multiple_of(k * width, width), width)
            return pltpu.make_async_copy(r_ref.at[inverse[first + k]], out_hbm.at[:, here], outs.at[k])

        @pl.loop(0, columns)
        def _(k):
            write(k).start()

        @pl.loop(0, columns)
        def _(k):
            write(k).wait()

    return pl.pallas_call(
        body,
        out_shape=jax.ShapeDtypeStruct((rows, cols), BF16),
        in_specs=[SMEM, pl.BlockSpec(memory_space=pltpu.VMEM)],
        out_specs=HBM,
        scratch_shapes=[pltpu.SMEM((owners,), jnp.int32), DMA((columns,))],
        compiler_params=pltpu.CompilerParams(vmem_limit_bytes=12 * 1024 * 1024),
        cost_estimate=cost(0, 4 * rows * cols),
        name="place",
    )(slots, returned)


def on_device(q_values, scales, block_slots, left_root, right_root, second_moment):
    count = lax.axis_size("fsdp")
    planes = lax.axis_size("grp")
    rows, cols = q_values.shape
    width = left_root.shape[-1]
    columns = cols // width
    first = width * 3 // 4

    def exchange(value):
        return lax.all_to_all(value, "fsdp", split_axis=0, concat_axis=0, tiled=True)

    arrived = exchange(pack(block_slots, q_values, scales, [], width, 0, first))
    own = square_sum(q_values, scales)
    sums = [own]
    for k in range(1, planes):
        sums.append(lax.ppermute(own, "grp", [(i, (i + k) % planes) for i in range(planes)]))
    *sums, l1, l2, r1, r2 = lax.optimization_barrier((*sums, *split_roots(left_root[0, 0], right_root[0, 0])))
    roots = (l1, l2, r1, r2)
    later = exchange(pack(block_slots, q_values, scales, sums, width, first, width - first))

    product, grad = products(block_slots, arrived, *roots, rows, columns)
    outgoing, fresh = graft(
        block_slots, later, *roots, product, grad, second_moment[0, 0], rows, columns, rows * count * cols * planes
    )
    update = place(block_slots, exchange(outgoing.reshape(count, rows, width)), cols)
    return (update, fresh[None, None])


def solution(mesh):
    in_specs = (
        P("fsdp", "grp"),
        P("fsdp", "grp"),
        P("grp", None),
        P("grp", "fsdp", None, None),
        P("grp", "fsdp", None, None),
        P("grp", "fsdp", None, None),
    )
    out_specs = (P("fsdp", "grp"), P("grp", "fsdp", None, None))
    return jax.shard_map(
        on_device, mesh=mesh, in_specs=in_specs, out_specs=out_specs, check_vma=False
    )
```

```python
import jax
import jax.numpy as jnp
from jax import lax
from jax.experimental import pallas as pl
from jax.experimental.pallas import tpu as pltpu
from jax.sharding import PartitionSpec as P

LANES = 128
EXTRA = 16
STEPS = 4
FINE = 16
F32 = jnp.float32
BF16 = jnp.bfloat16
HBM = pl.BlockSpec(memory_space=pltpu.HBM)
SMEM = pl.BlockSpec(memory_space=pltpu.SMEM)
PARAMS = pltpu.CompilerParams(vmem_limit_bytes=63 * 1024 * 1024)
DMA = pltpu.SemaphoreType.DMA


def cost(flops, nbytes):
    return pl.CostEstimate(flops=flops, bytes_accessed=nbytes, transcendentals=0)


def dot(a, b):
    return jnp.dot(a, b, preferred_element_type=F32)


def two(value):
    top = value.astype(BF16)
    return top, (value - top.astype(F32)).astype(BF16)


def fold(value):
    rows, cols = value.shape
    total = value[:, :LANES]
    for j in range(1, cols // LANES):
        total = total + value[:, j * LANES : (j + 1) * LANES]
    return total.reshape(rows // 8, 8, LANES).sum(axis=0)


def everywhere(value):
    return jnp.sum(value, axis=(0, 1), keepdims=True)


def invert(slots_ref, inverse_ref):
    for owner in range(slots_ref.shape[1]):
        inverse_ref[slots_ref[0, owner]] = owner


def own_band(slots_ref, columns):
    return lax.div(slots_ref[0, lax.axis_index("fsdp")], columns)


def pack(slots, q_values, scales, sums_of, width, start, part):
    owners = slots.shape[1]
    rows, cols = q_values.shape
    columns = cols // width
    groups = width // LANES
    here = part // LANES
    tall = here * rows + EXTRA
    sums = EXTRA - groups

    def body(slots_hbm, q_hbm, s_hbm, *rest):
        e_hbm = rest[: len(sums_of)]
        out_hbm, slots_ref, inverse, q_ref, s_ref, e_ref, turned, out_ref, ins, outs = rest[-10:]

        def q_read(k):
            at = pl.ds(pl.multiple_of(k * width + start, LANES), part)
            return pltpu.make_async_copy(q_hbm.at[:, at], q_ref.at[k], ins.at[k])

        def write(k, band):
            at = band * columns + k
            return pltpu.make_async_copy(out_ref.at[k], out_hbm.at[inverse[at]], outs.at[at])

        reads = [
            pltpu.make_async_copy(slots_hbm, slots_ref, ins.at[columns]),
            pltpu.make_async_copy(s_hbm, s_ref, ins.at[columns + 1]),
        ]
        for k, src in enumerate(e_hbm):
            reads.append(pltpu.make_async_copy(src, e_ref.at[k], ins.at[columns + 2 + k]))
        for read in reads:
            read.start()

        @pl.loop(0, columns)
        def _(k):
            q_read(k).start()

        bands = range(owners // columns) if e_hbm else [lax.div(lax.axis_index("fsdp") * rows, width)]
        for read in reads:
            read.wait()
        invert(slots_ref, inverse)
        padded = jnp.concatenate([s_ref[...].astype(F32), jnp.zeros((LANES - rows, LANES), F32)], axis=0)
        turned[...] = padded.T
        head = jnp.zeros((sums, LANES), F32)
        if e_hbm:
            value = e_ref[0]
            for k in range(1, len(e_hbm)):
                value = value + e_ref[k]
            high = value.astype(BF16)
            mid, low = two(value - high.astype(F32))
            row = lax.broadcasted_iota(jnp.int32, head.shape, 0)
            for k, term in enumerate((high, mid, low)):
                head = jnp.where(row == k, jnp.broadcast_to(term[:1].astype(F32), head.shape), head)

        @pl.loop(0, columns)
        def _(k):
            scale = turned[pl.ds(pl.multiple_of(k * groups, groups), groups), :]
            out_ref[k, here * rows :, :] = jnp.concatenate([head, scale], axis=0).astype(BF16)
            q_read(k).wait()
            for j in range(here):
                out_ref[k, j * rows : (j + 1) * rows, :] = q_ref[k, :, j * LANES : (j + 1) * LANES]
            for band in bands:
                write(k, band).start()

        @pl.loop(0, columns)
        def _(k):
            for band in bands:
                write(k, band).wait()

    operands = [slots, q_values, scales, *sums_of]
    return pl.pallas_call(
        body,
        out_shape=jax.ShapeDtypeStruct((owners, tall, LANES), BF16),
        in_specs=[HBM] * len(operands),
        out_specs=HBM,
        scratch_shapes=[
            pltpu.SMEM(slots.shape, jnp.int32),
            pltpu.SMEM((owners,), jnp.int32),
            pltpu.VMEM((columns, rows, part), BF16),
            pltpu.VMEM(scales.shape, BF16),
            pltpu.VMEM((max(len(sums_of), 1), 8, LANES), F32),
            pltpu.VMEM((LANES, LANES), F32),
            pltpu.VMEM((columns, tall, LANES), BF16),
            DMA((columns + 2 + len(sums_of),)),
            DMA((owners,)),
        ],
        compiler_params=PARAMS,
        cost_estimate=cost(0, 2 * rows * cols + 2 * owners * tall * LANES),
        name=f"pack_{start}",
    )(*operands)


def square_sum(q_values, scales):
    rows, cols = q_values.shape
    groups = scales.shape[1]
    group = cols // groups

    def body(q_hbm, s_hbm, out_ref, q_ref, s_ref, sems):
        reads = [pltpu.make_async_copy(q_hbm, q_ref, sems.at[0]), pltpu.make_async_copy(s_hbm, s_ref, sems.at[1])]
        for read in reads:
            read.start()
        for read in reads:
            read.wait()
        total = jnp.zeros((rows, group), F32)
        for j in range(groups):
            grad = q_ref[:, j * group : (j + 1) * group].astype(F32) * s_ref[:, j : j + 1].astype(F32)
            total = total + grad * grad
        out_ref[...] = jnp.full((8, LANES), jnp.sum(total))

    return pl.pallas_call(
        body,
        out_shape=jax.ShapeDtypeStruct((8, LANES), F32),
        in_specs=[HBM] * 2,
        scratch_shapes=[pltpu.VMEM((rows, cols), BF16), pltpu.VMEM(scales.shape, BF16), DMA((2,))],
        compiler_params=PARAMS,
        cost_estimate=cost(3 * rows * cols, 2 * rows * cols),
        name="square_sum",
    )(q_values, scales)


def split_roots(left, right):
    size = left.shape[0]
    rows = size // STEPS

    def body(l_hbm, r_hbm, l1_hbm, l2_hbm, r1_hbm, r2_hbm, full, top, low, ins, outs):
        jobs = []
        for src, high_hbm, low_hbm in ((l_hbm, l1_hbm, l2_hbm), (r_hbm, r1_hbm, r2_hbm)):
            for n in range(STEPS):
                at = pl.ds(n * rows, rows)
                jobs.append((src.at[at], high_hbm.at[at], low_hbm.at[at]))
        reads = [pltpu.make_async_copy(job[0], full.at[k], ins.at[k]) for k, job in enumerate(jobs)]
        for read in reads:
            read.start()
        writes = []
        for k, (_, high_to, low_to) in enumerate(jobs):
            reads[k].wait()
            top[k], low[k] = two(full[k])
            for h, (src, to) in enumerate(((top.at[k], high_to), (low.at[k], low_to))):
                write = pltpu.make_async_copy(src, to, outs.at[2 * k + h])
                write.start()
                writes.append(write)
        for write in writes:
            write.wait()

    jobs = 2 * STEPS
    return pl.pallas_call(
        body,
        out_shape=[jax.ShapeDtypeStruct((size, size), BF16)] * 4,
        in_specs=[HBM] * 2,
        out_specs=[HBM] * 4,
        scratch_shapes=[
            pltpu.VMEM((jobs, rows, size), F32),
            pltpu.VMEM((jobs, rows, size), BF16),
            pltpu.VMEM((jobs, rows, size), BF16),
            DMA((jobs,)),
            DMA((2 * jobs,)),
        ],
        compiler_params=PARAMS,
        cost_estimate=cost(4 * size * size, 16 * size * size),
        name="split_roots",
    )(left, right)


def dequant(a_ref, base, pieces, turned, rows, group, at_lane, grad_ref, h1, h2):
    tall = a_ref.shape[1]
    here = (tall - EXTRA) // rows
    scales = a_ref[pl.ds(base, pieces), here * rows :, :].astype(F32).reshape(pieces * EXTRA, LANES)
    turned[...] = scales.T
    for piece in range(pieces):
        at = slice(piece * rows, (piece + 1) * rows)
        for j in range(here):
            column = piece * EXTRA + EXTRA - 8 + group + j
            grad = a_ref[base + piece, j * rows : (j + 1) * rows, :].astype(F32) * turned[:rows, column : column + 1]
            grad_ref[at, at_lane + j * LANES : at_lane + (j + 1) * LANES] = grad
            lanes = slice(j * LANES, (j + 1) * LANES)
            h1[at, lanes], h2[at, lanes] = two(grad)


def products(slots, arrived, l1, l2, r1, r2, rows, columns):
    size = l1.shape[0]
    _, tall, _ = arrived.shape
    pieces = size // rows
    part = tall // rows * LANES
    block = size // STEPS

    def body(
        slots_ref, a_hbm, l1_hbm, l2_hbm, r1_hbm, r2_hbm, p_hbm, grad_hbm,
        a_ref, l1_ref, l2_ref, r1_ref, r2_ref, grad_ref, h1, h2, t1, t2, p_ref, turned, ins, outs,
    ):
        band = own_band(slots_ref, columns)
        deep = pl.ds(0, part)
        pairs = (
            (a_hbm.at[pl.ds(band * pieces, pieces)], a_ref),
            (l1_hbm, l1_ref),
            (l2_hbm, l2_ref),
            (r1_hbm.at[deep], r1_ref),
            (r2_hbm.at[deep], r2_ref),
        )
        reads = [pltpu.make_async_copy(s, t, ins.at[k]) for k, (s, t) in enumerate(pairs)]
        for read in reads[:3]:
            read.start()
        reads[0].wait()
        for read in reads[3:]:
            read.start()
        dequant(a_ref, 0, pieces, turned, rows, 0, 0, grad_ref, h1, h2)
        for read in reads[1:3]:
            read.wait()
        keep = pltpu.make_async_copy(grad_ref, grad_hbm, outs.at[STEPS])
        keep.start()

        @pl.loop(0, part // block)
        def _(n):
            at = pl.ds(pl.multiple_of(n * block, block), block)
            half = dot(l1_ref[...], h1[:, at]) + (dot(l1_ref[...], h2[:, at]) + dot(l2_ref[...], h1[:, at]))
            t1[:, at], t2[:, at] = two(half)

        for read in reads[3:]:
            read.wait()

        def p_copy(n):
            at = pl.ds(pl.multiple_of(n * block, block), block)
            return pltpu.make_async_copy(p_ref.at[:, at], p_hbm.at[:, at], outs.at[n])

        @pl.loop(0, STEPS)
        def _(n):
            at = pl.ds(pl.multiple_of(n * block, block), block)
            p_ref[:, at] = dot(t1[...], r1_ref[:, at]) + (dot(t1[...], r2_ref[:, at]) + dot(t2[...], r1_ref[:, at]))
            p_copy(n).start()

        for n in range(STEPS):
            p_copy(n).wait()
        keep.wait()

    square = (size, size)
    narrow = (size, part)
    return pl.pallas_call(
        body,
        out_shape=[jax.ShapeDtypeStruct(square, F32), jax.ShapeDtypeStruct(narrow, F32)],
        in_specs=[SMEM] + [HBM] * 5,
        out_specs=[HBM] * 2,
        scratch_shapes=[pltpu.VMEM((pieces, tall, LANES), BF16)]
        + [pltpu.VMEM(square, BF16)] * 2
        + [pltpu.VMEM((part, size), BF16)] * 2
        + [pltpu.VMEM(narrow, F32)]
        + [pltpu.VMEM(narrow, BF16)] * 4
        + [pltpu.VMEM(square, F32), pltpu.VMEM((LANES, pieces * EXTRA), F32), DMA((5,)), DMA((STEPS + 1,))],
        compiler_params=PARAMS,
        cost_estimate=cost(12 * size * size * part, 20 * size * size),
        name="products",
    )(slots, arrived, l1, l2, r1, r2)


def graft(slots, arrived, l1, l2, r1, r2, earlier, grad, moment, rows, columns, entries):
    size = moment.shape[0]
    owners, tall, _ = arrived.shape
    pieces = size // rows
    block = size // STEPS
    done = grad.shape[1]
    part = size - done
    thin = size // FINE

    def body(
        slots_hbm, a_hbm, l1_hbm, l2_hbm, r1_hbm, r2_hbm, p_hbm, grad_hbm, m_hbm, out_hbm, fresh_hbm,
        slots_ref, a_ref, l1_ref, l2_ref, r1_ref, r2_ref, p_ref, grad_ref, h1, h2, t1, t2, m_ref, out_ref,
        turned, asum, psum, ins, outs,
    ):
        deep = pl.ds(done, part)

        def cut(n):
            return pl.ds(pl.multiple_of(n * block, block), block)

        pairs = (
            (slots_hbm, slots_ref),
            (a_hbm, a_ref),
            (l1_hbm, l1_ref),
            (l2_hbm, l2_ref),
            (r1_hbm.at[deep], r1_ref),
            (r2_hbm.at[deep], r2_ref),
        )
        reads = [pltpu.make_async_copy(s, t, ins.at[3, k]) for k, (s, t) in enumerate(pairs)]

        def p_read(n):
            at = cut(n)
            return pltpu.make_async_copy(p_hbm.at[:, at], p_ref.at[:, at], ins.at[0, n])

        def adam_reads(n):
            at = cut(n)
            pairs = ((grad_hbm.at[at], grad_ref.at[at, pl.ds(0, done)]), (m_hbm.at[at], m_ref.at[at]))
            return [pltpu.make_async_copy(s, t, ins.at[1 + k, n]) for k, (s, t) in enumerate(pairs)]

        for read in reads[:4]:
            read.start()
        for read in reads[:2]:
            read.wait()
        band = own_band(slots_ref, columns)
        base = band * pieces

        for read in reads[4:]:
            read.start()

        @pl.loop(0, STEPS)
        def _(n):
            for read in [p_read(n), *adam_reads(n)]:
                read.start()

        dequant(a_ref, base, pieces, turned, rows, done // LANES, done, grad_ref, h1, h2)
        heads = jnp.sum(a_ref[:, tall - EXTRA :, :].astype(F32), axis=0)[: EXTRA - 8]
        total = jnp.sum(heads, axis=0, keepdims=True)[:, :1]
        bound = 0.5 * jnp.sqrt(jnp.full((1, 1), entries, F32)) / jnp.sqrt(jnp.where(total > 0, total, 1.0))
        clip = jnp.where(total > 0, jnp.minimum(bound, 1.0), 1.0)
        asum[...] = jnp.zeros_like(asum)
        psum[...] = jnp.zeros_like(psum)
        for read in reads[2:4]:
            read.wait()

        def fresh_copy(n):
            return pltpu.make_async_copy(m_ref.at[cut(n)], fresh_hbm.at[cut(n)], outs.at[0, n])

        def out_copy(n):
            to = pl.ds(pl.multiple_of(band * size + n * block, block), block)
            return pltpu.make_async_copy(out_ref.at[cut(n)], out_hbm.at[to], outs.at[1, n])

        def adam(n):
            for read in adam_reads(n):
                read.wait()
            steps = []
            for k in range(block // thin):
                line = pl.ds(pl.multiple_of(n * block + k * thin, thin), thin)
                held = grad_ref[line, :] * clip
                square = held * held
                fresh = 0.9 * m_ref[line, :] + 0.1 * square
                m_ref[line, :] = fresh
                root = fresh * lax.rsqrt(fresh) + 1e-08
                inverse = pl.reciprocal(root, approx=True)
                ratios = held * (inverse * (2.0 - root * inverse))
                steps.append(fold(ratios * ratios))
            asum[...] += sum(steps)
            fresh_copy(n).start()

        half = dot(l1_ref[...], h1[...]) + (dot(l1_ref[...], h2[...]) + dot(l2_ref[...], h1[...]))
        t1[...], t2[...] = two(half)
        for read in reads[4:]:
            read.wait()

        @pl.loop(0, STEPS)
        def _(n):
            p_read(n).wait()
            at = cut(n)
            more = dot(t1[...], r1_ref[:, at]) + (dot(t1[...], r2_ref[:, at]) + dot(t2[...], r1_ref[:, at]))
            product = p_ref[:, at] + more
            p_ref[:, at] = product
            psum[...] += fold(product * product)
            adam(n)

        norm = jnp.sqrt(everywhere(psum[...]) * (clip * clip) + 1e-12)
        ratio = clip * (jnp.sqrt(everywhere(asum[...])) / norm)

        @pl.loop(0, STEPS)
        def _(n):
            out_ref[cut(n), :] = (p_ref[cut(n), :] * ratio).astype(BF16)
            out_copy(n).start()

        for n in range(STEPS):
            fresh_copy(n).wait()
            out_copy(n).wait()

    square = (size, size)
    return pl.pallas_call(
        body,
        out_shape=[
            jax.ShapeDtypeStruct((owners * rows, size), BF16),
            jax.ShapeDtypeStruct(square, F32),
        ],
        in_specs=[HBM] * 9,
        out_specs=[HBM, HBM],
        scratch_shapes=[pltpu.SMEM(slots.shape, jnp.int32), pltpu.VMEM((owners, tall, LANES), BF16)]
        + [pltpu.VMEM(square, BF16)] * 2
        + [pltpu.VMEM((part, size), BF16)] * 2
        + [pltpu.VMEM(square, F32)] * 2
        + [pltpu.VMEM((size, part), BF16)] * 4
        + [
            pltpu.VMEM(square, F32),
            pltpu.VMEM(square, BF16),
            pltpu.VMEM((LANES, pieces * EXTRA), F32),
            pltpu.VMEM((8, LANES), F32),
            pltpu.VMEM((8, LANES), F32),
            DMA((4, 6)),
            DMA((2, STEPS)),
        ],
        compiler_params=PARAMS,
        cost_estimate=cost(12 * size * size * part, 24 * size * size),
        name="graft",
    )(slots, arrived, l1, l2, r1, r2, earlier, grad, moment)


def place(slots, returned, cols):
    owners, rows, width = returned.shape
    columns = cols // width

    def body(slots_ref, r_ref, out_hbm, inverse, outs):
        first = lax.div(lax.axis_index("fsdp") * rows, width) * columns
        invert(slots_ref, inverse)

        def write(k):
            here = pl.ds(pl.multiple_of(k * width, width), width)
            return pltpu.make_async_copy(r_ref.at[inverse[first + k]], out_hbm.at[:, here], outs.at[k])

        @pl.loop(0, columns)
        def _(k):
            write(k).start()

        @pl.loop(0, columns)
        def _(k):
            write(k).wait()

    return pl.pallas_call(
        body,
        out_shape=jax.ShapeDtypeStruct((rows, cols), BF16),
        in_specs=[SMEM, pl.BlockSpec(memory_space=pltpu.VMEM)],
        out_specs=HBM,
        scratch_shapes=[pltpu.SMEM((owners,), jnp.int32), DMA((columns,))],
        compiler_params=pltpu.CompilerParams(vmem_limit_bytes=12 * 1024 * 1024),
        cost_estimate=cost(0, 4 * rows * cols),
        name="place",
    )(slots, returned)


def on_device(q_values, scales, block_slots, left_root, right_root, second_moment):
    count = lax.axis_size("fsdp")
    planes = lax.axis_size("grp")
    rows, cols = q_values.shape
    width = left_root.shape[-1]
    columns = cols // width
    first = width * 3 // 4

    def exchange(value):
        return lax.all_to_all(value, "fsdp", split_axis=0, concat_axis=0, tiled=True)

    arrived = exchange(pack(block_slots, q_values, scales, [], width, 0, first))
    own = square_sum(q_values, scales)
    sums = [own]
    for k in range(1, planes):
        sums.append(lax.ppermute(own, "grp", [(i, (i + k) % planes) for i in range(planes)]))
    *sums, l1, l2, r1, r2 = lax.optimization_barrier((*sums, *split_roots(left_root[0, 0], right_root[0, 0])))
    roots = (l1, l2, r1, r2)
    later = exchange(pack(block_slots, q_values, scales, sums, width, first, width - first))

    product, grad = products(block_slots, arrived, *roots, rows, columns)
    outgoing, fresh = graft(
        block_slots, later, *roots, product, grad, second_moment[0, 0], rows, columns, rows * count * cols * planes
    )
    update = place(block_slots, exchange(outgoing.reshape(count, rows, width)), cols)
    return (update, fresh[None, None])


def solution(mesh):
    in_specs = (
        P("fsdp", "grp"),
        P("fsdp", "grp"),
        P("grp", None),
        P("grp", "fsdp", None, None),
        P("grp", "fsdp", None, None),
        P("grp", "fsdp", None, None),
    )
    out_specs = (P("fsdp", "grp"), P("grp", "fsdp", None, None))
    return jax.shard_map(
        on_device, mesh=mesh, in_specs=in_specs, out_specs=out_specs, check_vma=False
    )
```
